512 devices in a mesh: sample: 8 (over y, z_hi), space: 64 (over z_lo, x, core).
Axes of the slice: x: 4, y: 4, z: 16 (z_hi: 2, z_lo: 8; z = z_hi * 8 + z_lo), core: 2. Of those that a mesh axis runs over, the one named last changes fastest.
Arguments:
- activations: bfloat16 [8, 64, 16, 16, 128], P('sample', 'space'), may hold values from -6 to 6
- conv_weight: bfloat16 [3456, 256], replicated, may hold values from -0.109375 to 0.109375
- conv_bias: float32 [256], replicated, may hold values from -3 to 3
- cotangent: bfloat16 [8, 64, 16, 16, 256], P('sample', 'space'), may hold values from -6 to 6
- basis_panels: bfloat16 [8, 432, 3456], P('sample', None, 'space'), may hold values from -0.109375 to 0.109375
- panel_owner: int32 [8], replicated, may hold values from 0 to 7, each once
- output_basis: float32 [256, 256], replicated, may hold values from -0.375 to 0.375
- input_eigen: float32 [3456], P('space'), may hold values from 0.001 to 1
- output_eigen: float32 [256], replicated, may hold values from 0.001 to 1
Outputs:
- data_grad: bfloat16 [8, 64, 16, 16, 128], P('sample', 'space')
- update: float32 [3456, 256], P('space')
The draws below stay inside these ranges and needn't reach their ends.
Inputs may be any that keep to these rules, and one draw needn't show every extreme that they name: Every sample index stores exactly one row panel: panel j of the basis sits in slot panel_owner[j].
All inputs are finite; a program needn't handle non-finite values.
Results may differ from the reference program's by a relative error of at most 0.0055.
Values may be sent and summed in bfloat16 or wider, within the bound.
No kernel may reach another device: no remote copies, remote signals or barrier semaphores. Data moves between devices by JAX's collectives and lax.ppermute only.
A program may use at most 64 MiB of HBM per device.

```python
import math
import jax
import jax.numpy as jnp
from jax import lax

C_IN = 128
C_OUT = 256
YW = 16
XW = 16
P_SIZE = 3456
PANEL = 432
SAMPLES = 8
Z = 64
CELLS = 131072
N_SAMPLE = 8


def block_levels(own_key, shape, cuts, smallest, largest):
    loudness, own = 1.0, jax.random.fold_in(own_key, 6)
    for dim, blocks in cuts:
        draws = jnp.exp(jax.random.uniform(jax.random.fold_in(own, dim), (blocks,), jnp.float32, smallest / len(cuts), largest / len(cuts)))
        loudness = loudness * jnp.repeat(draws, shape[dim] // blocks).reshape([-1 if axis == dim else 1 for axis in range(len(shape))])
    return loudness


def centred(key, shape, width, most, shards=(), dtype=jnp.bfloat16):
    array = jax.random.normal(key, shape, jnp.float32) * width
    if len(shards) > 0:
        array = block_levels(key, shape, shards, -0.22, 0.18) * array
    return jnp.clip(array, min=-most, max=most).astype(dtype)


def setup_inputs(seed: int = 0) -> dict:
    arg_keys = jax.random.split(jax.random.key(seed), 10)
    activations = centred(arg_keys[0], (SAMPLES, Z, YW, XW, C_IN), 1.0, 6.0, ((0, 8), (1, 64)))
    conv_weight = centred(arg_keys[1], (P_SIZE, C_OUT), P_SIZE ** -0.5, 0.109375)
    conv_bias = centred(arg_keys[2], (C_OUT,), 0.5, 3.0, (), jnp.float32)
    cotangent = centred(arg_keys[3], (SAMPLES, Z, YW, XW, C_OUT), 1.0, 6.0, ((0, 8), (1, 64)))
    basis_panels = centred(arg_keys[4], (N_SAMPLE, PANEL, P_SIZE), P_SIZE ** -0.5, 0.109375, ((0, 8), (2, 64)))
    panel_owner = jax.random.permutation(arg_keys[5], N_SAMPLE).astype(jnp.int32)
    output_basis = centred(arg_keys[6], (C_OUT, C_OUT), C_OUT ** -0.5, 0.375, (), jnp.float32)
    input_eigen = jnp.clip(jnp.exp(math.log(1.0) - 6.9077552 * jax.random.uniform(arg_keys[7], (P_SIZE,), jnp.float32) ** block_levels(arg_keys[7], (P_SIZE,), ((0, 64),), -0.2, 0.2)), 0.001, 1.0)
    output_eigen = jnp.clip(jnp.exp(jax.random.uniform(arg_keys[8], (C_OUT,), jnp.float32, math.log(0.001), math.log(1.0))), 0.001, 1.0)
    return dict(activations=activations, conv_weight=conv_weight, conv_bias=conv_bias, cotangent=cotangent, basis_panels=basis_panels, panel_owner=panel_owner, output_basis=output_basis, input_eigen=input_eigen, output_eigen=output_eigen)


DAMPING = 1e-3


def tap_matrix(padded, flipped):
    planes = padded.shape[0] - 2
    height = padded.shape[1] - 2
    breadth = padded.shape[2] - 2
    pieces = []
    for z_step in range(3):
        for y_step in range(3):
            for x_step in range(3):
                z_from = 2 - z_step if flipped else z_step
                y_from = 2 - y_step if flipped else y_step
                x_from = 2 - x_step if flipped else x_step
                pieces.append(padded[z_from:z_from + planes, y_from:y_from + height, x_from:x_from + breadth, :])
    stacked = jnp.concatenate(pieces, axis=-1)
    return stacked.reshape(planes * height * breadth, stacked.shape[-1])


def pad_space(volume):
    return jnp.pad(volume, ((1, 1), (1, 1), (1, 1), (0, 0)))


def delta_of(pre_act, cot_rows):
    logistic = jax.nn.sigmoid(pre_act)
    return (cot_rows.astype(jnp.float32) * logistic * (1.0 + pre_act * (1.0 - logistic))).astype(jnp.bfloat16)


def reference(activations, conv_weight, conv_bias, cotangent, basis_panels, panel_owner, output_basis, input_eigen, output_eigen):
    in_width = activations.shape[-1]
    out_width = conv_weight.shape[1]
    weight_back = conv_weight.reshape(27, in_width, out_width).transpose(0, 2, 1).reshape(27 * out_width, in_width)

    def one_sample(pair):
        volume, cot = pair
        dims = volume.shape
        patches = tap_matrix(pad_space(volume), False)
        pre_act = jnp.dot(patches, conv_weight, preferred_element_type=jnp.float32) + conv_bias
        delta = delta_of(pre_act, cot.reshape(-1, out_width))
        grad_part = lax.dot_general(patches, delta, (((0,), (0,)), ((), ())), preferred_element_type=jnp.float32)
        back = tap_matrix(pad_space(delta.reshape(dims[0], dims[1], dims[2], out_width)), True)
        data = jnp.dot(back, weight_back, preferred_element_type=jnp.float32).astype(jnp.bfloat16)
        return data.reshape(dims), grad_part

    data_grad, grad_parts = lax.map(one_sample, (activations, cotangent))
    weight_grad = jnp.sum(grad_parts, axis=0) / CELLS
    basis = jnp.take(basis_panels, panel_owner, axis=0).reshape(P_SIZE, P_SIZE).astype(jnp.float32)
    highest = lax.Precision.HIGHEST
    rotated = jnp.dot(jnp.dot(basis.T, weight_grad, precision=highest), output_basis, precision=highest)
    scaled = rotated / (input_eigen[:, None] * output_eigen[None, :] + DAMPING)
    turned = jnp.dot(scaled, output_basis.T, precision=highest)
    update = jnp.dot(basis, turned, precision=highest)
    return data_grad, update
```

```python
import functools

import jax
import jax.numpy as jnp
from jax import lax
from jax.experimental import pallas as pl
from jax.experimental.pallas import tpu as pltpu
from jax.sharding import Mesh
from jax.sharding import PartitionSpec as P

DAMPING = 0.001
CELLS = 131072
BF16 = jnp.bfloat16
F32 = jnp.float32
VMEM = pl.BlockSpec(memory_space=pltpu.VMEM)
SMEM = pl.BlockSpec(memory_space=pltpu.SMEM)
LIMIT = 48 * 1024 * 1024
YS = ("y", "zh")
ZS = ("zh", "zl")
XC = ("x", "c")
YXC = ("y", "x", "c")
SPACE = ("zl", "x", "c")


def call(body, out_shape, inputs, scratch=(), smem=0, flops=0):
    specs = [SMEM] * smem + [VMEM] * (len(inputs) - smem)
    many = isinstance(out_shape, (list, tuple))
    return pl.pallas_call(
        body,
        out_shape=out_shape,
        in_specs=specs,
        out_specs=[VMEM] * len(out_shape) if many else VMEM,
        scratch_shapes=list(scratch),
        compiler_params=pltpu.CompilerParams(vmem_limit_bytes=LIMIT),
        cost_estimate=pl.CostEstimate(
            flops=flops,
            bytes_accessed=sum(a.size * a.dtype.itemsize for a in inputs),
            transcendentals=0,
        ),
    )(*inputs)


def shape(dims, dtype):
    return jax.ShapeDtypeStruct(dims, dtype)


def iota(dims, axis):
    return lax.broadcasted_iota(jnp.int32, dims, axis)


def exchange(x, axes):
    return lax.all_to_all(x, axes, 0, 0)


def contract0(a, b):
    return lax.dot_general(a, b, (((0,), (0,)), ((), ())), preferred_element_type=F32)


def x_shifted(rows, step):
    if step == 0:
        return rows
    x = iota(rows.shape, 0) & 15
    inside = (x + step >= 0) & (x + step < 16)
    return jnp.where(inside, pltpu.roll(rows, (-step) % 256, 0), 0.0)


def basis_body(panel_ref, eigen_ref, out_ref):
    panel = panel_ref[...]
    eigen = eigen_ref[...]
    first = eigen.astype(BF16).astype(F32)
    second = (eigen - first).astype(BF16).astype(F32)
    third = eigen - first - second
    for pair in range(4):
        row = iota((432, 128), 0)
        lane = iota((432, 128), 1)
        pick = ((row & 7) == 2 * pair + (lane >> 6)) & ((row >> 3) == (lane & 63))
        block = contract0(panel, jnp.where(pick, 1.0, 0.0).astype(BF16))
        block = jnp.concatenate([block, jnp.zeros((10, 128), F32)], axis=0)
        if pair == 0:
            at = iota((64, 128), 1)
            block = jnp.where(at == 54, first, block)
            block = jnp.where(at == 55, second, block)
            block = jnp.where(at == 56, third, block)
        out_ref[pair] = block.astype(BF16)


def forward_body(place_ref, low_ref, mine_ref, high_ref, weight_ref, bias_ref, cot_ref, delta_ref, send_ref, patches):
    planes = (low_ref[...], mine_ref[...], high_ref[...])
    none = jnp.zeros((16, 128), BF16)
    for a in range(3):
        wide = planes[a].astype(F32)
        for c in range(3):
            moved = x_shifted(wide, c - 1).astype(BF16)
            for b in range(3):
                at = (9 * a + 3 * b + c) * 128
                if b == 0:
                    shifted = jnp.concatenate([none, moved[:240]], axis=0)
                elif b == 2:
                    shifted = jnp.concatenate([moved[16:], none], axis=0)
                else:
                    shifted = moved
                patches[:, at : at + 128] = shifted
    pre = jnp.dot(patches[...], weight_ref[...], preferred_element_type=F32) + bias_ref[...]
    logistic = 1.0 / (1.0 + jnp.exp(-pre))
    delta = (cot_ref[...].astype(F32) * logistic * (1.0 + pre * (1.0 - logistic))).astype(BF16)
    delta_ref[...] = delta
    rim = jnp.where(place_ref[0] < 4, planes[0].astype(F32), planes[2].astype(F32))
    act_t = planes[1].astype(F32).T.astype(BF16)
    rim_t = rim.T.astype(BF16)
    for x in range(4):
        for c in range(2):
            to = 2 * x + c
            for half in range(2):
                lanes = slice(128 * half, 128 * half + 128)
                rows = slice(32 * x, 32 * x + 32)
                send_ref[to, 32 * half : 32 * half + 32] = act_t[rows, lanes]
                send_ref[to, 64 + 32 * half : 96 + 32 * half] = rim_t[rows, lanes]
            send_ref[to, 128:] = delta[:, 128 * c : 128 * c + 128]


def weight_grad_body(got_ref, out_ref, moved, deltas):
    pieces = []
    for plane, at in [(0, 64)] + [(e, 0) for e in range(8)] + [(7, 64)]:
        pieces.append(got_ref[plane, at : at + 32].astype(F32))
        pieces.append(got_ref[plane, at + 32 : at + 64].astype(F32))
    acts = jnp.concatenate(pieces, axis=1)
    lane = iota((32, 2560), 1)
    x = lane & 15
    y = (lane >> 4) & 15
    for b in range(3):
        for c in range(3):
            step = 16 * (b - 1) + (c - 1)
            turned = pltpu.roll(acts, (-step) % 2560, 1) if step else acts
            inside = (x + c >= 1) & (x + c < 17) & (y + b >= 1) & (y + b < 17)
            moved[32 * (3 * b + c) : 32 * (3 * b + c) + 32, :] = jnp.where(inside, turned, 0.0).astype(BF16)
    for e in range(8):
        deltas[256 * e : 256 * e + 256, :] = got_ref[e, 128:]
    rows = [
        jnp.dot(moved[:, 256 * a : 256 * a + 2048], deltas[...], preferred_element_type=F32) for a in range(3)
    ]
    whole = jnp.concatenate(rows, axis=0).reshape(27, 4, 8, 128)
    for to in range(4):
        part = jnp.concatenate([whole[:, to].reshape(216, 128), jnp.zeros((8, 128), F32)], axis=0)
        out_ref[to] = part.astype(BF16)


def over_y_body(got_ref, out_ref, total):
    total[...] = sum(got_ref[i].astype(F32) for i in range(4)) * (1.0 / CELLS)
    for r in range(8):
        rows = total[pl.ds(r, 28, stride=8), :]
        rows = jnp.concatenate([rows, jnp.zeros((4, 128), F32)], axis=0).astype(BF16)
        out_ref[r] = rows
        out_ref[8 + r] = rows


def over_z_body(got_ref, out_ref):
    total = sum(got_ref[i].astype(F32) for i in range(16)).astype(BF16)
    for to in range(32):
        out_ref[to] = total


def rotate_body(owner_ref, place_ref, got_ref, basis_ref, out_ref):
    zh, zl = place_ref[0], place_ref[1]
    groups = [
        jnp.concatenate([got_ref[2 * g], got_ref[2 * g + 1]], axis=1) for g in range(16)
    ]
    grads = jnp.concatenate(groups, axis=0)
    row = iota((512, 512), 0)
    h = 54 * (row >> 6) + (row & 63)
    source = (4 * (h & 3) + ((h >> 2) & 3)) * 32 + (h >> 4)
    pick = ((row & 63) < 54) & (source == iota((512, 512), 1))
    ordered = jnp.dot(jnp.where(pick, 1.0, 0.0).astype(BF16), grads, preferred_element_type=F32).astype(BF16)
    half = (iota((64, 128), 1) >> 6) == (zl & 1)
    total = jnp.zeros((64, 256), F32)
    for j in range(8):
        block = basis_ref[8 * zh + owner_ref[j], zl >> 1]
        block = jnp.where(half, block.astype(F32), 0.0).astype(BF16)
        rows = ordered[64 * j : 64 * j + 64]
        total = total + jnp.dot(block, jnp.concatenate([rows, rows], axis=0), preferred_element_type=F32)
    total = jnp.concatenate([total[:56, :128], total[:56, 128:]], axis=0).astype(BF16)
    for to in range(16):
        out_ref[to] = total


def update_body(owner_ref, place_ref, got_ref, basis_ref, out_basis_ref, out_eigen_ref, out_ref):
    zl = place_ref[1]
    slot = owner_ref[zl]
    highest = lax.Precision.HIGHEST
    whole = jnp.zeros((512, 256), F32)
    for zh in range(2):
        total = sum(got_ref[8 * zh + i].astype(F32) for i in range(8))
        rotated = jnp.concatenate([total[:56], total[56:]], axis=1)
        rotated = jnp.concatenate([rotated, jnp.zeros((8, 256), F32)], axis=0)
        rotated = jnp.dot(rotated, out_basis_ref[...], precision=highest, preferred_element_type=F32)
        terms = basis_ref[8 * zh, 0].astype(F32)
        eigen = (terms[:, 54:55] + terms[:, 55:56]) + terms[:, 56:57]
        scaled = rotated / (eigen * out_eigen_ref[...] + DAMPING)
        scaled = jnp.where(iota((64, 256), 0) < 54, scaled, 0.0)
        turned = lax.dot_general(
            scaled, out_basis_ref[...], (((1,), (1,)), ((), ())), precision=highest, preferred_element_type=F32
        )
        high = turned.astype(BF16)
        rest = (turned - high.astype(F32)).astype(BF16)
        parts = []
        for pair in range(4):
            block = basis_ref[8 * zh + slot, pair]
            parts.append(contract0(block, high) + contract0(block, rest))
        whole = whole + jnp.concatenate(parts, axis=0)
    row = iota((512, 512), 0)
    t = 54 * (row >> 6) + (row & 63)
    source = 64 * (t & 7) + (t >> 3)
    pick = ((row & 63) < 54) & (source == iota((512, 512), 1))
    ordered = jnp.dot(jnp.where(pick, 1.0, 0.0).astype(BF16), whole.astype(BF16), preferred_element_type=F32)
    out_ref[...] = ordered.astype(BF16).reshape(8, 64, 256)


def over_xc_body(got_ref, out_ref):
    total = sum(got_ref[i].astype(F32) for i in range(8))[:56]
    for to in range(4):
        out_ref[to] = total


def last_body(got_ref, out_ref):
    out_ref[...] = ((got_ref[0] + got_ref[1]) + (got_ref[2] + got_ref[3]))[:54]


def data_grad_body(low_ref, mine_ref, high_ref, weight_ref, out_ref, back):
    none = jnp.zeros((16, 256), BF16)
    total = jnp.zeros((256, 128), F32)
    for a in range(3):
        wide = (high_ref, mine_ref, low_ref)[a][...].astype(F32)
        for c in range(3):
            moved = x_shifted(wide, 1 - c).astype(BF16)
            for b in range(3):
                if b == 2:
                    shifted = jnp.concatenate([none, moved[:240]], axis=0)
                elif b == 0:
                    shifted = jnp.concatenate([moved[16:], none], axis=0)
                else:
                    shifted = moved
                tap = 9 * a + 3 * b + c
                total = total + lax.dot_general(
                    shifted,
                    weight_ref[128 * tap : 128 * tap + 128, :],
                    (((1,), (1,)), ((), ())),
                    preferred_element_type=F32,
                )
    out_ref[...] = total.astype(BF16)


def neighbours(block):
    count = 64
    up = [(i, i + 1) for i in range(count - 1)]
    down = [(i + 1, i) for i in range(count - 1)]
    return lax.ppermute(block, SPACE, up), lax.ppermute(block, SPACE, down)


def per_device(
    activations,
    conv_weight,
    conv_bias,
    cotangent,
    basis_panels,
    panel_owner,
    output_basis,
    input_eigen,
    output_eigen,
):
    place = jnp.stack([lax.axis_index("zh"), lax.axis_index("zl")]).astype(jnp.int32)
    inner = lax.axis_index(XC).astype(jnp.int32).reshape(1)
    plane = activations.reshape(256, 128)
    low, high = neighbours(plane)

    eigen = jnp.pad(input_eigen, (0, 10), constant_values=1.0).reshape(64, 1)
    stored = call(basis_body, shape((4, 64, 128), BF16), (basis_panels[0], eigen))
    turn = [(8 * a + b, 8 * b + a) for a in range(8) for b in range(8)]
    stored = lax.ppermute(stored, ("y", "zh", "zl"), turn)
    basis = lax.all_gather(stored, ZS)

    delta, send = call(
        forward_body,
        [shape((256, 256), BF16), shape((8, 384, 128), BF16)],
        (inner, low, plane, high, conv_weight, conv_bias.reshape(1, 256), cotangent.reshape(256, 256)),
        [pltpu.VMEM((256, 3456), BF16)],
        smem=1,
        flops=2 * 256 * 3456 * 256,
    )
    delta_low, delta_high = neighbours(delta)
    got = exchange(send, XC)
    part = call(
        weight_grad_body,
        shape((4, 224, 128), BF16),
        (got,),
        [pltpu.VMEM((288, 2560), BF16), pltpu.VMEM((2048, 128), BF16)],
        flops=2 * 864 * 2048 * 128,
    )
    part = call(
        over_y_body, shape((16, 32, 128), BF16), (exchange(part, "y"),), [pltpu.VMEM((224, 128), F32)]
    )
    part = call(over_z_body, shape((32, 32, 128), BF16), (exchange(part, ZS),))
    grads = exchange(part, YXC)
    data = call(
        data_grad_body,
        shape((256, 128), BF16),
        (delta_low, delta, delta_high, conv_weight),
        [pltpu.VMEM((256, 256), BF16)],
        flops=2 * 256 * 3456 * 256,
    )
    rotated = call(
        rotate_body, shape((16, 112, 128), BF16), (panel_owner, place, grads, basis), smem=2
    )
    rotated = exchange(rotated, ZS)
    part = call(
        update_body,
        shape((8, 64, 256), BF16),
        (panel_owner, place, rotated, basis, output_basis, output_eigen.reshape(1, 256)),
        smem=2,
    )
    part = call(over_xc_body, shape((4, 56, 256), F32), (exchange(part, XC),))
    update = call(last_body, shape((54, 256), F32), (exchange(part, "y"),))
    return (data.reshape(1, 1, 16, 16, 128), update)


def solution(mesh):
    fine = Mesh(mesh.devices.reshape(4, 2, 8, 4, 2), ("y", "zh", "zl", "x", "c"))
    both = P(YS, SPACE, None, None, None)
    return jax.shard_map(
        per_device,
        mesh=fine,
        in_specs=(both, P(), P(), both, P(YS, None, SPACE), P(), P(), P(SPACE), P()),
        out_specs=(both, P(SPACE, None)),
        check_vma=False,
    )
```

```python
import jax
import jax.numpy as jnp
from jax import lax
from jax.experimental import pallas as pl
from jax.experimental.pallas import tpu as pltpu
from jax.sharding import Mesh
from jax.sharding import PartitionSpec as P

DAMPING = 0.001
CELLS = 131072
BF16 = jnp.bfloat16
F32 = jnp.float32
VMEM = pl.BlockSpec(memory_space=pltpu.VMEM)
SMEM = pl.BlockSpec(memory_space=pltpu.SMEM)
LIMIT = 48 * 1024 * 1024
ANY = pl.BlockSpec(memory_space=pl.ANY)
AXES = ("y", "zh", "zg", "zl", "x", "c")
SIZES = (4, 2, 2, 4, 4, 2)
SAMPLE = ("y", "zh")
XC = ("x", "c")
YXC = ("y", "x", "c")
SPACE = ("zg", "zl", "x", "c")


def call(body, out_shape, scalars=(), arrays=(), remote=(), scratch=(), flops=0):
    many = isinstance(out_shape, (list, tuple))
    inputs = (*scalars, *arrays, *remote)
    return pl.pallas_call(
        body,
        out_shape=out_shape,
        in_specs=[SMEM] * len(scalars) + [VMEM] * len(arrays) + [ANY] * len(remote),
        out_specs=[VMEM] * len(out_shape) if many else VMEM,
        scratch_shapes=list(scratch),
        compiler_params=pltpu.CompilerParams(vmem_limit_bytes=LIMIT),
        cost_estimate=pl.CostEstimate(
            flops=flops,
            bytes_accessed=sum(a.size * a.dtype.itemsize for a in inputs),
            transcendentals=0,
        ),
    )(*inputs)


def shape(dims, dtype):
    return jax.ShapeDtypeStruct(dims, dtype)


def iota(dims, axis):
    return lax.broadcasted_iota(jnp.int32, dims, axis)


def exchange(x, axes):
    return lax.all_to_all(x, axes, 0, 0)


def started(copies):
    for copy in copies:
        copy.start()
    return copies


def x_shifted(rows, step):
    if step == 0:
        return rows
    x = iota(rows.shape, 0) & 15
    inside = (x + step >= 0) & (x + step < 16)
    return jnp.where(inside, pltpu.roll(rows, (-step) % 256, 0), 0.0)


def basis_body(panel, eigen_any, out_ref, eigen, sem):
    copy = pltpu.make_async_copy(eigen_any, eigen, sem)
    copy.start()
    copy.wait()
    row = iota((54, 54), 0)
    column = jnp.sum(jnp.where(row == iota((54, 54), 1), eigen[...], 0.0), axis=1, keepdims=True)
    column = jnp.concatenate([column, jnp.ones((10, 1), F32)], axis=0)
    first = column.astype(BF16).astype(F32)
    second = (column - first).astype(BF16).astype(F32)
    third = column - first - second
    for r in range(4):
        pick = iota((432, 128), 0) == 4 * iota((432, 128), 1) + r
        block = jnp.dot(panel[...], jnp.where(pick, 1.0, 0.0).astype(BF16), preferred_element_type=F32)
        block = jnp.concatenate([block, jnp.zeros((10, 128), F32)], axis=0)
        if r == 0:
            at = iota((64, 128), 1)
            block = jnp.where(at == 108, first, block)
            block = jnp.where(at == 109, second, block)
            block = jnp.where(at == 110, third, block)
        out_ref[r] = block.astype(BF16)


def pack_body(own_ref, other_ref, after_ref, out_ref):
    out_ref[0] = own_ref[...]
    out_ref[1] = other_ref[...]
    out_ref[2] = own_ref[...]
    out_ref[3] = other_ref[...]


def forward_body(
    place_ref, low_ref, high_ref, mine_any, weight_any, bias_any, cot_any,
    delta_ref, send_ref, patches, mine, weight, bias, cot, sems,
):
    copies = started(
        [
            pltpu.make_async_copy(source, target, sems.at[i])
            for i, (source, target) in enumerate(
                [(mine_any, mine), (weight_any, weight), (bias_any, bias), (cot_any, cot)]
            )
        ]
    )
    none = jnp.zeros((16, 128), BF16)
    for a in (0, 2, 1):
        if a == 1:
            copies[0].wait()
        wide = (low_ref, mine, high_ref)[a][...].astype(F32)
        for c in range(3):
            moved = x_shifted(wide, c - 1).astype(BF16)
            for b in range(3):
                at = (9 * a + 3 * b + c) * 128
                if b == 0:
                    shifted = jnp.concatenate([none, moved[:240]], axis=0)
                elif b == 2:
                    shifted = jnp.concatenate([moved[16:], none], axis=0)
                else:
                    shifted = moved
                patches[:, at : at + 128] = shifted
    for copy in copies[1:]:
        copy.wait()
    pre = jnp.dot(patches[...], weight[...], preferred_element_type=F32) + bias[...]
    logistic = 1.0 / (1.0 + jnp.exp(-pre))
    delta = (cot[...].astype(F32) * logistic * (1.0 + pre * (1.0 - logistic))).astype(BF16)
    delta_ref[...] = delta
    rim = jnp.where(place_ref[0] < 4, low_ref[...].astype(F32), high_ref[...].astype(F32))
    act_t = mine[...].astype(F32).T.astype(BF16)
    rim_t = rim.T.astype(BF16)
    for x in range(4):
        for c in range(2):
            to = 2 * x + c
            for half in range(2):
                lanes = slice(128 * half, 128 * half + 128)
                rows = slice(32 * x, 32 * x + 32)
                send_ref[to, 32 * half : 32 * half + 32] = act_t[rows, lanes]
                send_ref[to, 64 + 32 * half : 96 + 32 * half] = rim_t[rows, lanes]
            send_ref[to, 128:] = delta[:, 128 * c : 128 * c + 128]


def weight_grad_body(got_ref, out_ref, moved, deltas, whole):
    pieces = []
    for plane, at in [(0, 64)] + [(e, 0) for e in range(8)] + [(7, 64)]:
        pieces.append(got_ref[plane, at : at + 32].astype(F32))
        pieces.append(got_ref[plane, at + 32 : at + 64].astype(F32))
    acts = jnp.concatenate(pieces, axis=1)
    lane = iota((32, 2560), 1)
    x = lane & 15
    y = (lane >> 4) & 15
    for b in range(3):
        for c in range(3):
            step = 16 * (b - 1) + (c - 1)
            turned = pltpu.roll(acts, (-step) % 2560, 1) if step else acts
            inside = (x + c >= 1) & (x + c < 17) & (y + b >= 1) & (y + b < 17)
            moved[32 * (3 * b + c) : 32 * (3 * b + c) + 32, :] = jnp.where(inside, turned, 0.0).astype(BF16)
    for e in range(8):
        deltas[256 * e : 256 * e + 256, :] = got_ref[e, 128:]
    for a in range(3):
        whole[288 * a : 288 * a + 288, :] = jnp.dot(
            moved[:, 256 * a : 256 * a + 2048], deltas[...], preferred_element_type=F32
        )
    none = jnp.zeros((5, 128), F32)
    for y_to in range(4):
        for z_to in range(4):
            parts = []
            for e in range(2):
                parts.append(whole[pl.ds(8 * y_to + 4 * e + z_to, 27, stride=32), :])
                parts.append(none)
            out_ref[4 * y_to + z_to] = jnp.concatenate(parts, axis=0).astype(BF16)


def over_y_zl_body(got_ref, out_ref):
    total = sum(got_ref[i].astype(F32) for i in range(16)) * (1.0 / CELLS)
    for to in range(4):
        out_ref[to] = total.astype(BF16)


def over_zh_zg_body(got_ref, out_ref):
    total = ((got_ref[0].astype(F32) + got_ref[1].astype(F32)) + (got_ref[2].astype(F32) + got_ref[3].astype(F32))).astype(BF16)
    for to in range(32):
        out_ref[to] = total


def slot_of(owner, zh):
    return owner >> 1, (owner & 1) ^ zh


def rotate_body(owner_ref, place_ref, got_ref, basis_any, out_ref, basis, grads, ordered, sems):
    zh, zl = place_ref[0], place_ref[1]
    copies = []
    for j in range(8):
        first, second = slot_of(owner_ref[j], zh)
        copies.append(pltpu.make_async_copy(basis_any.at[first, second, zl], basis.at[j], sems.at[j]))
    started(copies)
    for y in range(4):
        for x in range(4):
            at = 32 * (8 * x + 2 * y)
            for c in range(2):
                grads[c, at : at + 64, :] = got_ref[8 * y + 2 * x + c].astype(F32)
    for tap in range(27):
        for c in range(2):
            ordered[32 * tap : 32 * tap + 32, 128 * c : 128 * c + 128] = grads[c, pl.ds(tap, 32, stride=32), :]
    ordered[864:, :] = jnp.zeros((32, 256), F32)
    inside = iota((64, 128), 1) < 108
    total = jnp.zeros((64, 256), F32)
    for j in range(8):
        copies[j].wait()
        block = jnp.where(inside, basis[j].astype(F32), 0.0).astype(BF16)
        rows = ordered[108 * j : 108 * j + 128, :].astype(BF16)
        total = total + jnp.dot(block, rows, preferred_element_type=F32)
    for to in range(4):
        out_ref[to] = total[:56]


def update_body(
    owner_ref, place_ref, got_ref, basis_any, out_basis_any, out_eigen_any,
    out_ref, basis, out_basis, out_eigen, ordered, sems,
):
    zh, zl = place_ref[0], place_ref[1]
    copies = [
        pltpu.make_async_copy(out_basis_any, out_basis, sems.at[0]),
        pltpu.make_async_copy(out_eigen_any, out_eigen, sems.at[1]),
    ]
    for g in range(2):
        first, second = slot_of(owner_ref[zl + 4 * g], zh)
        copies.append(pltpu.make_async_copy(basis_any.at[first, second], basis.at[g], sems.at[2 + g]))
    started(copies)
    highest = lax.Precision.HIGHEST
    rotated = (got_ref[0] + got_ref[1]) + (got_ref[2] + got_ref[3])
    rotated = jnp.concatenate([rotated, jnp.zeros((8, 256), F32)], axis=0)
    for copy in copies:
        copy.wait()
    rotated = jnp.dot(rotated, out_basis[...], precision=highest, preferred_element_type=F32)
    terms = basis[0, 0].astype(F32)
    eigen = (terms[:, 108:109] + terms[:, 109:110]) + terms[:, 110:111]
    scaled = rotated / (eigen * out_eigen[...] + DAMPING)
    scaled = jnp.where(iota((64, 256), 0) < 54, scaled, 0.0)
    turned = lax.dot_general(
        scaled, out_basis[...], (((1,), (1,)), ((), ())), precision=highest, preferred_element_type=F32
    )
    high = turned.astype(BF16)
    rest = (turned - high.astype(F32)).astype(BF16)
    for g in range(2):
        for r in range(4):
            block = basis[g, r].astype(F32).T.astype(BF16)
            rows = jnp.dot(block, high, preferred_element_type=F32) + jnp.dot(block, rest, preferred_element_type=F32)
            for c in range(2):
                ordered[g, c, pl.ds(r, 108, stride=4), :] = rows[:108, 128 * c : 128 * c + 128]
        for c in range(2):
            ordered[g, c, 432:, :] = jnp.zeros((8, 128), F32)
    for c in range(2):
        for to in range(8):
            rows = [ordered[g, c, 54 * to : 54 * to + 56, :] for g in range(2)]
            out_ref[to, :, 128 * c : 128 * c + 128] = jnp.concatenate(rows, axis=0).astype(BF16)


def over_xc_body(got_ref, out_ref):
    total = sum(got_ref[i].astype(F32) for i in range(8))
    for g in range(2):
        rows = total[56 * g : 56 * g + 56]
        rows = jnp.concatenate([rows[:, :128], rows[:, 128:]], axis=0).astype(BF16)
        for y in range(4):
            out_ref[4 * g + y] = rows


def last_body(got_ref, out_ref):
    total = sum(got_ref[i].astype(F32) for i in range(8))
    out_ref[...] = jnp.concatenate([total[:54], total[56:110]], axis=1)


def data_grad_body(low_ref, high_ref, mine_ref, weight_any, out_ref, weight, sem):
    copy = pltpu.make_async_copy(weight_any, weight, sem)
    copy.start()
    none = jnp.zeros((16, 256), BF16)
    total = jnp.zeros((256, 128), F32)
    for a in range(3):
        wide = (high_ref, mine_ref, low_ref)[a][...].astype(F32)
        if a == 0:
            copy.wait()
        for c in range(3):
            moved = x_shifted(wide, 1 - c).astype(BF16)
            for b in range(3):
                if b == 2:
                    shifted = jnp.concatenate([none, moved[:240]], axis=0)
                elif b == 0:
                    shifted = jnp.concatenate([moved[16:], none], axis=0)
                else:
                    shifted = moved
                tap = 9 * a + 3 * b + c
                total = total + lax.dot_general(
                    shifted,
                    weight[128 * tap : 128 * tap + 128, :],
                    (((1,), (1,)), ((), ())),
                    preferred_element_type=F32,
                )
    out_ref[...] = total.astype(BF16)


def neighbours(block):
    count = 64
    up = [(i, i + 1) for i in range(count - 1)]
    down = [(i + 1, i) for i in range(count - 1)]
    return lax.ppermute(block, SPACE, up), lax.ppermute(block, SPACE, down)


def turned(block, flip):
    pairs = [
        (8 * y + 4 * zh + z, 8 * z + 4 * (zh ^ flip) + y) for y in range(4) for zh in range(2) for z in range(4)
    ]
    return lax.ppermute(block, ("y", "zh", "zl"), pairs)


def per_device(
    activations,
    conv_weight,
    conv_bias,
    cotangent,
    basis_panels,
    panel_owner,
    output_basis,
    input_eigen,
    output_eigen,
):
    dma = pltpu.SemaphoreType.DMA
    place = jnp.stack([lax.axis_index("zh"), lax.axis_index("zl")]).astype(jnp.int32)
    inner = lax.axis_index(XC).astype(jnp.int32).reshape(1)
    plane = activations.reshape(256, 128)
    low, high = neighbours(plane)

    stored = call(
        basis_body,
        shape((4, 64, 128), BF16),
        arrays=(basis_panels[0].T,),
        remote=(input_eigen.reshape(1, 54),),
        scratch=[pltpu.VMEM((1, 54), F32), dma],
    )
    own, other = turned(stored, 0), turned(stored, 1)

    delta, send = call(
        forward_body,
        [shape((256, 256), BF16), shape((8, 384, 128), BF16)],
        (inner,),
        (low, high),
        (plane, conv_weight, conv_bias.reshape(1, 256), cotangent.reshape(256, 256)),
        [
            pltpu.VMEM((256, 3456), BF16),
            pltpu.VMEM((256, 128), BF16),
            pltpu.VMEM((3456, 256), BF16),
            pltpu.VMEM((1, 256), F32),
            pltpu.VMEM((256, 256), BF16),
            dma((4,)),
        ],
        flops=2 * 256 * 3456 * 256,
    )
    packed = call(pack_body, shape((4, 4, 64, 128), BF16), arrays=(own, other), remote=(delta,))
    basis = lax.all_gather(packed, "zl")
    delta_low, delta_high = neighbours(delta)
    got = exchange(send, XC)
    part = call(
        weight_grad_body,
        shape((16, 64, 128), BF16),
        arrays=(got,),
        scratch=[pltpu.VMEM((288, 2560), BF16), pltpu.VMEM((2048, 128), BF16), pltpu.VMEM((864, 128), F32)],
        flops=2 * 864 * 2048 * 128,
    )
    part = call(over_y_zl_body, shape((4, 64, 128), BF16), arrays=(exchange(part, ("y", "zl")),))
    part = call(over_zh_zg_body, shape((32, 64, 128), BF16), arrays=(exchange(part, ("zh", "zg")),))
    grads = exchange(part, YXC)
    data = call(
        data_grad_body,
        shape((256, 128), BF16),
        arrays=(delta_low, delta_high, delta),
        remote=(conv_weight,),
        scratch=[pltpu.VMEM((3456, 256), BF16), dma],
        flops=2 * 256 * 3456 * 256,
    )
    rotated = call(
        rotate_body,
        shape((4, 56, 256), F32),
        (panel_owner, place),
        (grads,),
        (basis,),
        [
            pltpu.VMEM((8, 64, 128), BF16),
            pltpu.VMEM((2, 1024, 128), F32),
            pltpu.VMEM((896, 256), F32),
            dma((8,)),
        ],
    )
    part = call(
        update_body,
        shape((8, 112, 256), BF16),
        (panel_owner, place),
        (exchange(rotated, "zl"),),
        (basis, output_basis, output_eigen.reshape(1, 256)),
        [
            pltpu.VMEM((2, 4, 64, 128), BF16),
            pltpu.VMEM((256, 256), F32),
            pltpu.VMEM((1, 256), F32),
            pltpu.VMEM((2, 2, 440, 128), F32),
            dma((4,)),
        ],
    )
    part = call(over_xc_body, shape((8, 112, 128), BF16), arrays=(exchange(part, XC),))
    update = call(last_body, shape((54, 256), F32), arrays=(exchange(part, ("zg", "y")),))
    return (data.reshape(1, 1, 16, 16, 128), update)


def solution(mesh):
    fine = Mesh(mesh.devices.reshape(SIZES), AXES)
    both = P(SAMPLE, SPACE, None, None, None)
    return jax.shard_map(
        per_device,
        mesh=fine,
        in_specs=(both, P(), P(), both, P(SAMPLE, None, SPACE), P(), P(), P(SPACE), P()),
        out_specs=(both, P(SPACE, None)),
        check_vma=False,
    )
```

```python
import jax
import jax.numpy as jnp
from jax import lax
from jax.experimental import pallas as pl
from jax.experimental.pallas import tpu as pltpu
from jax.sharding import Mesh
from jax.sharding import PartitionSpec as P

DAMPING = 0.001
CELLS = 131072
BF16 = jnp.bfloat16
F32 = jnp.float32
VMEM = pl.BlockSpec(memory_space=pltpu.VMEM)
SMEM = pl.BlockSpec(memory_space=pltpu.SMEM)
LIMIT = 48 * 1024 * 1024
ANY = pl.BlockSpec(memory_space=pl.ANY)
AXES = ("y", "zh", "zg", "zl", "x", "c")
SIZES = (4, 2, 2, 4, 4, 2)
SAMPLE = ("y", "zh")
XC = ("x", "c")
YXC = ("y", "x", "c")
SPACE = ("zg", "zl", "x", "c")


def call(body, out_shape, scalars=(), arrays=(), remote=(), after=(), scratch=(), flops=0, limit=LIMIT):
    many = isinstance(out_shape, (list, tuple))
    inputs = (*scalars, *arrays, *remote, *after)
    kept = len(inputs) - len(after)

    def kernel(*refs):
        body(*refs[:kept], *refs[len(inputs) :])

    return pl.pallas_call(
        kernel,
        out_shape=out_shape,
        in_specs=[SMEM] * len(scalars) + [VMEM] * len(arrays) + [ANY] * (len(remote) + len(after)),
        out_specs=[VMEM] * len(out_shape) if many else VMEM,
        scratch_shapes=list(scratch),
        compiler_params=pltpu.CompilerParams(vmem_limit_bytes=limit),
        cost_estimate=pl.CostEstimate(
            flops=flops,
            bytes_accessed=sum(a.size * a.dtype.itemsize for a in inputs),
            transcendentals=0,
        ),
    )(*inputs)


def shape(dims, dtype):
    return jax.ShapeDtypeStruct(dims, dtype)


def iota(dims, axis):
    return lax.broadcasted_iota(jnp.int32, dims, axis)


def exchange(x, axes):
    return lax.all_to_all(x, axes, 0, 0)


def started(copies):
    for copy in copies:
        copy.start()
    return copies


def x_shifted(rows, step):
    if step == 0:
        return rows
    x = iota(rows.shape, 0) & 15
    inside = (x + step >= 0) & (x + step < 16)
    return jnp.where(inside, pltpu.roll(rows, (-step) % 256, 0), 0.0)


def basis_body(panel, eigen_any, out_ref, eigen, sem):
    copy = pltpu.make_async_copy(eigen_any, eigen, sem)
    copy.start()
    copy.wait()
    row = iota((54, 54), 0)
    column = jnp.sum(jnp.where(row == iota((54, 54), 1), eigen[...], 0.0), axis=1, keepdims=True)
    column = jnp.concatenate([column, jnp.ones((10, 1), F32)], axis=0)
    first = column.astype(BF16).astype(F32)
    second = (column - first).astype(BF16).astype(F32)
    third = column - first - second
    for r in range(4):
        pick = iota((432, 128), 0) == 4 * iota((432, 128), 1) + r
        block = jnp.dot(panel[...], jnp.where(pick, 1.0, 0.0).astype(BF16), preferred_element_type=F32)
        block = jnp.concatenate([block, jnp.zeros((10, 128), F32)], axis=0)
        if r == 0:
            at = iota((64, 128), 1)
            block = jnp.where(at == 108, first, block)
            block = jnp.where(at == 109, second, block)
            block = jnp.where(at == 110, third, block)
        out_ref[r] = block.astype(BF16)


def pack_body(own_ref, other_ref, out_ref):
    out_ref[0] = own_ref[...]
    out_ref[1] = other_ref[...]
    out_ref[2] = own_ref[...]
    out_ref[3] = other_ref[...]


def forward_body(
    place_ref, low_ref, high_ref, mine_any, weight_any, bias_any, cot_any,
    delta_ref, send_ref, patches, mine, weight, bias, cot, sems,
):
    copies = started(
        [
            pltpu.make_async_copy(source, target, sems.at[i])
            for i, (source, target) in enumerate(
                [(mine_any, mine), (weight_any, weight), (bias_any, bias), (cot_any, cot)]
            )
        ]
    )
    none = jnp.zeros((16, 128), BF16)
    for a in (0, 2, 1):
        if a == 1:
            copies[0].wait()
        wide = (low_ref, mine, high_ref)[a][...].astype(F32)
        for c in range(3):
            moved = x_shifted(wide, c - 1).astype(BF16)
            for b in range(3):
                at = (9 * a + 3 * b + c) * 128
                if b == 0:
                    shifted = jnp.concatenate([none, moved[:240]], axis=0)
                elif b == 2:
                    shifted = jnp.concatenate([moved[16:], none], axis=0)
                else:
                    shifted = moved
                patches[:, at : at + 128] = shifted
    for copy in copies[1:]:
        copy.wait()
    pre = jnp.dot(patches[...], weight[...], preferred_element_type=F32) + bias[...]
    logistic = 1.0 / (1.0 + jnp.exp(-pre))
    delta = (cot[...].astype(F32) * logistic * (1.0 + pre * (1.0 - logistic))).astype(BF16)
    delta_ref[...] = delta
    rim = jnp.where(place_ref[0] < 4, low_ref[...].astype(F32), high_ref[...].astype(F32))
    act_t = mine[...].astype(F32).T.astype(BF16)
    rim_t = rim.T.astype(BF16)
    for x in range(4):
        for c in range(2):
            to = 2 * x + c
            for half in range(2):
                lanes = slice(128 * half, 128 * half + 128)
                rows = slice(32 * x, 32 * x + 32)
                send_ref[to, 32 * half : 32 * half + 32] = act_t[rows, lanes]
                send_ref[to, 64 + 32 * half : 96 + 32 * half] = rim_t[rows, lanes]
            send_ref[to, 128:] = delta[:, 128 * c : 128 * c + 128]


def weight_grad_body(got_ref, out_ref, moved, deltas, whole):
    pieces = []
    for plane, at in [(0, 64)] + [(e, 0) for e in range(8)] + [(7, 64)]:
        pieces.append(got_ref[plane, at : at + 32].astype(F32))
        pieces.append(got_ref[plane, at + 32 : at + 64].astype(F32))
    acts = jnp.concatenate(pieces, axis=1)
    lane = iota((32, 2560), 1)
    x = lane & 15
    y = (lane >> 4) & 15
    for b in range(3):
        for c in range(3):
            step = 16 * (b - 1) + (c - 1)
            turned = pltpu.roll(acts, (-step) % 2560, 1) if step else acts
            inside = (x + c >= 1) & (x + c < 17) & (y + b >= 1) & (y + b < 17)
            moved[32 * (3 * b + c) : 32 * (3 * b + c) + 32, :] = jnp.where(inside, turned, 0.0).astype(BF16)
    for e in range(8):
        deltas[256 * e : 256 * e + 256, :] = got_ref[e, 128:]
    for a in range(3):
        whole[288 * a : 288 * a + 288, :] = jnp.dot(
            moved[:, 256 * a : 256 * a + 2048], deltas[...], preferred_element_type=F32
        )
    none = jnp.zeros((5, 128), F32)
    for y_to in range(4):
        for z_to in range(4):
            parts = []
            for e in range(2):
                parts.append(whole[pl.ds(8 * y_to + 4 * e + z_to, 27, stride=32), :])
                parts.append(none)
            out_ref[4 * y_to + z_to] = jnp.concatenate(parts, axis=0).astype(BF16)


def over_y_zl_body(got_ref, out_ref):
    total = sum(got_ref[i].astype(F32) for i in range(16)) * (1.0 / CELLS)
    for to in range(4):
        out_ref[to] = total.astype(BF16)


def over_zh_zg_body(got_ref, out_ref):
    total = ((got_ref[0].astype(F32) + got_ref[1].astype(F32)) + (got_ref[2].astype(F32) + got_ref[3].astype(F32))).astype(BF16)
    for to in range(32):
        out_ref[to] = total


def slot_of(owner, zh):
    return owner >> 1, (owner & 1) ^ zh


def rotate_body(owner_ref, place_ref, got_ref, basis_any, out_ref, panels_ref, basis, grads, ordered, sems):
    zh, zl = place_ref[0], place_ref[1]
    copies = []
    for j in range(8):
        first, second = slot_of(owner_ref[j], zh)
        copies.append(pltpu.make_async_copy(basis_any.at[first, second, zl], basis.at[j], sems.at[j]))
    for g in range(2):
        first, second = slot_of(owner_ref[zl + 4 * g], zh)
        copies.append(pltpu.make_async_copy(basis_any.at[first, second], panels_ref.at[g], sems.at[8 + g]))
    started(copies)
    for y in range(4):
        for x in range(4):
            at = 32 * (8 * x + 2 * y)
            for c in range(2):
                grads[c, at : at + 64, :] = got_ref[8 * y + 2 * x + c].astype(F32)
    for tap in range(27):
        for c in range(2):
            ordered[32 * tap : 32 * tap + 32, 128 * c : 128 * c + 128] = grads[c, pl.ds(tap, 32, stride=32), :]
    ordered[864:, :] = jnp.zeros((32, 256), F32)
    inside = iota((64, 128), 1) < 108
    total = jnp.zeros((64, 256), F32)
    for j in range(8):
        copies[j].wait()
        block = jnp.where(inside, basis[j].astype(F32), 0.0).astype(BF16)
        rows = ordered[108 * j : 108 * j + 128, :].astype(BF16)
        total = total + jnp.dot(block, rows, preferred_element_type=F32)
    for to in range(4):
        out_ref[to] = total[:56]
    for copy in copies[8:]:
        copy.wait()


def update_body(
    got_ref, basis, out_basis_any, out_eigen_any, out_ref, out_basis, out_eigen, ordered, sems
):
    copies = [
        pltpu.make_async_copy(out_basis_any, out_basis, sems.at[0]),
        pltpu.make_async_copy(out_eigen_any, out_eigen, sems.at[1]),
    ]
    started(copies)
    highest = lax.Precision.HIGHEST
    rotated = (got_ref[0] + got_ref[1]) + (got_ref[2] + got_ref[3])
    rotated = jnp.concatenate([rotated, jnp.zeros((8, 256), F32)], axis=0)
    for copy in copies:
        copy.wait()
    rotated = jnp.dot(rotated, out_basis[...], precision=highest, preferred_element_type=F32)
    terms = basis[0, 0].astype(F32)
    eigen = (terms[:, 108:109] + terms[:, 109:110]) + terms[:, 110:111]
    scaled = rotated / (eigen * out_eigen[...] + DAMPING)
    scaled = jnp.where(iota((64, 256), 0) < 54, scaled, 0.0)
    turned = lax.dot_general(
        scaled, out_basis[...], (((1,), (1,)), ((), ())), precision=highest, preferred_element_type=F32
    )
    high = turned.astype(BF16)
    rest = (turned - high.astype(F32)).astype(BF16)
    for g in range(2):
        for r in range(4):
            block = basis[g, r].astype(F32).T.astype(BF16)
            rows = jnp.dot(block, high, preferred_element_type=F32) + jnp.dot(block, rest, preferred_element_type=F32)
            for c in range(2):
                ordered[g, c, pl.ds(r, 108, stride=4), :] = rows[:108, 128 * c : 128 * c + 128]
        for c in range(2):
            ordered[g, c, 432:, :] = jnp.zeros((8, 128), F32)
    for c in range(2):
        for to in range(8):
            rows = [ordered[g, c, 54 * to : 54 * to + 56, :] for g in range(2)]
            out_ref[to, :, 128 * c : 128 * c + 128] = jnp.concatenate(rows, axis=0).astype(BF16)


def over_xc_body(got_ref, out_ref):
    total = sum(got_ref[i].astype(F32) for i in range(8))
    for g in range(2):
        rows = total[56 * g : 56 * g + 56]
        rows = jnp.concatenate([rows[:, :128], rows[:, 128:]], axis=0).astype(BF16)
        for y in range(4):
            out_ref[4 * g + y] = rows


def last_body(got_ref, out_ref):
    total = sum(got_ref[i].astype(F32) for i in range(8))
    out_ref[...] = jnp.concatenate([total[:54], total[56:110]], axis=1)


def data_grad_body(low_ref, high_ref, mine_ref, weight_any, out_ref, token_ref, weight, sem):
    copy = pltpu.make_async_copy(weight_any, weight, sem)
    copy.start()
    none = jnp.zeros((16, 256), BF16)
    total = jnp.zeros((256, 128), F32)
    for a in range(3):
        wide = (high_ref, mine_ref, low_ref)[a][...].astype(F32)
        if a == 0:
            copy.wait()
        for c in range(3):
            moved = x_shifted(wide, 1 - c).astype(BF16)
            for b in range(3):
                if b == 2:
                    shifted = jnp.concatenate([none, moved[:240]], axis=0)
                elif b == 0:
                    shifted = jnp.concatenate([moved[16:], none], axis=0)
                else:
                    shifted = moved
                tap = 9 * a + 3 * b + c
                total = total + lax.dot_general(
                    shifted,
                    weight[128 * tap : 128 * tap + 128, :],
                    (((1,), (1,)), ((), ())),
                    preferred_element_type=F32,
                )
    out_ref[...] = total.astype(BF16)
    token_ref[...] = jnp.zeros((8, 128), F32)


def neighbours(block):
    count = 64
    up = [(i, i + 1) for i in range(count - 1)]
    down = [(i + 1, i) for i in range(count - 1)]
    return lax.ppermute(block, SPACE, up), lax.ppermute(block, SPACE, down)


def turned(block, flip):
    pairs = [
        (8 * y + 4 * zh + z, 8 * z + 4 * (zh ^ flip) + y) for y in range(4) for zh in range(2) for z in range(4)
    ]
    return lax.ppermute(block, ("y", "zh", "zl"), pairs)


def per_device(
    activations,
    conv_weight,
    conv_bias,
    cotangent,
    basis_panels,
    panel_owner,
    output_basis,
    input_eigen,
    output_eigen,
):
    dma = pltpu.SemaphoreType.DMA
    place = jnp.stack([lax.axis_index("zh"), lax.axis_index("zl")]).astype(jnp.int32)
    inner = lax.axis_index(XC).astype(jnp.int32).reshape(1)
    plane = activations.reshape(256, 128)
    low, high = neighbours(plane)

    stored = call(
        basis_body,
        shape((4, 64, 128), BF16),
        arrays=(basis_panels[0].T,),
        remote=(input_eigen.reshape(1, 54),),
        scratch=[pltpu.VMEM((1, 54), F32), dma],
        flops=4_000_000_000,
    )
    own, other = turned(stored, 0), turned(stored, 1)

    delta, send = call(
        forward_body,
        [shape((256, 256), BF16), shape((8, 384, 128), BF16)],
        (inner,),
        (low, high),
        (plane, conv_weight, conv_bias.reshape(1, 256), cotangent.reshape(256, 256)),
        (own,),
        [
            pltpu.VMEM((256, 3456), BF16),
            pltpu.VMEM((256, 128), BF16),
            pltpu.VMEM((3456, 256), BF16),
            pltpu.VMEM((1, 256), F32),
            pltpu.VMEM((256, 256), BF16),
            dma((4,)),
        ],
        flops=2 * 256 * 3456 * 256,
    )
    delta_low, delta_high = neighbours(delta)
    got = exchange(send, XC)
    part = call(
        weight_grad_body,
        shape((16, 64, 128), BF16),
        arrays=(got,),
        after=(other, delta_low, delta_high),
        scratch=[pltpu.VMEM((288, 2560), BF16), pltpu.VMEM((2048, 128), BF16), pltpu.VMEM((864, 128), F32)],
        flops=2 * 864 * 2048 * 128,
    )
    packed = call(pack_body, shape((4, 4, 64, 128), BF16), arrays=(own, other), after=(part,))
    basis = lax.all_gather(packed, "zl")
    data, token = call(
        data_grad_body,
        [shape((256, 128), BF16), shape((8, 128), F32)],
        arrays=(delta_low, delta_high, delta),
        remote=(conv_weight,),
        after=(part,),
        scratch=[pltpu.VMEM((3456, 256), BF16), dma],
        flops=2 * 256 * 3456 * 256,
    )
    part = call(over_y_zl_body, shape((4, 64, 128), BF16), arrays=(exchange(part, ("y", "zl")),), after=(token,))
    part = call(over_zh_zg_body, shape((32, 64, 128), BF16), arrays=(exchange(part, ("zh", "zg")),))
    grads = exchange(part, YXC)
    rotated, panels = call(
        rotate_body,
        [shape((4, 56, 256), F32), shape((2, 4, 64, 128), BF16)],
        (panel_owner, place),
        (grads,),
        (basis,),
        scratch=[
            pltpu.VMEM((8, 64, 128), BF16),
            pltpu.VMEM((2, 1024, 128), F32),
            pltpu.VMEM((896, 256), F32),
            dma((10,)),
        ],
        limit=LIMIT + 15_000_000,
    )
    part = call(
        update_body,
        shape((8, 112, 256), BF16),
        (),
        (exchange(rotated, "zl"), panels),
        (output_basis, output_eigen.reshape(1, 256)),
        scratch=[
            pltpu.VMEM((256, 256), F32),
            pltpu.VMEM((1, 256), F32),
            pltpu.VMEM((2, 2, 440, 128), F32),
            dma((2,)),
        ],
    )
    part = call(over_xc_body, shape((8, 112, 128), BF16), arrays=(exchange(part, XC),))
    update = call(last_body, shape((54, 256), F32), arrays=(exchange(part, ("zg", "y")),))
    return (data.reshape(1, 1, 16, 16, 128), update)


def solution(mesh):
    fine = Mesh(mesh.devices.reshape(SIZES), AXES)
    both = P(SAMPLE, SPACE, None, None, None)
    return jax.shard_map(
        per_device,
        mesh=fine,
        in_specs=(both, P(), P(), both, P(SAMPLE, None, SPACE), P(), P(), P(SPACE), P()),
        out_specs=(both, P(SPACE, None)),
        check_vma=False,
    )
```

```python
import jax
import jax.numpy as jnp
from jax import lax
from jax.experimental import pallas as pl
from jax.experimental.pallas import tpu as pltpu
from jax.sharding import Mesh
from jax.sharding import PartitionSpec as P

DAMPING = 0.001
CELLS = 131072
BF16 = jnp.bfloat16
F32 = jnp.float32
VMEM = pl.BlockSpec(memory_space=pltpu.VMEM)
SMEM = pl.BlockSpec(memory_space=pltpu.SMEM)
LIMIT = 48 * 1024 * 1024
ANY = pl.BlockSpec(memory_space=pl.ANY)
AXES = ("y", "zh", "zg", "zl", "x", "c")
SIZES = (4, 2, 2, 4, 4, 2)
SAMPLE = ("y", "zh")
XC = ("x", "c")
YXC = ("y", "x", "c")
SPACE = ("zg", "zl", "x", "c")


def call(body, out_shape, scalars=(), arrays=(), remote=(), after=(), scratch=(), flops=0, limit=LIMIT):
    many = isinstance(out_shape, (list, tuple))
    inputs = (*scalars, *arrays, *remote, *after)
    kept = len(inputs) - len(after)

    def kernel(*refs):
        body(*refs[:kept], *refs[len(inputs) :])

    return pl.pallas_call(
        kernel,
        out_shape=out_shape,
        in_specs=[SMEM] * len(scalars) + [VMEM] * len(arrays) + [ANY] * (len(remote) + len(after)),
        out_specs=[VMEM] * len(out_shape) if many else VMEM,
        scratch_shapes=list(scratch),
        compiler_params=pltpu.CompilerParams(vmem_limit_bytes=limit),
        cost_estimate=pl.CostEstimate(
            flops=flops,
            bytes_accessed=sum(a.size * a.dtype.itemsize for a in inputs),
            transcendentals=0,
        ),
    )(*inputs)


def shape(dims, dtype):
    return jax.ShapeDtypeStruct(dims, dtype)


def iota(dims, axis):
    return lax.broadcasted_iota(jnp.int32, dims, axis)


def exchange(x, axes):
    return lax.all_to_all(x, axes, 0, 0)


def started(copies):
    for copy in copies:
        copy.start()
    return copies


def x_shifted(rows, step):
    if step == 0:
        return rows
    x = iota(rows.shape, 0) & 15
    inside = (x + step >= 0) & (x + step < 16)
    return jnp.where(inside, pltpu.roll(rows, (-step) % 256, 0), 0.0)


def basis_body(panel, eigen_any, out_ref, eigen, sem):
    copy = pltpu.make_async_copy(eigen_any, eigen, sem)
    copy.start()
    copy.wait()
    row = iota((54, 54), 0)
    column = jnp.sum(jnp.where(row == iota((54, 54), 1), eigen[...], 0.0), axis=1, keepdims=True)
    column = jnp.concatenate([column, jnp.ones((10, 1), F32)], axis=0)
    first = column.astype(BF16).astype(F32)
    second = (column - first).astype(BF16).astype(F32)
    third = column - first - second
    for r in range(4):
        pick = iota((432, 128), 0) == 4 * iota((432, 128), 1) + r
        block = jnp.dot(panel[...], jnp.where(pick, 1.0, 0.0).astype(BF16), preferred_element_type=F32)
        block = jnp.concatenate([block, jnp.zeros((10, 128), F32)], axis=0)
        if r == 0:
            at = iota((64, 128), 1)
            block = jnp.where(at == 108, first, block)
            block = jnp.where(at == 109, second, block)
            block = jnp.where(at == 110, third, block)
        out_ref[r] = block.astype(BF16)


def forward_body(
    place_ref, low_ref, high_ref, basis_ref, mine_any, weight_any, bias_any, cot_any,
    delta_ref, send_ref, twice_ref, patches, mine, weight, bias, cot, sems,
):
    copies = started(
        [
            pltpu.make_async_copy(source, target, sems.at[i])
            for i, (source, target) in enumerate(
                [(mine_any, mine), (weight_any, weight), (bias_any, bias), (cot_any, cot)]
            )
        ]
    )
    twice_ref[0] = basis_ref[...]
    twice_ref[1] = basis_ref[...]
    none = jnp.zeros((16, 128), BF16)
    for a in (0, 2, 1):
        if a == 1:
            copies[0].wait()
        wide = (low_ref, mine, high_ref)[a][...].astype(F32)
        for c in range(3):
            moved = x_shifted(wide, c - 1).astype(BF16)
            for b in range(3):
                at = (9 * a + 3 * b + c) * 128
                if b == 0:
                    shifted = jnp.concatenate([none, moved[:240]], axis=0)
                elif b == 2:
                    shifted = jnp.concatenate([moved[16:], none], axis=0)
                else:
                    shifted = moved
                patches[:, at : at + 128] = shifted
    for copy in copies[1:]:
        copy.wait()
    pre = jnp.dot(patches[...], weight[...], preferred_element_type=F32) + bias[...]
    logistic = 1.0 / (1.0 + jnp.exp(-pre))
    delta = (cot[...].astype(F32) * logistic * (1.0 + pre * (1.0 - logistic))).astype(BF16)
    delta_ref[...] = delta
    rim = jnp.where(place_ref[0] < 4, low_ref[...].astype(F32), high_ref[...].astype(F32))
    act_t = mine[...].astype(F32).T.astype(BF16)
    rim_t = rim.T.astype(BF16)
    for x in range(4):
        for c in range(2):
            to = 2 * x + c
            for half in range(2):
                lanes = slice(128 * half, 128 * half + 128)
                rows = slice(32 * x, 32 * x + 32)
                send_ref[to, 32 * half : 32 * half + 32] = act_t[rows, lanes]
                send_ref[to, 64 + 32 * half : 96 + 32 * half] = rim_t[rows, lanes]
            send_ref[to, 128:] = delta[:, 128 * c : 128 * c + 128]


def weight_grad_body(got_ref, out_ref, moved, deltas, whole):
    pieces = []
    for plane, at in [(0, 64)] + [(e, 0) for e in range(8)] + [(7, 64)]:
        pieces.append(got_ref[plane, at : at + 32].astype(F32))
        pieces.append(got_ref[plane, at + 32 : at + 64].astype(F32))
    acts = jnp.concatenate(pieces, axis=1)
    lane = iota((32, 2560), 1)
    x = lane & 15
    y = (lane >> 4) & 15
    for b in range(3):
        for c in range(3):
            step = 16 * (b - 1) + (c - 1)
            turned = pltpu.roll(acts, (-step) % 2560, 1) if step else acts
            inside = (x + c >= 1) & (x + c < 17) & (y + b >= 1) & (y + b < 17)
            moved[32 * (3 * b + c) : 32 * (3 * b + c) + 32, :] = jnp.where(inside, turned, 0.0).astype(BF16)
    for e in range(8):
        deltas[256 * e : 256 * e + 256, :] = got_ref[e, 128:]
    for a in range(3):
        whole[288 * a : 288 * a + 288, :] = jnp.dot(
            moved[:, 256 * a : 256 * a + 2048], deltas[...], preferred_element_type=F32
        )
    none = jnp.zeros((5, 128), F32)
    for y_to in range(4):
        for z_to in range(4):
            parts = []
            for e in range(2):
                parts.append(whole[pl.ds(8 * y_to + 4 * e + z_to, 27, stride=32), :])
                parts.append(none)
            out_ref[4 * y_to + z_to] = jnp.concatenate(parts, axis=0).astype(BF16)


def over_y_zl_body(got_ref, out_ref):
    total = sum(got_ref[i].astype(F32) for i in range(16)) * (1.0 / CELLS)
    for to in range(4):
        out_ref[to] = total.astype(BF16)


def over_zh_zg_body(got_ref, out_ref):
    total = ((got_ref[0].astype(F32) + got_ref[1].astype(F32)) + (got_ref[2].astype(F32) + got_ref[3].astype(F32))).astype(BF16)
    for to in range(32):
        out_ref[to] = total


def slot_of(owner):
    return 4 * (owner & 1) + (owner >> 1)


def rotate_body(owner_ref, place_ref, got_ref, basis_any, out_ref, panels_ref, basis, grads, ordered, sems):
    zl = place_ref[0]
    copies = []
    for j in range(8):
        slot = slot_of(owner_ref[j])
        copies.append(pltpu.make_async_copy(basis_any.at[slot, 0, zl], basis.at[j], sems.at[j]))
    for g in range(2):
        slot = slot_of(owner_ref[zl + 4 * g])
        copies.append(pltpu.make_async_copy(basis_any.at[slot, 0], panels_ref.at[g], sems.at[8 + g]))
    started(copies)
    for y in range(4):
        for x in range(4):
            at = 32 * (8 * x + 2 * y)
            for c in range(2):
                grads[c, at : at + 64, :] = got_ref[8 * y + 2 * x + c].astype(F32)
    for tap in range(27):
        for c in range(2):
            ordered[32 * tap : 32 * tap + 32, 128 * c : 128 * c + 128] = grads[c, pl.ds(tap, 32, stride=32), :]
    ordered[864:, :] = jnp.zeros((32, 256), F32)
    inside = iota((64, 128), 1) < 108
    total = jnp.zeros((64, 256), F32)
    for j in range(8):
        copies[j].wait()
        block = jnp.where(inside, basis[j].astype(F32), 0.0).astype(BF16)
        rows = ordered[108 * j : 108 * j + 128, :].astype(BF16)
        total = total + jnp.dot(block, rows, preferred_element_type=F32)
    for to in range(4):
        out_ref[to] = total[:56]
    for copy in copies[8:]:
        copy.wait()


def update_body(
    got_ref, basis, out_basis_any, out_eigen_any, out_ref, out_basis, out_eigen, ordered, sems
):
    copies = [
        pltpu.make_async_copy(out_basis_any, out_basis, sems.at[0]),
        pltpu.make_async_copy(out_eigen_any, out_eigen, sems.at[1]),
    ]
    started(copies)
    highest = lax.Precision.HIGHEST
    rotated = (got_ref[0] + got_ref[1]) + (got_ref[2] + got_ref[3])
    rotated = jnp.concatenate([rotated, jnp.zeros((8, 256), F32)], axis=0)
    for copy in copies:
        copy.wait()
    rotated = jnp.dot(rotated, out_basis[...], precision=highest, preferred_element_type=F32)
    terms = basis[0, 0].astype(F32)
    eigen = (terms[:, 108:109] + terms[:, 109:110]) + terms[:, 110:111]
    scaled = rotated / (eigen * out_eigen[...] + DAMPING)
    scaled = jnp.where(iota((64, 256), 0) < 54, scaled, 0.0)
    turned = lax.dot_general(
        scaled, out_basis[...], (((1,), (1,)), ((), ())), precision=highest, preferred_element_type=F32
    )
    high = turned.astype(BF16)
    rest = (turned - high.astype(F32)).astype(BF16)
    for g in range(2):
        for r in range(4):
            block = basis[g, r].astype(F32).T.astype(BF16)
            rows = jnp.dot(block, high, preferred_element_type=F32) + jnp.dot(block, rest, preferred_element_type=F32)
            for c in range(2):
                ordered[g, c, pl.ds(r, 108, stride=4), :] = rows[:108, 128 * c : 128 * c + 128]
        for c in range(2):
            ordered[g, c, 432:, :] = jnp.zeros((8, 128), F32)
    for c in range(2):
        for to in range(8):
            rows = [ordered[g, c, 54 * to : 54 * to + 56, :] for g in range(2)]
            out_ref[to, :, 128 * c : 128 * c + 128] = jnp.concatenate(rows, axis=0).astype(BF16)


def over_xc_body(got_ref, out_ref):
    total = sum(got_ref[i].astype(F32) for i in range(8))
    for g in range(2):
        rows = total[56 * g : 56 * g + 56]
        rows = jnp.concatenate([rows[:, :128], rows[:, 128:]], axis=0).astype(BF16)
        for y in range(4):
            out_ref[4 * g + y] = rows


def last_body(got_ref, out_ref):
    total = sum(got_ref[i].astype(F32) for i in range(8))
    out_ref[...] = jnp.concatenate([total[:54], total[56:110]], axis=1)


def data_grad_body(low_ref, high_ref, mine_ref, weight_any, out_ref, token_ref, weight, sem):
    copy = pltpu.make_async_copy(weight_any, weight, sem)
    copy.start()
    none = jnp.zeros((16, 256), BF16)
    total = jnp.zeros((256, 128), F32)
    for a in range(3):
        wide = (high_ref, mine_ref, low_ref)[a][...].astype(F32)
        if a == 0:
            copy.wait()
        for c in range(3):
            moved = x_shifted(wide, 1 - c).astype(BF16)
            for b in range(3):
                if b == 2:
                    shifted = jnp.concatenate([none, moved[:240]], axis=0)
                elif b == 0:
                    shifted = jnp.concatenate([moved[16:], none], axis=0)
                else:
                    shifted = moved
                tap = 9 * a + 3 * b + c
                total = total + lax.dot_general(
                    shifted,
                    weight[128 * tap : 128 * tap + 128, :],
                    (((1,), (1,)), ((), ())),
                    preferred_element_type=F32,
                )
    out_ref[...] = total.astype(BF16)
    token_ref[...] = jnp.zeros((8, 128), F32)


def neighbours(block):
    count = 64
    up = [(i, i + 1) for i in range(count - 1)]
    down = [(i + 1, i) for i in range(count - 1)]
    return lax.ppermute(block, SPACE, up), lax.ppermute(block, SPACE, down)


def turned(block):
    return lax.ppermute(block, ("y", "zl"), [(4 * y + z, 4 * z + y) for y in range(4) for z in range(4)])


def per_device(
    activations,
    conv_weight,
    conv_bias,
    cotangent,
    basis_panels,
    panel_owner,
    output_basis,
    input_eigen,
    output_eigen,
):
    dma = pltpu.SemaphoreType.DMA
    place = lax.axis_index("zl").astype(jnp.int32).reshape(1)
    inner = lax.axis_index(XC).astype(jnp.int32).reshape(1)
    plane = activations.reshape(256, 128)
    low, high = neighbours(plane)

    stored = call(
        basis_body,
        shape((4, 64, 128), BF16),
        arrays=(basis_panels[0].T,),
        remote=(input_eigen.reshape(1, 54),),
        scratch=[pltpu.VMEM((1, 54), F32), dma],
        flops=4_000_000_000,
    )

    delta, send, twice = call(
        forward_body,
        [shape((256, 256), BF16), shape((8, 384, 128), BF16), shape((2, 4, 64, 128), BF16)],
        (inner,),
        (low, high, turned(stored)),
        (plane, conv_weight, conv_bias.reshape(1, 256), cotangent.reshape(256, 256)),
        scratch=[
            pltpu.VMEM((256, 3456), BF16),
            pltpu.VMEM((256, 128), BF16),
            pltpu.VMEM((3456, 256), BF16),
            pltpu.VMEM((1, 256), F32),
            pltpu.VMEM((256, 256), BF16),
            dma((4,)),
        ],
        flops=2 * 256 * 3456 * 256,
    )
    basis = lax.all_gather(twice, ("zh", "zl"))
    delta_low, delta_high = neighbours(delta)
    got = exchange(send, XC)
    part = call(
        weight_grad_body,
        shape((16, 64, 128), BF16),
        arrays=(got,),
        after=(delta_low, delta_high),
        scratch=[pltpu.VMEM((288, 2560), BF16), pltpu.VMEM((2048, 128), BF16), pltpu.VMEM((864, 128), F32)],
        flops=2 * 864 * 2048 * 128,
    )
    data, token = call(
        data_grad_body,
        [shape((256, 128), BF16), shape((8, 128), F32)],
        arrays=(delta_low, delta_high, delta),
        remote=(conv_weight,),
        after=(part,),
        scratch=[pltpu.VMEM((3456, 256), BF16), dma],
        flops=2 * 256 * 3456 * 256,
    )
    part = call(over_y_zl_body, shape((4, 64, 128), BF16), arrays=(exchange(part, ("y", "zl")),), after=(token,))
    part = call(over_zh_zg_body, shape((32, 64, 128), BF16), arrays=(exchange(part, ("zh", "zg")),))
    grads = exchange(part, YXC)
    rotated, panels = call(
        rotate_body,
        [shape((4, 56, 256), F32), shape((2, 4, 64, 128), BF16)],
        (panel_owner, place),
        (grads,),
        (basis,),
        scratch=[
            pltpu.VMEM((8, 64, 128), BF16),
            pltpu.VMEM((2, 1024, 128), F32),
            pltpu.VMEM((896, 256), F32),
            dma((10,)),
        ],
        limit=LIMIT + 15_000_000,
    )
    part = call(
        update_body,
        shape((8, 112, 256), BF16),
        (),
        (exchange(rotated, "zl"), panels),
        (output_basis, output_eigen.reshape(1, 256)),
        scratch=[
            pltpu.VMEM((256, 256), F32),
            pltpu.VMEM((1, 256), F32),
            pltpu.VMEM((2, 2, 440, 128), F32),
            dma((2,)),
        ],
    )
    part = call(over_xc_body, shape((8, 112, 128), BF16), arrays=(exchange(part, XC),))
    update = call(last_body, shape((54, 256), F32), arrays=(exchange(part, ("zg", "y")),))
    return (data.reshape(1, 1, 16, 16, 128), update)


def solution(mesh):
    fine = Mesh(mesh.devices.reshape(SIZES), AXES)
    both = P(SAMPLE, SPACE, None, None, None)
    return jax.shard_map(
        per_device,
        mesh=fine,
        in_specs=(both, P(), P(), both, P(SAMPLE, None, SPACE), P(), P(), P(SPACE), P()),
        out_specs=(both, P(SPACE, None)),
        check_vma=False,
    )
```

```python
import jax
import jax.numpy as jnp
from jax import lax
from jax.experimental import pallas as pl
from jax.experimental.pallas import tpu as pltpu
from jax.sharding import Mesh
from jax.sharding import PartitionSpec as P

DAMPING = 0.001
CELLS = 131072
BF16 = jnp.bfloat16
F32 = jnp.float32
VMEM = pl.BlockSpec(memory_space=pltpu.VMEM)
SMEM = pl.BlockSpec(memory_space=pltpu.SMEM)
LIMIT = 48 * 1024 * 1024
ANY = pl.BlockSpec(memory_space=pl.ANY)
AXES = ("y", "zh", "zg", "zl", "x", "c")
SIZES = (4, 2, 2, 4, 4, 2)
SAMPLE = ("y", "zh")
XC = ("x", "c")
YXC = ("y", "x", "c")
SPACE = ("zg", "zl", "x", "c")


def call(body, out_shape, scalars=(), arrays=(), remote=(), after=(), scratch=(), flops=0, limit=LIMIT):
    many = isinstance(out_shape, (list, tuple))
    inputs = (*scalars, *arrays, *remote, *after)
    kept = len(inputs) - len(after)

    def kernel(*refs):
        body(*refs[:kept], *refs[len(inputs) :])

    return pl.pallas_call(
        kernel,
        out_shape=out_shape,
        in_specs=[SMEM] * len(scalars) + [VMEM] * len(arrays) + [ANY] * (len(remote) + len(after)),
        out_specs=[VMEM] * len(out_shape) if many else VMEM,
        scratch_shapes=list(scratch),
        compiler_params=pltpu.CompilerParams(vmem_limit_bytes=limit),
        cost_estimate=pl.CostEstimate(
            flops=flops,
            bytes_accessed=sum(a.size * a.dtype.itemsize for a in inputs),
            transcendentals=0,
        ),
    )(*inputs)


def shape(dims, dtype):
    return jax.ShapeDtypeStruct(dims, dtype)


def iota(dims, axis):
    return lax.broadcasted_iota(jnp.int32, dims, axis)


def exchange(x, axes):
    return lax.all_to_all(x, axes, 0, 0)


def started(copies):
    for copy in copies:
        copy.start()
    return copies


def x_shifted(rows, step):
    if step == 0:
        return rows
    x = iota(rows.shape, 0) & 15
    inside = (x + step >= 0) & (x + step < 16)
    return jnp.where(inside, pltpu.roll(rows, (-step) % 256, 0), 0.0)


def basis_body(panel, eigen_any, out_ref, eigen, sem):
    copy = pltpu.make_async_copy(eigen_any, eigen, sem)
    copy.start()
    copy.wait()
    row = iota((54, 54), 0)
    column = jnp.sum(jnp.where(row == iota((54, 54), 1), eigen[...], 0.0), axis=1, keepdims=True)
    column = jnp.concatenate([column, jnp.ones((10, 1), F32)], axis=0)
    first = column.astype(BF16).astype(F32)
    second = (column - first).astype(BF16).astype(F32)
    third = column - first - second
    for r in range(4):
        pick = iota((432, 128), 0) == 4 * iota((432, 128), 1) + r
        block = jnp.dot(panel[...], jnp.where(pick, 1.0, 0.0).astype(BF16), preferred_element_type=F32)
        block = jnp.concatenate([block, jnp.zeros((10, 128), F32)], axis=0)
        if r == 0:
            at = iota((64, 128), 1)
            block = jnp.where(at == 108, first, block)
            block = jnp.where(at == 109, second, block)
            block = jnp.where(at == 110, third, block)
        out_ref[r] = block.astype(BF16)


def forward_body(
    place_ref, low_ref, high_ref, mine_any, weight_any, bias_any, cot_any,
    delta_ref, send_ref, patches, mine, weight, bias, cot, sems,
):
    copies = started(
        [
            pltpu.make_async_copy(source, target, sems.at[i])
            for i, (source, target) in enumerate(
                [(mine_any, mine), (weight_any, weight), (bias_any, bias), (cot_any, cot)]
            )
        ]
    )
    none = jnp.zeros((16, 128), BF16)
    for a in (0, 2, 1):
        if a == 1:
            copies[0].wait()
        wide = (low_ref, mine, high_ref)[a][...].astype(F32)
        for c in range(3):
            moved = x_shifted(wide, c - 1).astype(BF16)
            for b in range(3):
                at = (9 * a + 3 * b + c) * 128
                if b == 0:
                    shifted = jnp.concatenate([none, moved[:240]], axis=0)
                elif b == 2:
                    shifted = jnp.concatenate([moved[16:], none], axis=0)
                else:
                    shifted = moved
                patches[:, at : at + 128] = shifted
    for copy in copies[1:]:
        copy.wait()
    pre = jnp.dot(patches[...], weight[...], preferred_element_type=F32) + bias[...]
    logistic = 1.0 / (1.0 + jnp.exp(-pre))
    delta = (cot[...].astype(F32) * logistic * (1.0 + pre * (1.0 - logistic))).astype(BF16)
    delta_ref[...] = delta
    rim = jnp.where(place_ref[0] < 4, low_ref[...].astype(F32), high_ref[...].astype(F32))
    act_t = mine[...].astype(F32).T.astype(BF16)
    rim_t = rim.T.astype(BF16)
    for x in range(4):
        for c in range(2):
            to = 2 * x + c
            for half in range(2):
                lanes = slice(128 * half, 128 * half + 128)
                rows = slice(32 * x, 32 * x + 32)
                send_ref[to, 32 * half : 32 * half + 32] = act_t[rows, lanes]
                send_ref[to, 64 + 32 * half : 96 + 32 * half] = rim_t[rows, lanes]
            send_ref[to, 128:] = delta[:, 128 * c : 128 * c + 128]


def weight_grad_body(got_ref, out_ref, moved, deltas, whole):
    pieces = []
    for plane, at in [(0, 64)] + [(e, 0) for e in range(8)] + [(7, 64)]:
        pieces.append(got_ref[plane, at : at + 32].astype(F32))
        pieces.append(got_ref[plane, at + 32 : at + 64].astype(F32))
    acts = jnp.concatenate(pieces, axis=1)
    lane = iota((32, 2560), 1)
    x = lane & 15
    y = (lane >> 4) & 15
    for b in range(3):
        for c in range(3):
            step = 16 * (b - 1) + (c - 1)
            turned = pltpu.roll(acts, (-step) % 2560, 1) if step else acts
            inside = (x + c >= 1) & (x + c < 17) & (y + b >= 1) & (y + b < 17)
            moved[32 * (3 * b + c) : 32 * (3 * b + c) + 32, :] = jnp.where(inside, turned, 0.0).astype(BF16)
    for e in range(8):
        deltas[256 * e : 256 * e + 256, :] = got_ref[e, 128:]
    for a in range(3):
        whole[288 * a : 288 * a + 288, :] = jnp.dot(
            moved[:, 256 * a : 256 * a + 2048], deltas[...], preferred_element_type=F32
        )
    none = jnp.zeros((5, 128), F32)
    for y_to in range(4):
        for z_to in range(4):
            parts = []
            for e in range(2):
                parts.append(whole[pl.ds(8 * y_to + 4 * e + z_to, 27, stride=32), :])
                parts.append(none)
            out_ref[4 * y_to + z_to] = jnp.concatenate(parts, axis=0).astype(BF16)


def over_y_zl_body(got_ref, out_ref):
    total = sum(got_ref[i].astype(F32) for i in range(16)) * (1.0 / CELLS)
    for to in range(4):
        out_ref[to] = total.astype(BF16)


def over_zh_zg_body(got_ref, out_ref):
    total = ((got_ref[0].astype(F32) + got_ref[1].astype(F32)) + (got_ref[2].astype(F32) + got_ref[3].astype(F32))).astype(BF16)
    for to in range(32):
        out_ref[to] = total


def slot_of(owner):
    return owner & 1, owner >> 1


def rotate_body(owner_ref, place_ref, got_ref, basis_any, out_ref, panels_ref, basis, grads, ordered, sems):
    zg, zl = place_ref[0], place_ref[1]
    copies = []
    for j in range(8):
        zh, z = slot_of(owner_ref[j])
        copies.append(pltpu.make_async_copy(basis_any.at[zh, zg, z, zl], basis.at[j], sems.at[j]))
    for g in range(2):
        zh, z = slot_of(owner_ref[zl + 4 * g])
        copies.append(pltpu.make_async_copy(basis_any.at[zh, zg, z], panels_ref.at[g], sems.at[8 + g]))
    started(copies)
    for y in range(4):
        for x in range(4):
            at = 32 * (8 * x + 2 * y)
            for c in range(2):
                grads[c, at : at + 64, :] = got_ref[8 * y + 2 * x + c].astype(F32)
    for tap in range(27):
        for c in range(2):
            ordered[32 * tap : 32 * tap + 32, 128 * c : 128 * c + 128] = grads[c, pl.ds(tap, 32, stride=32), :]
    ordered[864:, :] = jnp.zeros((32, 256), F32)
    inside = iota((64, 128), 1) < 108
    total = jnp.zeros((64, 256), F32)
    for j in range(8):
        copies[j].wait()
        block = jnp.where(inside, basis[j].astype(F32), 0.0).astype(BF16)
        rows = ordered[108 * j : 108 * j + 128, :].astype(BF16)
        total = total + jnp.dot(block, rows, preferred_element_type=F32)
    for to in range(4):
        out_ref[to] = total[:56]
    for copy in copies[8:]:
        copy.wait()


def update_body(
    got_ref, basis, out_basis_any, out_eigen_any, out_ref, out_basis, out_eigen, ordered, sems
):
    copies = [
        pltpu.make_async_copy(out_basis_any, out_basis, sems.at[0]),
        pltpu.make_async_copy(out_eigen_any, out_eigen, sems.at[1]),
    ]
    started(copies)
    highest = lax.Precision.HIGHEST
    rotated = (got_ref[0] + got_ref[1]) + (got_ref[2] + got_ref[3])
    rotated = jnp.concatenate([rotated, jnp.zeros((8, 256), F32)], axis=0)
    for copy in copies:
        copy.wait()
    rotated = jnp.dot(rotated, out_basis[...], precision=highest, preferred_element_type=F32)
    terms = basis[0, 0].astype(F32)
    eigen = (terms[:, 108:109] + terms[:, 109:110]) + terms[:, 110:111]
    scaled = rotated / (eigen * out_eigen[...] + DAMPING)
    scaled = jnp.where(iota((64, 256), 0) < 54, scaled, 0.0)
    turned = lax.dot_general(
        scaled, out_basis[...], (((1,), (1,)), ((), ())), precision=highest, preferred_element_type=F32
    )
    high = turned.astype(BF16)
    rest = (turned - high.astype(F32)).astype(BF16)
    for g in range(2):
        for r in range(4):
            block = basis[g, r].astype(F32).T.astype(BF16)
            rows = jnp.dot(block, high, preferred_element_type=F32) + jnp.dot(block, rest, preferred_element_type=F32)
            for c in range(2):
                ordered[g, c, pl.ds(r, 108, stride=4), :] = rows[:108, 128 * c : 128 * c + 128]
        for c in range(2):
            ordered[g, c, 432:, :] = jnp.zeros((8, 128), F32)
    for c in range(2):
        for to in range(8):
            rows = [ordered[g, c, 54 * to : 54 * to + 56, :] for g in range(2)]
            out_ref[to, :, 128 * c : 128 * c + 128] = jnp.concatenate(rows, axis=0).astype(BF16)


def over_xc_body(got_ref, out_ref):
    total = sum(got_ref[i].astype(F32) for i in range(8))
    for g in range(2):
        rows = total[56 * g : 56 * g + 56]
        rows = jnp.concatenate([rows[:, :128], rows[:, 128:]], axis=0).astype(BF16)
        for y in range(4):
            out_ref[4 * g + y] = rows


def last_body(got_ref, out_ref):
    total = sum(got_ref[i].astype(F32) for i in range(8))
    out_ref[...] = jnp.concatenate([total[:54], total[56:110]], axis=1)


def data_grad_body(low_ref, high_ref, mine_ref, weight_any, out_ref, token_ref, weight, sem):
    copy = pltpu.make_async_copy(weight_any, weight, sem)
    copy.start()
    none = jnp.zeros((16, 256), BF16)
    total = jnp.zeros((256, 128), F32)
    for a in range(3):
        wide = (high_ref, mine_ref, low_ref)[a][...].astype(F32)
        if a == 0:
            copy.wait()
        for c in range(3):
            moved = x_shifted(wide, 1 - c).astype(BF16)
            for b in range(3):
                if b == 2:
                    shifted = jnp.concatenate([none, moved[:240]], axis=0)
                elif b == 0:
                    shifted = jnp.concatenate([moved[16:], none], axis=0)
                else:
                    shifted = moved
                tap = 9 * a + 3 * b + c
                total = total + lax.dot_general(
                    shifted,
                    weight[128 * tap : 128 * tap + 128, :],
                    (((1,), (1,)), ((), ())),
                    preferred_element_type=F32,
                )
    out_ref[...] = total.astype(BF16)
    token_ref[...] = jnp.zeros((8, 128), F32)


def neighbours(block):
    count = 64
    up = [(i, i + 1) for i in range(count - 1)]
    down = [(i + 1, i) for i in range(count - 1)]
    return lax.ppermute(block, SPACE, up), lax.ppermute(block, SPACE, down)


def turned(block):
    return lax.ppermute(block, ("y", "zl"), [(4 * y + z, 4 * z + y) for y in range(4) for z in range(4)])


def per_device(
    activations,
    conv_weight,
    conv_bias,
    cotangent,
    basis_panels,
    panel_owner,
    output_basis,
    input_eigen,
    output_eigen,
):
    dma = pltpu.SemaphoreType.DMA
    place = jnp.stack([lax.axis_index("zg"), lax.axis_index("zl")]).astype(jnp.int32)
    inner = lax.axis_index(XC).astype(jnp.int32).reshape(1)
    plane = activations.reshape(256, 128)
    low, high = neighbours(plane)

    stored = call(
        basis_body,
        shape((4, 64, 128), BF16),
        arrays=(basis_panels[0].T,),
        remote=(input_eigen.reshape(1, 54),),
        scratch=[pltpu.VMEM((1, 54), F32), dma],
        flops=4_000_000_000,
    )

    stored = turned(stored)
    basis = lax.all_gather(stored, ("zh", "zg", "zl")).reshape(2, 2, 4, 4, 64, 128)
    delta, send = call(
        forward_body,
        [shape((256, 256), BF16), shape((8, 384, 128), BF16)],
        (inner,),
        (low, high),
        (plane, conv_weight, conv_bias.reshape(1, 256), cotangent.reshape(256, 256)),
        (stored,),
        scratch=[
            pltpu.VMEM((256, 3456), BF16),
            pltpu.VMEM((256, 128), BF16),
            pltpu.VMEM((3456, 256), BF16),
            pltpu.VMEM((1, 256), F32),
            pltpu.VMEM((256, 256), BF16),
            dma((4,)),
        ],
        flops=2 * 256 * 3456 * 256,
    )
    delta_low, delta_high = neighbours(delta)
    got = exchange(send, XC)
    part = call(
        weight_grad_body,
        shape((16, 64, 128), BF16),
        arrays=(got,),
        after=(delta_low, delta_high),
        scratch=[pltpu.VMEM((288, 2560), BF16), pltpu.VMEM((2048, 128), BF16), pltpu.VMEM((864, 128), F32)],
        flops=2 * 864 * 2048 * 128,
    )
    data, token = call(
        data_grad_body,
        [shape((256, 128), BF16), shape((8, 128), F32)],
        arrays=(delta_low, delta_high, delta),
        remote=(conv_weight,),
        after=(part,),
        scratch=[pltpu.VMEM((3456, 256), BF16), dma],
        flops=2 * 256 * 3456 * 256,
    )
    part = call(over_y_zl_body, shape((4, 64, 128), BF16), arrays=(exchange(part, ("y", "zl")),), after=(token,))
    part = call(over_zh_zg_body, shape((32, 64, 128), BF16), arrays=(exchange(part, ("zh", "zg")),))
    grads = exchange(part, YXC)
    rotated, panels = call(
        rotate_body,
        [shape((4, 56, 256), F32), shape((2, 4, 64, 128), BF16)],
        (panel_owner, place),
        (grads,),
        (basis,),
        scratch=[
            pltpu.VMEM((8, 64, 128), BF16),
            pltpu.VMEM((2, 1024, 128), F32),
            pltpu.VMEM((896, 256), F32),
            dma((10,)),
        ],
        limit=LIMIT + 15_000_000,
    )
    part = call(
        update_body,
        shape((8, 112, 256), BF16),
        (),
        (exchange(rotated, "zl"), panels),
        (output_basis, output_eigen.reshape(1, 256)),
        scratch=[
            pltpu.VMEM((256, 256), F32),
            pltpu.VMEM((1, 256), F32),
            pltpu.VMEM((2, 2, 440, 128), F32),
            dma((2,)),
        ],
    )
    part = call(over_xc_body, shape((8, 112, 128), BF16), arrays=(exchange(part, XC),))
    update = call(last_body, shape((54, 256), F32), arrays=(exchange(part, ("zg", "y")),))
    return (data.reshape(1, 1, 16, 16, 128), update)


def solution(mesh):
    fine = Mesh(mesh.devices.reshape(SIZES), AXES)
    both = P(SAMPLE, SPACE, None, None, None)
    return jax.shard_map(
        per_device,
        mesh=fine,
        in_specs=(both, P(), P(), both, P(SAMPLE, None, SPACE), P(), P(), P(SPACE), P()),
        out_specs=(both, P(SPACE, None)),
        check_vma=False,
    )
```

```python
import jax
import jax.numpy as jnp
from jax import lax
from jax.experimental import pallas as pl
from jax.experimental.pallas import tpu as pltpu
from jax.sharding import Mesh
from jax.sharding import PartitionSpec as P

DAMPING = 0.001
CELLS = 131072
BF16 = jnp.bfloat16
F32 = jnp.float32
VMEM = pl.BlockSpec(memory_space=pltpu.VMEM)
SMEM = pl.BlockSpec(memory_space=pltpu.SMEM)
LIMIT = 48 * 1024 * 1024
ANY = pl.BlockSpec(memory_space=pl.ANY)
AXES = ("y", "zh", "zg", "zl", "x", "c")
SIZES = (4, 2, 2, 4, 4, 2)
SAMPLE = ("y", "zh")
XC = ("x", "c")
YXC = ("y", "x", "c")
SPACE = ("zg", "zl", "x", "c")


def call(body, out_shape, scalars=(), arrays=(), remote=(), after=(), scratch=(), flops=0, limit=LIMIT):
    many = isinstance(out_shape, (list, tuple))
    inputs = (*scalars, *arrays, *remote, *after)
    kept = len(inputs) - len(after)

    def kernel(*refs):
        body(*refs[:kept], *refs[len(inputs) :])

    return pl.pallas_call(
        kernel,
        out_shape=out_shape,
        in_specs=[SMEM] * len(scalars) + [VMEM] * len(arrays) + [ANY] * (len(remote) + len(after)),
        out_specs=[VMEM] * len(out_shape) if many else VMEM,
        scratch_shapes=list(scratch),
        compiler_params=pltpu.CompilerParams(vmem_limit_bytes=limit),
        cost_estimate=pl.CostEstimate(
            flops=flops,
            bytes_accessed=sum(a.size * a.dtype.itemsize for a in inputs),
            transcendentals=0,
        ),
    )(*inputs)


def shape(dims, dtype):
    return jax.ShapeDtypeStruct(dims, dtype)


def iota(dims, axis):
    return lax.broadcasted_iota(jnp.int32, dims, axis)


def exchange(x, axes):
    return lax.all_to_all(x, axes, 0, 0)


def started(copies):
    for copy in copies:
        copy.start()
    return copies


def x_shifted(rows, step):
    if step == 0:
        return rows
    x = iota(rows.shape, 0) & 15
    inside = (x + step >= 0) & (x + step < 16)
    return jnp.where(inside, pltpu.roll(rows, (-step) % 256, 0), 0.0)


def basis_body(panel, eigen_any, out_ref, eigen, sem):
    copy = pltpu.make_async_copy(eigen_any, eigen, sem)
    copy.start()
    copy.wait()
    row = iota((54, 54), 0)
    column = jnp.sum(jnp.where(row == iota((54, 54), 1), eigen[...], 0.0), axis=1, keepdims=True)
    column = jnp.concatenate([column, jnp.ones((10, 1), F32)], axis=0)
    first = column.astype(BF16).astype(F32)
    second = (column - first).astype(BF16).astype(F32)
    third = column - first - second
    for r in range(4):
        pick = iota((432, 128), 0) == 4 * iota((432, 128), 1) + r
        block = jnp.dot(panel[...], jnp.where(pick, 1.0, 0.0).astype(BF16), preferred_element_type=F32)
        block = jnp.concatenate([block, jnp.zeros((10, 128), F32)], axis=0)
        at = iota((64, 128), 1)
        block = jnp.where(at == 108, first, block)
        block = jnp.where(at == 109, second, block)
        block = jnp.where(at == 110, third, block)
        out_ref[r] = block.astype(BF16)


def forward_body(
    place_ref, low_ref, high_ref, mine_any, weight_any, bias_any, cot_any,
    delta_ref, send_ref, patches, mine, weight, bias, cot, sems,
):
    copies = started(
        [
            pltpu.make_async_copy(source, target, sems.at[i])
            for i, (source, target) in enumerate(
                [(mine_any, mine), (weight_any, weight), (bias_any, bias), (cot_any, cot)]
            )
        ]
    )
    none = jnp.zeros((16, 128), BF16)
    for a in (0, 2, 1):
        if a == 1:
            copies[0].wait()
        wide = (low_ref, mine, high_ref)[a][...].astype(F32)
        for c in range(3):
            moved = x_shifted(wide, c - 1).astype(BF16)
            for b in range(3):
                at = (9 * a + 3 * b + c) * 128
                if b == 0:
                    shifted = jnp.concatenate([none, moved[:240]], axis=0)
                elif b == 2:
                    shifted = jnp.concatenate([moved[16:], none], axis=0)
                else:
                    shifted = moved
                patches[:, at : at + 128] = shifted
    for copy in copies[1:]:
        copy.wait()
    pre = jnp.dot(patches[...], weight[...], preferred_element_type=F32) + bias[...]
    logistic = 1.0 / (1.0 + jnp.exp(-pre))
    delta = (cot[...].astype(F32) * logistic * (1.0 + pre * (1.0 - logistic))).astype(BF16)
    delta_ref[...] = delta
    rim = jnp.where(place_ref[0] < 4, low_ref[...].astype(F32), high_ref[...].astype(F32))
    act_t = mine[...].astype(F32).T.astype(BF16)
    rim_t = rim.T.astype(BF16)
    for x in range(4):
        for c in range(2):
            to = 2 * x + c
            for half in range(2):
                lanes = slice(128 * half, 128 * half + 128)
                rows = slice(32 * x, 32 * x + 32)
                send_ref[to, 32 * half : 32 * half + 32] = act_t[rows, lanes]
                send_ref[to, 64 + 32 * half : 96 + 32 * half] = rim_t[rows, lanes]
            send_ref[to, 128:] = delta[:, 128 * c : 128 * c + 128]


def weight_grad_body(got_ref, basis_ref, out_ref, moved, deltas, whole):
    pieces = []
    for plane, at in [(0, 64)] + [(e, 0) for e in range(8)] + [(7, 64)]:
        pieces.append(got_ref[plane, at : at + 32].astype(F32))
        pieces.append(got_ref[plane, at + 32 : at + 64].astype(F32))
    acts = jnp.concatenate(pieces, axis=1)
    lane = iota((32, 2560), 1)
    x = lane & 15
    y = (lane >> 4) & 15
    for b in range(3):
        for c in range(3):
            step = 16 * (b - 1) + (c - 1)
            turned = pltpu.roll(acts, (-step) % 2560, 1) if step else acts
            inside = (x + c >= 1) & (x + c < 17) & (y + b >= 1) & (y + b < 17)
            moved[32 * (3 * b + c) : 32 * (3 * b + c) + 32, :] = jnp.where(inside, turned, 0.0).astype(BF16)
    for e in range(8):
        deltas[256 * e : 256 * e + 256, :] = got_ref[e, 128:]
    for a in range(3):
        whole[288 * a : 288 * a + 288, :] = jnp.dot(
            moved[:, 256 * a : 256 * a + 2048], deltas[...], preferred_element_type=F32
        )
    none = jnp.zeros((5, 128), F32)
    for y_to in range(4):
        for z_to in range(4):
            parts = []
            for e in range(2):
                parts.append(whole[pl.ds(8 * y_to + 4 * e + z_to, 27, stride=32), :])
                parts.append(none)
            out_ref[4 * y_to + z_to, :64] = jnp.concatenate(parts, axis=0).astype(BF16)
            out_ref[4 * y_to + z_to, 64:] = basis_ref[z_to]


def over_y_zl_body(place_ref, got_ref, out_ref, basis_ref):
    total = sum(got_ref[i, :64].astype(F32) for i in range(16)) * (1.0 / CELLS)
    for to in range(4):
        out_ref[to] = total.astype(BF16)
    for y in range(4):
        basis_ref[y] = got_ref[4 * y + place_ref[0], 64:]


def over_zh_zg_body(got_ref, out_ref):
    total = ((got_ref[0].astype(F32) + got_ref[1].astype(F32)) + (got_ref[2].astype(F32) + got_ref[3].astype(F32))).astype(BF16)
    for to in range(32):
        out_ref[to] = total


def rotate_body(owner_ref, place_ref, got_ref, own_ref, other_ref, out_ref, basis, grads, ordered):
    basis[0] = own_ref[...]
    basis[1] = other_ref[...]
    slots = [(place_ref[1] ^ (owner_ref[j] & 1), owner_ref[j] >> 1) for j in range(8)]
    for y in range(4):
        for x in range(4):
            at = 32 * (8 * x + 2 * y)
            for c in range(2):
                grads[c, at : at + 64, :] = got_ref[8 * y + 2 * x + c].astype(F32)
    for tap in range(27):
        for c in range(2):
            ordered[32 * tap : 32 * tap + 32, 128 * c : 128 * c + 128] = grads[c, pl.ds(tap, 32, stride=32), :]
    ordered[864:, :] = jnp.zeros((32, 256), F32)
    inside = iota((64, 128), 1) < 108
    total = jnp.zeros((64, 256), F32)
    for j in range(8):
        block = jnp.where(inside, basis[slots[j]].astype(F32), 0.0).astype(BF16)
        rows = ordered[108 * j : 108 * j + 128, :].astype(BF16)
        total = total + jnp.dot(block, rows, preferred_element_type=F32)
    total = jnp.concatenate([total[:56, :128], total[:56, 128:]], axis=0)
    high = total.astype(BF16)
    rest = (total - high.astype(F32)).astype(BF16)
    for to in range(4):
        out_ref[to, :112] = high
        out_ref[to, 112:224] = rest
        for g in range(2):
            out_ref[to, 224 + 64 * g : 288 + 64 * g] = basis[slots[to + 4 * g]]


def update_body(got_ref, out_basis_any, out_eigen_any, out_ref, out_basis, out_eigen, ordered, sems):
    copies = [
        pltpu.make_async_copy(out_basis_any, out_basis, sems.at[0]),
        pltpu.make_async_copy(out_eigen_any, out_eigen, sems.at[1]),
    ]
    started(copies)
    highest = lax.Precision.HIGHEST
    total = sum(got_ref[i, :112].astype(F32) + got_ref[i, 112:224].astype(F32) for i in range(4))
    rotated = jnp.concatenate([total[:56], total[56:]], axis=1)
    rotated = jnp.concatenate([rotated, jnp.zeros((8, 256), F32)], axis=0)
    for copy in copies:
        copy.wait()
    rotated = jnp.dot(rotated, out_basis[...], precision=highest, preferred_element_type=F32)
    terms = got_ref[0, 224:288].astype(F32)
    eigen = (terms[:, 108:109] + terms[:, 109:110]) + terms[:, 110:111]
    scaled = rotated / (eigen * out_eigen[...] + DAMPING)
    scaled = jnp.where(iota((64, 256), 0) < 54, scaled, 0.0)
    turned = lax.dot_general(
        scaled, out_basis[...], (((1,), (1,)), ((), ())), precision=highest, preferred_element_type=F32
    )
    high = turned.astype(BF16)
    rest = (turned - high.astype(F32)).astype(BF16)
    for g in range(2):
        for r in range(4):
            block = got_ref[r, 224 + 64 * g : 288 + 64 * g].astype(F32).T.astype(BF16)
            rows = jnp.dot(block, high, preferred_element_type=F32) + jnp.dot(block, rest, preferred_element_type=F32)
            for c in range(2):
                ordered[g, c, pl.ds(r, 108, stride=4), :] = rows[:108, 128 * c : 128 * c + 128]
        for c in range(2):
            ordered[g, c, 432:, :] = jnp.zeros((8, 128), F32)
    for c in range(2):
        for to in range(8):
            rows = [ordered[g, c, 54 * to : 54 * to + 56, :] for g in range(2)]
            out_ref[to, :, 128 * c : 128 * c + 128] = jnp.concatenate(rows, axis=0).astype(BF16)


def over_xc_body(got_ref, out_ref):
    total = sum(got_ref[i].astype(F32) for i in range(8))
    for g in range(2):
        rows = total[56 * g : 56 * g + 56]
        rows = jnp.concatenate([rows[:, :128], rows[:, 128:]], axis=0).astype(BF16)
        for y in range(4):
            out_ref[4 * g + y] = rows


def last_body(got_ref, out_ref):
    total = sum(got_ref[i].astype(F32) for i in range(8))
    out_ref[...] = jnp.concatenate([total[:54], total[56:110]], axis=1)


def data_grad_body(low_ref, high_ref, mine_ref, weight_any, out_ref, token_ref, weight, sem):
    copy = pltpu.make_async_copy(weight_any, weight, sem)
    copy.start()
    none = jnp.zeros((16, 256), BF16)
    total = jnp.zeros((256, 128), F32)
    for a in range(3):
        wide = (high_ref, mine_ref, low_ref)[a][...].astype(F32)
        if a == 0:
            copy.wait()
        for c in range(3):
            moved = x_shifted(wide, 1 - c).astype(BF16)
            for b in range(3):
                if b == 2:
                    shifted = jnp.concatenate([none, moved[:240]], axis=0)
                elif b == 0:
                    shifted = jnp.concatenate([moved[16:], none], axis=0)
                else:
                    shifted = moved
                tap = 9 * a + 3 * b + c
                total = total + lax.dot_general(
                    shifted,
                    weight[128 * tap : 128 * tap + 128, :],
                    (((1,), (1,)), ((), ())),
                    preferred_element_type=F32,
                )
    out_ref[...] = total.astype(BF16)
    token_ref[...] = jnp.zeros((8, 128), F32)


def neighbours(block):
    count = 64
    up = [(i, i + 1) for i in range(count - 1)]
    down = [(i + 1, i) for i in range(count - 1)]
    return lax.ppermute(block, SPACE, up), lax.ppermute(block, SPACE, down)


def per_device(
    activations,
    conv_weight,
    conv_bias,
    cotangent,
    basis_panels,
    panel_owner,
    output_basis,
    input_eigen,
    output_eigen,
):
    dma = pltpu.SemaphoreType.DMA
    place = jnp.stack([lax.axis_index("y"), lax.axis_index("zh")]).astype(jnp.int32)
    inner = lax.axis_index(XC).astype(jnp.int32).reshape(1)
    plane = activations.reshape(256, 128)
    low, high = neighbours(plane)

    delta, send = call(
        forward_body,
        [shape((256, 256), BF16), shape((8, 384, 128), BF16)],
        (inner,),
        (low, high),
        (plane, conv_weight, conv_bias.reshape(1, 256), cotangent.reshape(256, 256)),
        scratch=[
            pltpu.VMEM((256, 3456), BF16),
            pltpu.VMEM((256, 128), BF16),
            pltpu.VMEM((3456, 256), BF16),
            pltpu.VMEM((1, 256), F32),
            pltpu.VMEM((256, 256), BF16),
            dma((4,)),
        ],
        flops=2 * 256 * 3456 * 256,
    )
    delta_low, delta_high = neighbours(delta)
    got = exchange(send, XC)
    stored = call(
        basis_body,
        shape((4, 64, 128), BF16),
        arrays=(basis_panels[0].T,),
        remote=(input_eigen.reshape(1, 54),),
        after=(delta,),
        scratch=[pltpu.VMEM((1, 54), F32), dma],
    )
    part = call(
        weight_grad_body,
        shape((16, 128, 128), BF16),
        arrays=(got, stored),
        after=(delta_low, delta_high),
        scratch=[pltpu.VMEM((288, 2560), BF16), pltpu.VMEM((2048, 128), BF16), pltpu.VMEM((864, 128), F32)],
        flops=2 * 864 * 2048 * 128,
    )
    data, token = call(
        data_grad_body,
        [shape((256, 128), BF16), shape((8, 128), F32)],
        arrays=(delta_low, delta_high, delta),
        remote=(conv_weight,),
        after=(part,),
        scratch=[pltpu.VMEM((3456, 256), BF16), dma],
        flops=2 * 256 * 3456 * 256,
    )
    part, own = call(
        over_y_zl_body,
        [shape((4, 64, 128), BF16), shape((4, 64, 128), BF16)],
        (place,),
        (exchange(part, ("y", "zl")),),
        after=(token,),
    )
    other = lax.ppermute(own, "zh", [(0, 1), (1, 0)])
    part = call(over_zh_zg_body, shape((32, 64, 128), BF16), arrays=(exchange(part, ("zh", "zg")),))
    grads = exchange(part, YXC)
    rotated = call(
        rotate_body,
        shape((4, 352, 128), BF16),
        (panel_owner, place),
        (grads, own, other),
        scratch=[
            pltpu.VMEM((2, 4, 64, 128), BF16),
            pltpu.VMEM((2, 1024, 128), F32),
            pltpu.VMEM((896, 256), F32),
        ],
    )
    part = call(
        update_body,
        shape((8, 112, 256), BF16),
        arrays=(exchange(rotated, "zl"),),
        remote=(output_basis, output_eigen.reshape(1, 256)),
        scratch=[
            pltpu.VMEM((256, 256), F32),
            pltpu.VMEM((1, 256), F32),
            pltpu.VMEM((2, 2, 440, 128), F32),
            dma((2,)),
        ],
    )
    part = call(over_xc_body, shape((8, 112, 128), BF16), arrays=(exchange(part, XC),))
    update = call(last_body, shape((54, 256), F32), arrays=(exchange(part, ("zg", "y")),))
    return (data.reshape(1, 1, 16, 16, 128), update)


def solution(mesh):
    fine = Mesh(mesh.devices.reshape(SIZES), AXES)
    both = P(SAMPLE, SPACE, None, None, None)
    return jax.shard_map(
        per_device,
        mesh=fine,
        in_specs=(both, P(), P(), both, P(SAMPLE, None, SPACE), P(), P(), P(SPACE), P()),
        out_specs=(both, P(SPACE, None)),
        check_vma=False,
    )
```

```python
import jax
import jax.numpy as jnp
from jax import lax
from jax.experimental import pallas as pl
from jax.experimental.pallas import tpu as pltpu
from jax.sharding import Mesh
from jax.sharding import PartitionSpec as P

DAMPING = 0.001
CELLS = 131072
BF16 = jnp.bfloat16
F32 = jnp.float32
VMEM = pl.BlockSpec(memory_space=pltpu.VMEM)
SMEM = pl.BlockSpec(memory_space=pltpu.SMEM)
LIMIT = 48 * 1024 * 1024
ANY = pl.BlockSpec(memory_space=pl.ANY)
AXES = ("y", "zh", "zg", "zl", "x", "c")
SIZES = (4, 2, 2, 4, 4, 2)
SAMPLE = ("y", "zh")
XC = ("x", "c")
YXC = ("y", "x", "c")
SPACE = ("zg", "zl", "x", "c")


def call(body, out_shape, scalars=(), arrays=(), remote=(), after=(), scratch=(), flops=0, limit=LIMIT):
    many = isinstance(out_shape, (list, tuple))
    inputs = (*scalars, *arrays, *remote, *after)
    kept = len(inputs) - len(after)

    def kernel(*refs):
        body(*refs[:kept], *refs[len(inputs) :])

    return pl.pallas_call(
        kernel,
        out_shape=out_shape,
        in_specs=[SMEM] * len(scalars) + [VMEM] * len(arrays) + [ANY] * (len(remote) + len(after)),
        out_specs=[VMEM] * len(out_shape) if many else VMEM,
        scratch_shapes=list(scratch),
        compiler_params=pltpu.CompilerParams(vmem_limit_bytes=limit),
        cost_estimate=pl.CostEstimate(
            flops=flops,
            bytes_accessed=sum(a.size * a.dtype.itemsize for a in inputs),
            transcendentals=0,
        ),
    )(*inputs)


def shape(dims, dtype):
    return jax.ShapeDtypeStruct(dims, dtype)


def iota(dims, axis):
    return lax.broadcasted_iota(jnp.int32, dims, axis)


def exchange(x, axes):
    return lax.all_to_all(x, axes, 0, 0)


def started(copies):
    for copy in copies:
        copy.start()
    return copies


def x_shifted(rows, step):
    if step == 0:
        return rows
    x = iota(rows.shape, 0) & 15
    inside = (x + step >= 0) & (x + step < 16)
    return jnp.where(inside, pltpu.roll(rows, (-step) % 256, 0), 0.0)


def basis_body(panel, eigen_any, out_ref, eigen, sem):
    copy = pltpu.make_async_copy(eigen_any, eigen, sem)
    copy.start()
    copy.wait()
    row = iota((54, 54), 0)
    column = jnp.sum(jnp.where(row == iota((54, 54), 1), eigen[...], 0.0), axis=1, keepdims=True)
    column = jnp.concatenate([column, jnp.ones((10, 1), F32)], axis=0)
    first = column.astype(BF16).astype(F32)
    second = (column - first).astype(BF16).astype(F32)
    third = column - first - second
    for r in range(4):
        pick = iota((432, 128), 0) == 4 * iota((432, 128), 1) + r
        block = jnp.dot(panel[...], jnp.where(pick, 1.0, 0.0).astype(BF16), preferred_element_type=F32)
        block = jnp.concatenate([block, jnp.zeros((10, 128), F32)], axis=0)
        at = iota((64, 128), 1)
        block = jnp.where(at == 108, first, block)
        block = jnp.where(at == 109, second, block)
        block = jnp.where(at == 110, third, block)
        out_ref[r] = block.astype(BF16)


def forward_body(
    place_ref, low_ref, high_ref, mine, weight, bias, cot, basis_ref, delta_ref, send_ref, slices_ref, patches
):
    for y in range(4):
        for r in range(4):
            slices_ref[4 * y + r] = basis_ref[r]
    none = jnp.zeros((16, 128), BF16)
    for a in range(3):
        wide = (low_ref, mine, high_ref)[a][...].astype(F32)
        for c in range(3):
            moved = x_shifted(wide, c - 1).astype(BF16)
            for b in range(3):
                at = (9 * a + 3 * b + c) * 128
                if b == 0:
                    shifted = jnp.concatenate([none, moved[:240]], axis=0)
                elif b == 2:
                    shifted = jnp.concatenate([moved[16:], none], axis=0)
                else:
                    shifted = moved
                patches[:, at : at + 128] = shifted
    pre = jnp.dot(patches[...], weight[...], preferred_element_type=F32) + bias[...]
    logistic = 1.0 / (1.0 + jnp.exp(-pre))
    delta = (cot[...].astype(F32) * logistic * (1.0 + pre * (1.0 - logistic))).astype(BF16)
    delta_ref[...] = delta
    rim = jnp.where(place_ref[0] < 4, low_ref[...].astype(F32), high_ref[...].astype(F32))
    act_t = mine[...].astype(F32).T.astype(BF16)
    rim_t = rim.T.astype(BF16)
    for x in range(4):
        for c in range(2):
            to = 2 * x + c
            for half in range(2):
                lanes = slice(128 * half, 128 * half + 128)
                rows = slice(32 * x, 32 * x + 32)
                send_ref[to, 32 * half : 32 * half + 32] = act_t[rows, lanes]
                send_ref[to, 64 + 32 * half : 96 + 32 * half] = rim_t[rows, lanes]
            send_ref[to, 128:] = delta[:, 128 * c : 128 * c + 128]


def weight_grad_body(got_ref, out_ref, moved, deltas, whole):
    pieces = []
    for plane, at in [(0, 64)] + [(e, 0) for e in range(8)] + [(7, 64)]:
        pieces.append(got_ref[plane, at : at + 32].astype(F32))
        pieces.append(got_ref[plane, at + 32 : at + 64].astype(F32))
    acts = jnp.concatenate(pieces, axis=1)
    lane = iota((32, 2560), 1)
    x = lane & 15
    y = (lane >> 4) & 15
    for b in range(3):
        for c in range(3):
            step = 16 * (b - 1) + (c - 1)
            turned = pltpu.roll(acts, (-step) % 2560, 1) if step else acts
            inside = (x + c >= 1) & (x + c < 17) & (y + b >= 1) & (y + b < 17)
            moved[32 * (3 * b + c) : 32 * (3 * b + c) + 32, :] = jnp.where(inside, turned, 0.0).astype(BF16)
    for e in range(8):
        deltas[256 * e : 256 * e + 256, :] = got_ref[e, 128:]
    for a in range(3):
        whole[288 * a : 288 * a + 288, :] = jnp.dot(
            moved[:, 256 * a : 256 * a + 2048], deltas[...], preferred_element_type=F32
        )
    none = jnp.zeros((5, 128), F32)
    for y_to in range(4):
        for z_to in range(4):
            parts = []
            for e in range(2):
                parts.append(whole[pl.ds(8 * y_to + 4 * e + z_to, 27, stride=32), :])
                parts.append(none)
            out_ref[4 * y_to + z_to] = jnp.concatenate(parts, axis=0).astype(BF16)


def over_y_zl_body(place_ref, got_ref, basis_ref, out_ref):
    total = (sum(got_ref[i].astype(F32) for i in range(16)) * (1.0 / CELLS)).astype(BF16)
    for to in range(4):
        out_ref[to, :64] = total
    for y in range(4):
        block = basis_ref[4 * y + place_ref[0]]
        for to in range(4):
            out_ref[to, 64 + 64 * y : 128 + 64 * y] = block


def over_zh_zg_body(got_ref, out_ref, basis_ref):
    total = sum(got_ref[i, :64].astype(F32) for i in range(4)).astype(BF16)
    for to in range(32):
        out_ref[to] = total
    for zh in range(2):
        for y in range(4):
            for zg in range(2):
                block = got_ref[2 * zh + zg, 64 + 64 * y : 128 + 64 * y]
                basis_ref[2 * y + zh, 64 * zg : 64 * zg + 64] = block


def rotate_body(owner_ref, place_ref, got_ref, basis_ref, out_ref, grads, ordered):
    for y in range(4):
        for x in range(4):
            at = 32 * (8 * x + 2 * y)
            for c in range(2):
                grads[c, at : at + 64, :] = got_ref[8 * y + 2 * x + c].astype(F32)
    for tap in range(27):
        for c in range(2):
            ordered[32 * tap : 32 * tap + 32, 128 * c : 128 * c + 128] = grads[c, pl.ds(tap, 32, stride=32), :]
    ordered[864:, :] = jnp.zeros((32, 256), F32)
    inside = iota((128, 128), 1) < 108
    total = jnp.zeros((128, 256), F32)
    for j in range(8):
        block = jnp.where(inside, basis_ref[owner_ref[j]].astype(F32), 0.0).astype(BF16)
        rows = ordered[108 * j : 108 * j + 128, :].astype(BF16)
        total = total + jnp.dot(block, rows, preferred_element_type=F32)
    total = jnp.concatenate(
        [total[64 * zg : 64 * zg + 56, 128 * c : 128 * c + 128] for zg in range(2) for c in range(2)], axis=0
    ).astype(BF16)
    for to in range(4):
        out_ref[to, :224] = total
        out_ref[to, 224:] = basis_ref[owner_ref[4 * place_ref[1] + to]]


def update_body(got_ref, out_basis_any, out_eigen_any, out_ref, out_basis, out_eigen, ordered, sems):
    copies = [
        pltpu.make_async_copy(out_basis_any, out_basis, sems.at[0]),
        pltpu.make_async_copy(out_eigen_any, out_eigen, sems.at[1]),
    ]
    started(copies)
    highest = lax.Precision.HIGHEST
    total = sum(got_ref[i, :224].astype(F32) for i in range(4))
    none = jnp.zeros((8, 256), F32)
    parts = []
    for zg in range(2):
        at = 112 * zg
        parts.append(jnp.concatenate([total[at : at + 56], total[at + 56 : at + 112]], axis=1))
        parts.append(none)
    rotated = jnp.concatenate(parts, axis=0)
    for copy in copies:
        copy.wait()
    rotated = jnp.dot(rotated, out_basis[...], precision=highest, preferred_element_type=F32)
    terms = got_ref[0, 224:].astype(F32)
    eigen = (terms[:, 108:109] + terms[:, 109:110]) + terms[:, 110:111]
    scaled = rotated / (eigen * out_eigen[...] + DAMPING)
    scaled = jnp.where((iota((128, 256), 0) & 63) < 54, scaled, 0.0)
    turned = lax.dot_general(
        scaled, out_basis[...], (((1,), (1,)), ((), ())), precision=highest, preferred_element_type=F32
    )
    high = turned.astype(BF16)
    rest = (turned - high.astype(F32)).astype(BF16)
    for r in range(4):
        block = got_ref[r, 224:].astype(F32).T.astype(BF16)
        rows = jnp.dot(block, high, preferred_element_type=F32) + jnp.dot(block, rest, preferred_element_type=F32)
        for c in range(2):
            ordered[c, pl.ds(r, 108, stride=4), :] = rows[:108, 128 * c : 128 * c + 128]
    for c in range(2):
        ordered[c, 432:, :] = jnp.zeros((8, 128), F32)
    for to in range(8):
        rows = [ordered[c, 54 * to : 54 * to + 56, :] for c in range(2)]
        out_ref[to] = jnp.concatenate(rows, axis=0).astype(BF16)


def over_xc_body(got_ref, out_ref):
    total = sum(got_ref[i].astype(F32) for i in range(8))
    for to in range(4):
        out_ref[to] = total


def last_body(got_ref, out_ref):
    total = (got_ref[0] + got_ref[1]) + (got_ref[2] + got_ref[3])
    out_ref[...] = jnp.concatenate([total[:54], total[56:110]], axis=1)


def data_grad_body(low_ref, high_ref, mine_ref, weight_any, out_ref, token_ref, weight, sem):
    copy = pltpu.make_async_copy(weight_any, weight, sem)
    copy.start()
    none = jnp.zeros((16, 256), BF16)
    total = jnp.zeros((256, 128), F32)
    for a in range(3):
        wide = (high_ref, mine_ref, low_ref)[a][...].astype(F32)
        if a == 0:
            copy.wait()
        for c in range(3):
            moved = x_shifted(wide, 1 - c).astype(BF16)
            for b in range(3):
                if b == 2:
                    shifted = jnp.concatenate([none, moved[:240]], axis=0)
                elif b == 0:
                    shifted = jnp.concatenate([moved[16:], none], axis=0)
                else:
                    shifted = moved
                tap = 9 * a + 3 * b + c
                total = total + lax.dot_general(
                    shifted,
                    weight[128 * tap : 128 * tap + 128, :],
                    (((1,), (1,)), ((), ())),
                    preferred_element_type=F32,
                )
    out_ref[...] = total.astype(BF16)
    token_ref[...] = jnp.zeros((8, 128), F32)


def neighbours(block):
    count = 64
    up = [(i, i + 1) for i in range(count - 1)]
    down = [(i + 1, i) for i in range(count - 1)]
    return lax.ppermute(block, SPACE, up), lax.ppermute(block, SPACE, down)


def per_device(
    activations,
    conv_weight,
    conv_bias,
    cotangent,
    basis_panels,
    panel_owner,
    output_basis,
    input_eigen,
    output_eigen,
):
    dma = pltpu.SemaphoreType.DMA
    place = jnp.stack([lax.axis_index("y"), lax.axis_index("zg")]).astype(jnp.int32)
    inner = lax.axis_index(XC).astype(jnp.int32).reshape(1)
    plane = activations.reshape(256, 128)
    low, high = neighbours(plane)

    stored = call(
        basis_body,
        shape((4, 64, 128), BF16),
        arrays=(basis_panels[0].T,),
        remote=(input_eigen.reshape(1, 54),),
        scratch=[pltpu.VMEM((1, 54), F32), dma],
        flops=4_000_000_000,
    )
    delta, send, slices = call(
        forward_body,
        [shape((256, 256), BF16), shape((8, 384, 128), BF16), shape((16, 64, 128), BF16)],
        (inner,),
        (low, high, plane, conv_weight, conv_bias.reshape(1, 256), cotangent.reshape(256, 256), stored),
        scratch=[pltpu.VMEM((256, 3456), BF16)],
        flops=2 * 256 * 3456 * 256,
    )
    slices = exchange(slices, ("y", "zl"))
    part = call(
        weight_grad_body,
        shape((16, 64, 128), BF16),
        arrays=(exchange(send, XC),),
        after=(slices,),
        scratch=[pltpu.VMEM((288, 2560), BF16), pltpu.VMEM((2048, 128), BF16), pltpu.VMEM((864, 128), F32)],
        flops=2 * 864 * 2048 * 128,
    )
    delta_low, delta_high = neighbours(delta)
    part = call(
        over_y_zl_body,
        shape((4, 320, 128), BF16),
        (place,),
        (exchange(part, ("y", "zl")), slices),
        after=(delta_low, delta_high),
    )
    data, token = call(
        data_grad_body,
        [shape((256, 128), BF16), shape((8, 128), F32)],
        arrays=(delta_low, delta_high, delta),
        remote=(conv_weight,),
        after=(part,),
        scratch=[pltpu.VMEM((3456, 256), BF16), dma],
        flops=2 * 256 * 3456 * 256,
    )
    part, basis = call(
        over_zh_zg_body,
        [shape((32, 64, 128), BF16), shape((8, 128, 128), BF16)],
        arrays=(exchange(part, ("zh", "zg")),),
        after=(token,),
    )
    rotated = call(
        rotate_body,
        shape((4, 352, 128), BF16),
        (panel_owner, place),
        (exchange(part, YXC), basis),
        scratch=[pltpu.VMEM((2, 1024, 128), F32), pltpu.VMEM((896, 256), F32)],
    )
    part = call(
        update_body,
        shape((8, 112, 128), BF16),
        arrays=(exchange(rotated, "zl"),),
        remote=(output_basis, output_eigen.reshape(1, 256)),
        scratch=[
            pltpu.VMEM((256, 256), F32),
            pltpu.VMEM((1, 256), F32),
            pltpu.VMEM((2, 440, 128), F32),
            dma((2,)),
        ],
    )
    part = call(over_xc_body, shape((4, 112, 128), F32), arrays=(exchange(part, XC),))
    update = call(last_body, shape((54, 256), F32), arrays=(exchange(part, "y"),))
    return (data.reshape(1, 1, 16, 16, 128), update)


def solution(mesh):
    fine = Mesh(mesh.devices.reshape(SIZES), AXES)
    both = P(SAMPLE, SPACE, None, None, None)
    return jax.shard_map(
        per_device,
        mesh=fine,
        in_specs=(both, P(), P(), both, P(SAMPLE, None, SPACE), P(), P(), P(SPACE), P()),
        out_specs=(both, P(SPACE, None)),
        check_vma=False,
    )
```

```python
import jax
import jax.numpy as jnp
from jax import lax
from jax.experimental import pallas as pl
from jax.experimental.pallas import tpu as pltpu
from jax.sharding import Mesh
from jax.sharding import PartitionSpec as P

DAMPING = 0.001
CELLS = 131072
BF16 = jnp.bfloat16
F32 = jnp.float32
VMEM = pl.BlockSpec(memory_space=pltpu.VMEM)
SMEM = pl.BlockSpec(memory_space=pltpu.SMEM)
LIMIT = 48 * 1024 * 1024
ANY = pl.BlockSpec(memory_space=pl.ANY)
AXES = ("y", "zh", "zg", "zl", "x", "c")
SIZES = (4, 2, 2, 4, 4, 2)
SAMPLE = ("y", "zh")
XC = ("x", "c")
YXC = ("y", "x", "c")
SPACE = ("zg", "zl", "x", "c")


def call(body, out_shape, scalars=(), arrays=(), remote=(), after=(), scratch=(), flops=0, limit=LIMIT):
    many = isinstance(out_shape, (list, tuple))
    inputs = (*scalars, *arrays, *remote, *after)
    kept = len(inputs) - len(after)

    def kernel(*refs):
        body(*refs[:kept], *refs[len(inputs) :])

    return pl.pallas_call(
        kernel,
        out_shape=out_shape,
        in_specs=[SMEM] * len(scalars) + [VMEM] * len(arrays) + [ANY] * (len(remote) + len(after)),
        out_specs=[VMEM] * len(out_shape) if many else VMEM,
        scratch_shapes=list(scratch),
        compiler_params=pltpu.CompilerParams(vmem_limit_bytes=limit),
        cost_estimate=pl.CostEstimate(
            flops=flops,
            bytes_accessed=sum(a.size * a.dtype.itemsize for a in inputs),
            transcendentals=0,
        ),
    )(*inputs)


def shape(dims, dtype):
    return jax.ShapeDtypeStruct(dims, dtype)


def iota(dims, axis):
    return lax.broadcasted_iota(jnp.int32, dims, axis)


def exchange(x, axes):
    return lax.all_to_all(x, axes, 0, 0)


def started(copies):
    for copy in copies:
        copy.start()
    return copies


def x_shifted(rows, step):
    if step == 0:
        return rows
    x = iota(rows.shape, 0) & 15
    inside = (x + step >= 0) & (x + step < 16)
    return jnp.where(inside, pltpu.roll(rows, (-step) % 256, 0), 0.0)


def basis_body(panel, eigen_any, out_ref, eigen, sem):
    copy = pltpu.make_async_copy(eigen_any, eigen, sem)
    copy.start()
    copy.wait()
    row = iota((54, 54), 0)
    column = jnp.sum(jnp.where(row == iota((54, 54), 1), eigen[...], 0.0), axis=1, keepdims=True)
    column = jnp.concatenate([column, jnp.ones((10, 1), F32)], axis=0)
    first = column.astype(BF16).astype(F32)
    second = (column - first).astype(BF16).astype(F32)
    third = column - first - second
    for r in range(4):
        pick = iota((432, 128), 0) == 4 * iota((432, 128), 1) + r
        block = jnp.dot(panel[...], jnp.where(pick, 1.0, 0.0).astype(BF16), preferred_element_type=F32)
        block = jnp.concatenate([block, jnp.zeros((10, 128), F32)], axis=0)
        at = iota((64, 128), 1)
        block = jnp.where(at == 108, first, block)
        block = jnp.where(at == 109, second, block)
        block = jnp.where(at == 110, third, block)
        out_ref[r] = block.astype(BF16)


def by_side(place_ref, inside, outside):
    first = place_ref[3] == 0
    inside, outside = inside[...].astype(F32), outside[...].astype(F32)
    return jnp.where(first, outside, inside), jnp.where(first, inside, outside)


def forward_body(
    place_ref, inside_ref, outside_ref, mine, weight, bias, cot, basis_ref, delta_ref, send_ref, same_ref, patches
):
    same_ref[...] = basis_ref[...]
    low, high = by_side(place_ref, inside_ref, outside_ref)
    planes = (low, mine[...].astype(F32), high)
    none = jnp.zeros((16, 128), BF16)
    for a in range(3):
        wide = planes[a]
        for c in range(3):
            moved = x_shifted(wide, c - 1).astype(BF16)
            for b in range(3):
                at = (9 * a + 3 * b + c) * 128
                if b == 0:
                    shifted = jnp.concatenate([none, moved[:240]], axis=0)
                elif b == 2:
                    shifted = jnp.concatenate([moved[16:], none], axis=0)
                else:
                    shifted = moved
                patches[:, at : at + 128] = shifted
    pre = jnp.dot(patches[...], weight[...], preferred_element_type=F32) + bias[...]
    logistic = 1.0 / (1.0 + jnp.exp(-pre))
    delta = (cot[...].astype(F32) * logistic * (1.0 + pre * (1.0 - logistic))).astype(BF16)
    delta_ref[...] = delta
    act_t = planes[1].T.astype(BF16)
    rim_t = jnp.where(place_ref[4] < 4, low, high).T.astype(BF16)
    for x in range(4):
        for c in range(2):
            to = 2 * x + c
            for half in range(2):
                lanes = slice(128 * half, 128 * half + 128)
                rows = slice(32 * x, 32 * x + 32)
                send_ref[to, 32 * half : 32 * half + 32] = act_t[rows, lanes]
                send_ref[to, 64 + 32 * half : 96 + 32 * half] = rim_t[rows, lanes]
            send_ref[to, 128:] = delta[:, 128 * c : 128 * c + 128]


def weight_grad_body(place_ref, got_ref, basis_ref, out_ref, own_ref, one_ref, two_ref, three_ref, moved, deltas, whole):
    pieces = []
    for plane, at in [(0, 64)] + [(e, 0) for e in range(8)] + [(7, 64)]:
        pieces.append(got_ref[plane, at : at + 32].astype(F32))
        pieces.append(got_ref[plane, at + 32 : at + 64].astype(F32))
    acts = jnp.concatenate(pieces, axis=1)
    lane = iota((32, 2560), 1)
    x = lane & 15
    y = (lane >> 4) & 15
    for b in range(3):
        for c in range(3):
            step = 16 * (b - 1) + (c - 1)
            turned = pltpu.roll(acts, (-step) % 2560, 1) if step else acts
            inside = (x + c >= 1) & (x + c < 17) & (y + b >= 1) & (y + b < 17)
            moved[32 * (3 * b + c) : 32 * (3 * b + c) + 32, :] = jnp.where(inside, turned, 0.0).astype(BF16)
    for e in range(8):
        deltas[256 * e : 256 * e + 256, :] = got_ref[e, 128:]
    for a in range(3):
        whole[288 * a : 288 * a + 288, :] = jnp.dot(
            moved[:, 256 * a : 256 * a + 2048], deltas[...], preferred_element_type=F32
        )
    for k, ref in enumerate((own_ref, one_ref, two_ref, three_ref)):
        ref[...] = basis_ref[place_ref[2] ^ k]
    none = jnp.zeros((5, 128), F32)
    for y_to in range(4):
        for z_to in range(4):
            parts = []
            for e in range(2):
                parts.append(whole[pl.ds(8 * y_to + 4 * e + z_to, 27, stride=32), :])
                parts.append(none)
            out_ref[4 * y_to + z_to] = jnp.concatenate(parts, axis=0).astype(BF16)


def over_y_zl_body(place_ref, got_ref, own_ref, one_ref, two_ref, three_ref, out_ref):
    total = (sum(got_ref[i].astype(F32) for i in range(16)) * (1.0 / CELLS)).astype(BF16)
    for to in range(4):
        out_ref[to, :64] = total
    for k, ref in enumerate((own_ref, one_ref, two_ref, three_ref)):
        at = pl.multiple_of(64 + 64 * (place_ref[2] ^ k), 64)
        for to in range(4):
            out_ref[to, pl.ds(at, 64)] = ref[...]


def over_zh_zg_body(owner_ref, place_ref, got_ref, out_ref, basis_ref, own_ref, one_ref, two_ref, three_ref):
    total = sum(got_ref[i, :64].astype(F32) for i in range(4)).astype(BF16)
    for to in range(32):
        out_ref[to] = total
    for zh in range(2):
        for y in range(4):
            for zg in range(2):
                block = got_ref[2 * zh + zg, 64 + 64 * y : 128 + 64 * y]
                basis_ref[2 * y + zh, 64 * zg : 64 * zg + 64] = block
    for k, ref in enumerate((own_ref, one_ref, two_ref, three_ref)):
        ref[...] = basis_ref[owner_ref[4 * place_ref[1] + (place_ref[2] ^ k)]]


def rotate_body(owner_ref, got_ref, basis_ref, out_ref, grads, ordered):
    for y in range(4):
        for x in range(4):
            at = 32 * (8 * x + 2 * y)
            for c in range(2):
                grads[c, at : at + 64, :] = got_ref[8 * y + 2 * x + c].astype(F32)
    for tap in range(27):
        for c in range(2):
            ordered[32 * tap : 32 * tap + 32, 128 * c : 128 * c + 128] = grads[c, pl.ds(tap, 32, stride=32), :]
    ordered[864:, :] = jnp.zeros((32, 256), F32)
    inside = iota((128, 128), 1) < 108
    total = jnp.zeros((128, 256), F32)
    for j in range(8):
        block = jnp.where(inside, basis_ref[owner_ref[j]].astype(F32), 0.0).astype(BF16)
        rows = ordered[108 * j : 108 * j + 128, :].astype(BF16)
        total = total + jnp.dot(block, rows, preferred_element_type=F32)
    total = jnp.concatenate(
        [total[64 * zg : 64 * zg + 56, 128 * c : 128 * c + 128] for zg in range(2) for c in range(2)], axis=0
    ).astype(BF16)
    for to in range(4):
        out_ref[to] = total


def update_body(
    place_ref, got_ref, own_ref, one_ref, two_ref, three_ref, out_basis_any, out_eigen_any,
    out_ref, panel, out_basis, out_eigen, ordered, sems,
):
    for k, ref in enumerate((own_ref, one_ref, two_ref, three_ref)):
        panel[place_ref[2] ^ k] = ref[...]
    copies = [
        pltpu.make_async_copy(out_basis_any, out_basis, sems.at[0]),
        pltpu.make_async_copy(out_eigen_any, out_eigen, sems.at[1]),
    ]
    started(copies)
    highest = lax.Precision.HIGHEST
    total = sum(got_ref[i].astype(F32) for i in range(4))
    none = jnp.zeros((8, 256), F32)
    parts = []
    for zg in range(2):
        at = 112 * zg
        parts.append(jnp.concatenate([total[at : at + 56], total[at + 56 : at + 112]], axis=1))
        parts.append(none)
    rotated = jnp.concatenate(parts, axis=0)
    for copy in copies:
        copy.wait()
    rotated = jnp.dot(rotated, out_basis[...], precision=highest, preferred_element_type=F32)
    terms = own_ref[...].astype(F32)
    eigen = (terms[:, 108:109] + terms[:, 109:110]) + terms[:, 110:111]
    scaled = rotated / (eigen * out_eigen[...] + DAMPING)
    scaled = jnp.where((iota((128, 256), 0) & 63) < 54, scaled, 0.0)
    turned = lax.dot_general(
        scaled, out_basis[...], (((1,), (1,)), ((), ())), precision=highest, preferred_element_type=F32
    )
    high = turned.astype(BF16)
    rest = (turned - high.astype(F32)).astype(BF16)
    for r in range(4):
        block = panel[r].astype(F32).T.astype(BF16)
        rows = jnp.dot(block, high, preferred_element_type=F32) + jnp.dot(block, rest, preferred_element_type=F32)
        for c in range(2):
            ordered[c, pl.ds(r, 108, stride=4), :] = rows[:108, 128 * c : 128 * c + 128]
    for c in range(2):
        ordered[c, 432:, :] = jnp.zeros((8, 128), F32)
    for to in range(8):
        rows = [ordered[c, 54 * to : 54 * to + 56, :] for c in range(2)]
        out_ref[to] = jnp.concatenate(rows, axis=0).astype(BF16)


def over_xc_body(got_ref, out_ref):
    total = sum(got_ref[i].astype(F32) for i in range(8))
    for to in range(4):
        out_ref[to] = total


def last_body(got_ref, out_ref):
    total = (got_ref[0] + got_ref[1]) + (got_ref[2] + got_ref[3])
    out_ref[...] = jnp.concatenate([total[:54], total[56:110]], axis=1)


def data_grad_body(place_ref, inside_ref, outside_ref, mine_ref, weight_any, out_ref, token_ref, weight, sem):
    copy = pltpu.make_async_copy(weight_any, weight, sem)
    copy.start()
    low, high = by_side(place_ref, inside_ref, outside_ref)
    planes = (high, mine_ref[...].astype(F32), low)
    none = jnp.zeros((16, 256), BF16)
    total = jnp.zeros((256, 128), F32)
    for a in range(3):
        wide = planes[a]
        if a == 0:
            copy.wait()
        for c in range(3):
            moved = x_shifted(wide, 1 - c).astype(BF16)
            for b in range(3):
                if b == 2:
                    shifted = jnp.concatenate([none, moved[:240]], axis=0)
                elif b == 0:
                    shifted = jnp.concatenate([moved[16:], none], axis=0)
                else:
                    shifted = moved
                tap = 9 * a + 3 * b + c
                total = total + lax.dot_general(
                    shifted,
                    weight[128 * tap : 128 * tap + 128, :],
                    (((1,), (1,)), ((), ())),
                    preferred_element_type=F32,
                )
    out_ref[...] = total.astype(BF16)
    token_ref[...] = jnp.zeros((8, 128), F32)


def neighbours(block):
    inside = lax.ppermute(block, "c", [(0, 1), (1, 0)])
    pairs = [(i, i + 1) for i in range(1, 63, 2)]
    return inside, lax.ppermute(block, SPACE, pairs + [(j, i) for i, j in pairs])


def among_zl(blocks):
    return [blocks[0]] + [lax.ppermute(blocks[k], "zl", [(i, i ^ k) for i in range(4)]) for k in (1, 2, 3)]


def per_device(
    activations,
    conv_weight,
    conv_bias,
    cotangent,
    basis_panels,
    panel_owner,
    output_basis,
    input_eigen,
    output_eigen,
):
    dma = pltpu.SemaphoreType.DMA
    place = jnp.stack([lax.axis_index(a) for a in ("y", "zg", "zl", "c", XC)]).astype(jnp.int32)
    plane = activations.reshape(256, 128)
    inside, outside = neighbours(plane)

    stored = call(
        basis_body,
        shape((4, 64, 128), BF16),
        arrays=(basis_panels[0].T,),
        remote=(input_eigen.reshape(1, 54),),
        scratch=[pltpu.VMEM((1, 54), F32), dma],
        flops=4_000_000_000,
    )
    delta, send, stored = call(
        forward_body,
        [shape((256, 256), BF16), shape((8, 384, 128), BF16), shape((4, 64, 128), BF16)],
        (place,),
        (inside, outside, plane, conv_weight, conv_bias.reshape(1, 256), cotangent.reshape(256, 256), stored),
        scratch=[pltpu.VMEM((256, 3456), BF16)],
        flops=2 * 256 * 3456 * 256,
    )
    stored = lax.ppermute(stored, ("y", "zl"), [(4 * y + z, 4 * z + y) for y in range(4) for z in range(4)])
    part, *slices = call(
        weight_grad_body,
        [shape((16, 64, 128), BF16)] + [shape((64, 128), BF16)] * 4,
        (place,),
        (exchange(send, XC), stored),
        scratch=[pltpu.VMEM((288, 2560), BF16), pltpu.VMEM((2048, 128), BF16), pltpu.VMEM((864, 128), F32)],
        flops=2 * 864 * 2048 * 128,
    )
    part = call(
        over_y_zl_body,
        shape((4, 320, 128), BF16),
        (place,),
        (exchange(part, ("y", "zl")), *among_zl(slices)),
    )
    inside, outside = neighbours(delta)
    data, token = call(
        data_grad_body,
        [shape((256, 128), BF16), shape((8, 128), F32)],
        (place,),
        (inside, outside, delta),
        (conv_weight,),
        after=(part,),
        scratch=[pltpu.VMEM((3456, 256), BF16), dma],
        flops=2 * 256 * 3456 * 256,
    )
    part, basis, *slices = call(
        over_zh_zg_body,
        [shape((32, 64, 128), BF16), shape((8, 128, 128), BF16)] + [shape((128, 128), BF16)] * 4,
        (panel_owner, place),
        (exchange(part, ("zh", "zg")),),
        after=(token,),
    )
    slices = among_zl(slices)
    rotated = call(
        rotate_body,
        shape((4, 224, 128), BF16),
        (panel_owner,),
        (exchange(part, YXC), basis),
        after=slices[1:],
        scratch=[pltpu.VMEM((2, 1024, 128), F32), pltpu.VMEM((896, 256), F32)],
    )
    part = call(
        update_body,
        shape((8, 112, 128), BF16),
        (place,),
        (exchange(rotated, "zl"), *slices),
        (output_basis, output_eigen.reshape(1, 256)),
        scratch=[
            pltpu.VMEM((4, 128, 128), BF16),
            pltpu.VMEM((256, 256), F32),
            pltpu.VMEM((1, 256), F32),
            pltpu.VMEM((2, 440, 128), F32),
            dma((2,)),
        ],
    )
    part = call(over_xc_body, shape((4, 112, 128), F32), arrays=(exchange(part, XC),))
    update = call(last_body, shape((54, 256), F32), arrays=(exchange(part, "y"),))
    return (data.reshape(1, 1, 16, 16, 128), update)


def solution(mesh):
    fine = Mesh(mesh.devices.reshape(SIZES), AXES)
    both = P(SAMPLE, SPACE, None, None, None)
    return jax.shard_map(
        per_device,
        mesh=fine,
        in_specs=(both, P(), P(), both, P(SAMPLE, None, SPACE), P(), P(), P(SPACE), P()),
        out_specs=(both, P(SPACE, None)),
        check_vma=False,
    )
```

```python
import jax
import jax.numpy as jnp
from jax import lax
from jax.experimental import pallas as pl
from jax.experimental.pallas import tpu as pltpu
from jax.sharding import Mesh
from jax.sharding import PartitionSpec as P

DAMPING = 0.001
CELLS = 131072
BF16 = jnp.bfloat16
F32 = jnp.float32
VMEM = pl.BlockSpec(memory_space=pltpu.VMEM)
SMEM = pl.BlockSpec(memory_space=pltpu.SMEM)
LIMIT = 48 * 1024 * 1024
ANY = pl.BlockSpec(memory_space=pl.ANY)
AXES = ("y", "zh", "zg", "zl", "x", "c")
SIZES = (4, 2, 2, 4, 4, 2)
SAMPLE = ("y", "zh")
XC = ("x", "c")
YXC = ("y", "x", "c")
SPACE = ("zg", "zl", "x", "c")


def call(body, out_shape, scalars=(), arrays=(), remote=(), after=(), scratch=(), flops=0, limit=LIMIT):
    many = isinstance(out_shape, (list, tuple))
    inputs = (*scalars, *arrays, *remote, *after)
    kept = len(inputs) - len(after)

    def kernel(*refs):
        body(*refs[:kept], *refs[len(inputs) :])

    return pl.pallas_call(
        kernel,
        out_shape=out_shape,
        in_specs=[SMEM] * len(scalars) + [VMEM] * len(arrays) + [ANY] * (len(remote) + len(after)),
        out_specs=[VMEM] * len(out_shape) if many else VMEM,
        scratch_shapes=list(scratch),
        compiler_params=pltpu.CompilerParams(vmem_limit_bytes=limit),
        cost_estimate=pl.CostEstimate(
            flops=flops,
            bytes_accessed=sum(a.size * a.dtype.itemsize for a in inputs),
            transcendentals=0,
        ),
    )(*inputs)


def shape(dims, dtype):
    return jax.ShapeDtypeStruct(dims, dtype)


def iota(dims, axis):
    return lax.broadcasted_iota(jnp.int32, dims, axis)


def exchange(x, axes):
    return lax.all_to_all(x, axes, 0, 0)


def started(copies):
    for copy in copies:
        copy.start()
    return copies


def x_shifted(rows, step):
    if step == 0:
        return rows
    x = iota(rows.shape, 0) & 15
    inside = (x + step >= 0) & (x + step < 16)
    return jnp.where(inside, pltpu.roll(rows, (-step) % 256, 0), 0.0)


def basis_body(panel, eigen_any, out_ref, eigen, sem):
    copy = pltpu.make_async_copy(eigen_any, eigen, sem)
    copy.start()
    copy.wait()
    row = iota((54, 54), 0)
    column = jnp.sum(jnp.where(row == iota((54, 54), 1), eigen[...], 0.0), axis=1, keepdims=True)
    column = jnp.concatenate([column, jnp.ones((10, 1), F32)], axis=0)
    first = column.astype(BF16).astype(F32)
    second = (column - first).astype(BF16).astype(F32)
    third = column - first - second
    for r in range(4):
        pick = iota((432, 128), 0) == 4 * iota((432, 128), 1) + r
        block = jnp.dot(panel[...], jnp.where(pick, 1.0, 0.0).astype(BF16), preferred_element_type=F32)
        block = jnp.concatenate([block, jnp.zeros((10, 128), F32)], axis=0)
        at = iota((64, 128), 1)
        block = jnp.where(at == 108, first, block)
        block = jnp.where(at == 109, second, block)
        block = jnp.where(at == 110, third, block)
        out_ref[r] = block.astype(BF16)


def by_side(place_ref, inside_ref, outside_ref, planes):
    second = place_ref[3]
    planes[2 - 2 * second] = inside_ref[...]
    planes[2 * second] = outside_ref[...]


def forward_body(
    place_ref, inside_ref, outside_ref, mine, weight, bias, cot, basis_ref,
    delta_ref, send_ref, own_ref, one_ref, two_ref, three_ref, patches, planes,
):
    for k, ref in enumerate((own_ref, one_ref, two_ref, three_ref)):
        ref[...] = basis_ref[place_ref[0] ^ k]
    by_side(place_ref, inside_ref, outside_ref, planes)
    planes[1] = mine[...]
    none = jnp.zeros((16, 128), BF16)
    for a in range(3):
        wide = planes[a].astype(F32)
        for c in range(3):
            moved = x_shifted(wide, c - 1).astype(BF16)
            for b in range(3):
                at = (9 * a + 3 * b + c) * 128
                if b == 0:
                    shifted = jnp.concatenate([none, moved[:240]], axis=0)
                elif b == 2:
                    shifted = jnp.concatenate([moved[16:], none], axis=0)
                else:
                    shifted = moved
                patches[:, at : at + 128] = shifted
    pre = jnp.dot(patches[...], weight[...], preferred_element_type=F32) + bias[...]
    logistic = 1.0 / (1.0 + jnp.exp(-pre))
    delta = (cot[...].astype(F32) * logistic * (1.0 + pre * (1.0 - logistic))).astype(BF16)
    delta_ref[...] = delta
    act_t = mine[...].astype(F32).T.astype(BF16)
    rim_t = planes[2 * (place_ref[4] >> 2)].astype(F32).T.astype(BF16)
    for x in range(4):
        for c in range(2):
            to = 2 * x + c
            for half in range(2):
                lanes = slice(128 * half, 128 * half + 128)
                rows = slice(32 * x, 32 * x + 32)
                send_ref[to, 32 * half : 32 * half + 32] = act_t[rows, lanes]
                send_ref[to, 64 + 32 * half : 96 + 32 * half] = rim_t[rows, lanes]
            send_ref[to, 128:] = delta[:, 128 * c : 128 * c + 128]


def weight_grad_body(got_ref, out_ref, moved, deltas, whole):
    pieces = []
    for plane, at in [(0, 64)] + [(e, 0) for e in range(8)] + [(7, 64)]:
        pieces.append(got_ref[plane, at : at + 32].astype(F32))
        pieces.append(got_ref[plane, at + 32 : at + 64].astype(F32))
    acts = jnp.concatenate(pieces, axis=1)
    lane = iota((32, 2560), 1)
    x = lane & 15
    y = (lane >> 4) & 15
    for b in range(3):
        for c in range(3):
            step = 16 * (b - 1) + (c - 1)
            turned = pltpu.roll(acts, (-step) % 2560, 1) if step else acts
            inside = (x + c >= 1) & (x + c < 17) & (y + b >= 1) & (y + b < 17)
            moved[32 * (3 * b + c) : 32 * (3 * b + c) + 32, :] = jnp.where(inside, turned, 0.0).astype(BF16)
    for e in range(8):
        deltas[256 * e : 256 * e + 256, :] = got_ref[e, 128:]
    for a in range(3):
        whole[288 * a : 288 * a + 288, :] = jnp.dot(
            moved[:, 256 * a : 256 * a + 2048], deltas[...], preferred_element_type=F32
        )
    none = jnp.zeros((5, 128), F32)
    for y_to in range(4):
        for z_to in range(4):
            parts = []
            for e in range(2):
                parts.append(whole[pl.ds(8 * y_to + 4 * e + z_to, 27, stride=32), :])
                parts.append(none)
            out_ref[4 * y_to + z_to] = jnp.concatenate(parts, axis=0).astype(BF16)


def over_y_zl_body(place_ref, got_ref, own_ref, one_ref, two_ref, three_ref, out_ref):
    total = (sum(got_ref[i].astype(F32) for i in range(16)) * (1.0 / CELLS)).astype(BF16)
    for to in range(4):
        out_ref[to, :64] = total
    for k, ref in enumerate((own_ref, one_ref, two_ref, three_ref)):
        at = pl.multiple_of(64 + 64 * (place_ref[2] ^ k), 64)
        for to in range(4):
            out_ref[to, pl.ds(at, 64)] = ref[...]


def over_zh_zg_body(owner_ref, place_ref, got_ref, out_ref, basis_ref, own_ref, one_ref, two_ref, three_ref):
    total = sum(got_ref[i, :64].astype(F32) for i in range(4)).astype(BF16)
    for to in range(32):
        out_ref[to] = total
    for zh in range(2):
        for y in range(4):
            for zg in range(2):
                block = got_ref[2 * zh + zg, 64 + 64 * y : 128 + 64 * y]
                basis_ref[2 * y + zh, 64 * zg : 64 * zg + 64] = block
    for k, ref in enumerate((own_ref, one_ref, two_ref, three_ref)):
        ref[...] = basis_ref[owner_ref[4 * place_ref[1] + (place_ref[2] ^ k)]]


def rotate_body(owner_ref, got_ref, basis_ref, out_ref, grads, ordered):
    for y in range(4):
        for x in range(4):
            at = 32 * (8 * x + 2 * y)
            for c in range(2):
                grads[c, at : at + 64, :] = got_ref[8 * y + 2 * x + c].astype(F32)
    for tap in range(27):
        for c in range(2):
            ordered[32 * tap : 32 * tap + 32, 128 * c : 128 * c + 128] = grads[c, pl.ds(tap, 32, stride=32), :]
    ordered[864:, :] = jnp.zeros((32, 256), F32)
    inside = iota((128, 128), 1) < 108
    total = jnp.zeros((128, 256), F32)
    for j in range(8):
        block = jnp.where(inside, basis_ref[owner_ref[j]].astype(F32), 0.0).astype(BF16)
        rows = ordered[108 * j : 108 * j + 128, :].astype(BF16)
        total = total + jnp.dot(block, rows, preferred_element_type=F32)
    total = jnp.concatenate(
        [total[64 * zg : 64 * zg + 56, 128 * c : 128 * c + 128] for zg in range(2) for c in range(2)], axis=0
    ).astype(BF16)
    for to in range(4):
        out_ref[to] = total


def update_body(
    place_ref, got_ref, own_ref, one_ref, two_ref, three_ref, out_basis_any, out_eigen_any,
    out_ref, panel, out_basis, out_eigen, ordered, sems,
):
    for k, ref in enumerate((own_ref, one_ref, two_ref, three_ref)):
        panel[place_ref[2] ^ k] = ref[...]
    copies = [
        pltpu.make_async_copy(out_basis_any, out_basis, sems.at[0]),
        pltpu.make_async_copy(out_eigen_any, out_eigen, sems.at[1]),
    ]
    started(copies)
    highest = lax.Precision.HIGHEST
    total = sum(got_ref[i].astype(F32) for i in range(4))
    none = jnp.zeros((8, 256), F32)
    parts = []
    for zg in range(2):
        at = 112 * zg
        parts.append(jnp.concatenate([total[at : at + 56], total[at + 56 : at + 112]], axis=1))
        parts.append(none)
    rotated = jnp.concatenate(parts, axis=0)
    for copy in copies:
        copy.wait()
    rotated = jnp.dot(rotated, out_basis[...], precision=highest, preferred_element_type=F32)
    terms = own_ref[...].astype(F32)
    eigen = (terms[:, 108:109] + terms[:, 109:110]) + terms[:, 110:111]
    scaled = rotated / (eigen * out_eigen[...] + DAMPING)
    scaled = jnp.where((iota((128, 256), 0) & 63) < 54, scaled, 0.0)
    turned = lax.dot_general(
        scaled, out_basis[...], (((1,), (1,)), ((), ())), precision=highest, preferred_element_type=F32
    )
    high = turned.astype(BF16)
    rest = (turned - high.astype(F32)).astype(BF16)
    for r in range(4):
        block = panel[r].astype(F32).T.astype(BF16)
        rows = jnp.dot(block, high, preferred_element_type=F32) + jnp.dot(block, rest, preferred_element_type=F32)
        for c in range(2):
            ordered[c, pl.ds(r, 108, stride=4), :] = rows[:108, 128 * c : 128 * c + 128]
    for c in range(2):
        ordered[c, 432:, :] = jnp.zeros((8, 128), F32)
    for to in range(8):
        rows = [ordered[c, 54 * to : 54 * to + 56, :] for c in range(2)]
        out_ref[to] = jnp.concatenate(rows, axis=0).astype(BF16)


def over_xc_body(got_ref, out_ref):
    total = sum(got_ref[i].astype(F32) for i in range(8))
    for to in range(4):
        out_ref[to] = total


def last_body(got_ref, out_ref):
    total = (got_ref[0] + got_ref[1]) + (got_ref[2] + got_ref[3])
    out_ref[...] = jnp.concatenate([total[:54], total[56:110]], axis=1)


def data_grad_body(place_ref, inside_ref, outside_ref, mine_ref, weight_any, out_ref, token_ref, weight, planes, sem):
    copy = pltpu.make_async_copy(weight_any, weight, sem)
    copy.start()
    by_side(place_ref, inside_ref, outside_ref, planes)
    planes[1] = mine_ref[...]
    none = jnp.zeros((16, 256), BF16)
    total = jnp.zeros((256, 128), F32)
    for a in range(3):
        wide = planes[2 - a].astype(F32)
        if a == 0:
            copy.wait()
        for c in range(3):
            moved = x_shifted(wide, 1 - c).astype(BF16)
            for b in range(3):
                if b == 2:
                    shifted = jnp.concatenate([none, moved[:240]], axis=0)
                elif b == 0:
                    shifted = jnp.concatenate([moved[16:], none], axis=0)
                else:
                    shifted = moved
                tap = 9 * a + 3 * b + c
                total = total + lax.dot_general(
                    shifted,
                    weight[128 * tap : 128 * tap + 128, :],
                    (((1,), (1,)), ((), ())),
                    preferred_element_type=F32,
                )
    out_ref[...] = total.astype(BF16)
    token_ref[...] = jnp.zeros((8, 128), F32)


def neighbours(block):
    inside = lax.ppermute(block, "c", [(0, 1), (1, 0)])
    pairs = [(i, i + 1) for i in range(1, 63, 2)]
    return inside, lax.ppermute(block, SPACE, pairs + [(j, i) for i, j in pairs])


def turned(blocks):
    return [
        lax.ppermute(block, ("y", "zl"), [(4 * y + z, 4 * z + (y ^ k)) for y in range(4) for z in range(4)])
        for k, block in enumerate(blocks)
    ]


def among_zl(blocks):
    return [blocks[0]] + [lax.ppermute(blocks[k], "zl", [(i, i ^ k) for i in range(4)]) for k in (1, 2, 3)]


def per_device(
    activations,
    conv_weight,
    conv_bias,
    cotangent,
    basis_panels,
    panel_owner,
    output_basis,
    input_eigen,
    output_eigen,
):
    dma = pltpu.SemaphoreType.DMA
    place = jnp.stack([lax.axis_index(a) for a in ("y", "zg", "zl", "c", XC)]).astype(jnp.int32)
    plane = activations.reshape(256, 128)
    inside, outside = neighbours(plane)

    stored = call(
        basis_body,
        shape((4, 64, 128), BF16),
        arrays=(basis_panels[0].T,),
        remote=(input_eigen.reshape(1, 54),),
        scratch=[pltpu.VMEM((1, 54), F32), dma],
        flops=4_000_000_000,
    )
    delta, send, *slices = call(
        forward_body,
        [shape((256, 256), BF16), shape((8, 384, 128), BF16)] + [shape((64, 128), BF16)] * 4,
        (place,),
        (inside, outside, plane, conv_weight, conv_bias.reshape(1, 256), cotangent.reshape(256, 256), stored),
        scratch=[pltpu.VMEM((256, 3456), BF16), pltpu.VMEM((3, 256, 128), BF16)],
        flops=2 * 256 * 3456 * 256,
    )
    slices = turned(slices)
    part = call(
        weight_grad_body,
        shape((16, 64, 128), BF16),
        arrays=(exchange(send, XC),),
        after=slices[:2],
        scratch=[pltpu.VMEM((288, 2560), BF16), pltpu.VMEM((2048, 128), BF16), pltpu.VMEM((864, 128), F32)],
        flops=2 * 864 * 2048 * 128,
    )
    part = call(
        over_y_zl_body,
        shape((4, 320, 128), BF16),
        (place,),
        (exchange(part, ("y", "zl")), *slices),
    )
    part, basis, *slices = call(
        over_zh_zg_body,
        [shape((32, 64, 128), BF16), shape((8, 128, 128), BF16)] + [shape((128, 128), BF16)] * 4,
        (panel_owner, place),
        (exchange(part, ("zh", "zg")),),
    )
    slices = among_zl(slices)
    rotated = call(
        rotate_body,
        shape((4, 224, 128), BF16),
        (panel_owner,),
        (exchange(part, YXC), basis),
        after=slices[1:2],
        scratch=[pltpu.VMEM((2, 1024, 128), F32), pltpu.VMEM((896, 256), F32)],
    )
    part = call(
        update_body,
        shape((8, 112, 128), BF16),
        (place,),
        (exchange(rotated, "zl"), *slices),
        (output_basis, output_eigen.reshape(1, 256)),
        scratch=[
            pltpu.VMEM((4, 128, 128), BF16),
            pltpu.VMEM((256, 256), F32),
            pltpu.VMEM((1, 256), F32),
            pltpu.VMEM((2, 440, 128), F32),
            dma((2,)),
        ],
    )
    inside, outside = neighbours(delta)
    part = call(
        over_xc_body, shape((4, 112, 128), F32), arrays=(exchange(part, XC),), after=(inside, outside)
    )
    data, token = call(
        data_grad_body,
        [shape((256, 128), BF16), shape((8, 128), F32)],
        (place,),
        (inside, outside, delta),
        (conv_weight,),
        after=(part,),
        scratch=[pltpu.VMEM((3456, 256), BF16), pltpu.VMEM((3, 256, 256), BF16), dma],
        flops=2 * 256 * 3456 * 256,
    )
    update = call(last_body, shape((54, 256), F32), arrays=(exchange(part, "y"),), after=(token,))
    return (data.reshape(1, 1, 16, 16, 128), update)


def solution(mesh):
    fine = Mesh(mesh.devices.reshape(SIZES), AXES)
    both = P(SAMPLE, SPACE, None, None, None)
    return jax.shard_map(
        per_device,
        mesh=fine,
        in_specs=(both, P(), P(), both, P(SAMPLE, None, SPACE), P(), P(), P(SPACE), P()),
        out_specs=(both, P(SPACE, None)),
        check_vma=False,
    )
```

```python
import jax
import jax.numpy as jnp
from jax import lax
from jax.experimental import pallas as pl
from jax.experimental.pallas import tpu as pltpu
from jax.sharding import Mesh
from jax.sharding import PartitionSpec as P

DAMPING = 0.001
CELLS = 131072
BF16 = jnp.bfloat16
F32 = jnp.float32
VMEM = pl.BlockSpec(memory_space=pltpu.VMEM)
SMEM = pl.BlockSpec(memory_space=pltpu.SMEM)
LIMIT = 48 * 1024 * 1024
ANY = pl.BlockSpec(memory_space=pl.ANY)
AXES = ("y", "zh", "zg", "zl", "x", "c")
SIZES = (4, 2, 2, 4, 4, 2)
SAMPLE = ("y", "zh")
XC = ("x", "c")
YXC = ("y", "x", "c")
SPACE = ("zg", "zl", "x", "c")


def call(body, out_shape, scalars=(), arrays=(), remote=(), after=(), scratch=(), flops=0, limit=LIMIT):
    many = isinstance(out_shape, (list, tuple))
    inputs = (*scalars, *arrays, *remote, *after)
    kept = len(inputs) - len(after)

    def kernel(*refs):
        body(*refs[:kept], *refs[len(inputs) :])

    return pl.pallas_call(
        kernel,
        out_shape=out_shape,
        in_specs=[SMEM] * len(scalars) + [VMEM] * len(arrays) + [ANY] * (len(remote) + len(after)),
        out_specs=[VMEM] * len(out_shape) if many else VMEM,
        scratch_shapes=list(scratch),
        compiler_params=pltpu.CompilerParams(vmem_limit_bytes=limit),
        cost_estimate=pl.CostEstimate(
            flops=flops,
            bytes_accessed=sum(a.size * a.dtype.itemsize for a in inputs),
            transcendentals=0,
        ),
    )(*inputs)


def shape(dims, dtype):
    return jax.ShapeDtypeStruct(dims, dtype)


def iota(dims, axis):
    return lax.broadcasted_iota(jnp.int32, dims, axis)


def exchange(x, axes):
    return lax.all_to_all(x, axes, 0, 0)


def started(copies):
    for copy in copies:
        copy.start()
    return copies


def x_shifted(rows, step):
    if step == 0:
        return rows
    x = iota(rows.shape, 0) & 15
    inside = (x + step >= 0) & (x + step < 16)
    return jnp.where(inside, pltpu.roll(rows, (-step) % 256, 0), 0.0)


def basis_body(panel, eigen_any, out_ref, eigen, sem):
    copy = pltpu.make_async_copy(eigen_any, eigen, sem)
    copy.start()
    copy.wait()
    row = iota((54, 54), 0)
    column = jnp.sum(jnp.where(row == iota((54, 54), 1), eigen[...], 0.0), axis=1, keepdims=True)
    column = jnp.concatenate([column, jnp.ones((10, 1), F32)], axis=0)
    first = column.astype(BF16).astype(F32)
    second = (column - first).astype(BF16).astype(F32)
    third = column - first - second
    for r in range(4):
        pick = iota((432, 128), 0) == 4 * iota((432, 128), 1) + r
        block = jnp.dot(panel[...], jnp.where(pick, 1.0, 0.0).astype(BF16), preferred_element_type=F32)
        block = jnp.concatenate([block, jnp.zeros((10, 128), F32)], axis=0)
        at = iota((64, 128), 1)
        block = jnp.where(at == 108, first, block)
        block = jnp.where(at == 109, second, block)
        block = jnp.where(at == 110, third, block)
        out_ref[r] = block.astype(BF16)


def by_side(core_ref, inside_ref, outside_ref, planes):
    second = core_ref[0]
    planes[2 - 2 * second] = inside_ref[...]
    planes[2 * second] = outside_ref[...]


def forward_body(
    y_ref, core_ref, inner_ref, inside_ref, outside_ref, mine, weight, bias, cot, basis_ref,
    delta_ref, send_ref, even_ref, odd_ref, patches, planes,
):
    for k, ref in enumerate((even_ref, odd_ref)):
        ref[0] = basis_ref[y_ref[0] ^ k]
        ref[1] = basis_ref[y_ref[0] ^ k ^ 2]
    by_side(core_ref, inside_ref, outside_ref, planes)
    planes[1] = mine[...]
    none = jnp.zeros((16, 128), BF16)
    for a in range(3):
        wide = planes[a].astype(F32)
        for c in range(3):
            moved = x_shifted(wide, c - 1).astype(BF16)
            for b in range(3):
                at = (9 * a + 3 * b + c) * 128
                if b == 0:
                    shifted = jnp.concatenate([none, moved[:240]], axis=0)
                elif b == 2:
                    shifted = jnp.concatenate([moved[16:], none], axis=0)
                else:
                    shifted = moved
                patches[:, at : at + 128] = shifted
    pre = jnp.dot(patches[...], weight[...], preferred_element_type=F32) + bias[...]
    logistic = 1.0 / (1.0 + jnp.exp(-pre))
    delta = (cot[...].astype(F32) * logistic * (1.0 + pre * (1.0 - logistic))).astype(BF16)
    delta_ref[...] = delta
    act_t = mine[...].astype(F32).T.astype(BF16)
    rim_t = planes[2 * (inner_ref[0] >> 2)].astype(F32).T.astype(BF16)
    for x in range(4):
        for c in range(2):
            to = 2 * x + c
            for half in range(2):
                lanes = slice(128 * half, 128 * half + 128)
                rows = slice(32 * x, 32 * x + 32)
                send_ref[to, 32 * half : 32 * half + 32] = act_t[rows, lanes]
                send_ref[to, 64 + 32 * half : 96 + 32 * half] = rim_t[rows, lanes]
            send_ref[to, 128:] = delta[:, 128 * c : 128 * c + 128]


def weight_grad_body(got_ref, even_ref, odd_ref, out_ref, pair_ref, moved, deltas, whole):
    pieces = []
    for plane, at in [(0, 64)] + [(e, 0) for e in range(8)] + [(7, 64)]:
        pieces.append(got_ref[plane, at : at + 32].astype(F32))
        pieces.append(got_ref[plane, at + 32 : at + 64].astype(F32))
    acts = jnp.concatenate(pieces, axis=1)
    lane = iota((32, 2560), 1)
    x = lane & 15
    y = (lane >> 4) & 15
    for b in range(3):
        for c in range(3):
            step = 16 * (b - 1) + (c - 1)
            turned = pltpu.roll(acts, (-step) % 2560, 1) if step else acts
            inside = (x + c >= 1) & (x + c < 17) & (y + b >= 1) & (y + b < 17)
            moved[32 * (3 * b + c) : 32 * (3 * b + c) + 32, :] = jnp.where(inside, turned, 0.0).astype(BF16)
    for e in range(8):
        deltas[256 * e : 256 * e + 256, :] = got_ref[e, 128:]
    for a in range(3):
        whole[288 * a : 288 * a + 288, :] = jnp.dot(
            moved[:, 256 * a : 256 * a + 2048], deltas[...], preferred_element_type=F32
        )
    pair_ref[0] = even_ref[1]
    pair_ref[1] = odd_ref[1]
    none = jnp.zeros((5, 128), F32)
    for y_to in range(4):
        for z_to in range(4):
            parts = []
            for e in range(2):
                parts.append(whole[pl.ds(8 * y_to + 4 * e + z_to, 27, stride=32), :])
                parts.append(none)
            out_ref[4 * y_to + z_to] = jnp.concatenate(parts, axis=0).astype(BF16)


def over_y_zl_body(zl_ref, got_ref, even_ref, odd_ref, pair_ref, out_ref):
    total = (sum(got_ref[i].astype(F32) for i in range(16)) * (1.0 / CELLS)).astype(BF16)
    for to in range(4):
        out_ref[to, :64] = total
    for k, ref in enumerate((even_ref.at[0], odd_ref.at[0], pair_ref.at[0], pair_ref.at[1])):
        at = pl.multiple_of(64 + 64 * (zl_ref[0] ^ k), 64)
        for to in range(4):
            out_ref[to, pl.ds(at, 64)] = ref[...]


def over_zh_zg_body(owner_ref, zg_ref, zl_ref, got_ref, out_ref, basis_ref, here_ref, next_ref):
    total = sum(got_ref[i, :64].astype(F32) for i in range(4)).astype(BF16)
    for to in range(32):
        out_ref[to] = total
    for j in range(8):
        at = pl.multiple_of(64 + 64 * (owner_ref[j] >> 1), 64)
        for zg in range(2):
            basis_ref[j, 64 * zg : 64 * zg + 64] = got_ref[2 * (owner_ref[j] & 1) + zg, pl.ds(at, 64)]
    for k, ref in enumerate((here_ref, next_ref)):
        ref[0] = basis_ref[4 * zg_ref[0] + (zl_ref[0] ^ k)]
        ref[1] = basis_ref[4 * zg_ref[0] + (zl_ref[0] ^ k ^ 2)]


def rotate_body(got_ref, basis_ref, here_ref, next_ref, out_ref, pair_ref, grads, ordered):
    pair_ref[0] = here_ref[1]
    pair_ref[1] = next_ref[1]
    for y in range(4):
        for x in range(4):
            at = 32 * (8 * x + 2 * y)
            for c in range(2):
                grads[c, at : at + 64, :] = got_ref[8 * y + 2 * x + c].astype(F32)
    for tap in range(27):
        for c in range(2):
            ordered[32 * tap : 32 * tap + 32, 128 * c : 128 * c + 128] = grads[c, pl.ds(tap, 32, stride=32), :]
    ordered[864:, :] = jnp.zeros((32, 256), F32)
    inside = iota((128, 128), 1) < 108
    total = jnp.zeros((128, 256), F32)
    for j in range(8):
        block = jnp.where(inside, basis_ref[j].astype(F32), 0.0).astype(BF16)
        rows = ordered[108 * j : 108 * j + 128, :].astype(BF16)
        total = total + jnp.dot(block, rows, preferred_element_type=F32)
    total = jnp.concatenate(
        [total[64 * zg : 64 * zg + 56, 128 * c : 128 * c + 128] for zg in range(2) for c in range(2)], axis=0
    ).astype(BF16)
    for to in range(4):
        out_ref[to] = total


def update_body(
    zl_ref, got_ref, here_ref, next_ref, pair_ref, out_basis_any, out_eigen_any,
    out_ref, panel, out_basis, out_eigen, ordered, sems,
):
    for k, ref in enumerate((here_ref.at[0], next_ref.at[0], pair_ref.at[0], pair_ref.at[1])):
        panel[zl_ref[0] ^ k] = ref[...]
    copies = [
        pltpu.make_async_copy(out_basis_any, out_basis, sems.at[0]),
        pltpu.make_async_copy(out_eigen_any, out_eigen, sems.at[1]),
    ]
    started(copies)
    highest = lax.Precision.HIGHEST
    total = sum(got_ref[i].astype(F32) for i in range(4))
    none = jnp.zeros((8, 256), F32)
    parts = []
    for zg in range(2):
        at = 112 * zg
        parts.append(jnp.concatenate([total[at : at + 56], total[at + 56 : at + 112]], axis=1))
        parts.append(none)
    rotated = jnp.concatenate(parts, axis=0)
    for copy in copies:
        copy.wait()
    rotated = jnp.dot(rotated, out_basis[...], precision=highest, preferred_element_type=F32)
    terms = here_ref[0].astype(F32)
    eigen = (terms[:, 108:109] + terms[:, 109:110]) + terms[:, 110:111]
    scaled = rotated / (eigen * out_eigen[...] + DAMPING)
    scaled = jnp.where((iota((128, 256), 0) & 63) < 54, scaled, 0.0)
    turned = lax.dot_general(
        scaled, out_basis[...], (((1,), (1,)), ((), ())), precision=highest, preferred_element_type=F32
    )
    high = turned.astype(BF16)
    rest = (turned - high.astype(F32)).astype(BF16)
    for r in range(4):
        block = panel[r].astype(F32).T.astype(BF16)
        rows = jnp.dot(block, high, preferred_element_type=F32) + jnp.dot(block, rest, preferred_element_type=F32)
        for c in range(2):
            ordered[c, pl.ds(r, 108, stride=4), :] = rows[:108, 128 * c : 128 * c + 128]
    for c in range(2):
        ordered[c, 432:, :] = jnp.zeros((8, 128), F32)
    for to in range(8):
        rows = [ordered[c, 54 * to : 54 * to + 56, :] for c in range(2)]
        out_ref[to] = jnp.concatenate(rows, axis=0).astype(BF16)


def over_xc_body(got_ref, out_ref):
    total = sum(got_ref[i].astype(F32) for i in range(8))
    for to in range(4):
        out_ref[to] = total


def last_body(got_ref, out_ref):
    total = (got_ref[0] + got_ref[1]) + (got_ref[2] + got_ref[3])
    out_ref[...] = jnp.concatenate([total[:54], total[56:110]], axis=1)


def data_grad_body(core_ref, inside_ref, outside_ref, mine_ref, weight_any, out_ref, token_ref, weight, planes, sem):
    copy = pltpu.make_async_copy(weight_any, weight, sem)
    copy.start()
    by_side(core_ref, inside_ref, outside_ref, planes)
    planes[1] = mine_ref[...]
    none = jnp.zeros((16, 256), BF16)
    total = jnp.zeros((256, 128), F32)
    for a in range(3):
        wide = planes[2 - a].astype(F32)
        if a == 0:
            copy.wait()
        for c in range(3):
            moved = x_shifted(wide, 1 - c).astype(BF16)
            for b in range(3):
                if b == 2:
                    shifted = jnp.concatenate([none, moved[:240]], axis=0)
                elif b == 0:
                    shifted = jnp.concatenate([moved[16:], none], axis=0)
                else:
                    shifted = moved
                tap = 9 * a + 3 * b + c
                total = total + lax.dot_general(
                    shifted,
                    weight[128 * tap : 128 * tap + 128, :],
                    (((1,), (1,)), ((), ())),
                    preferred_element_type=F32,
                )
    out_ref[...] = total.astype(BF16)
    token_ref[...] = jnp.zeros((8, 128), F32)


def neighbours(block):
    inside = lax.ppermute(block, "c", [(0, 1), (1, 0)])
    pairs = [(i, i + 1) for i in range(1, 63, 2)]
    return inside, lax.ppermute(block, SPACE, pairs + [(j, i) for i, j in pairs])


def turned(block, k):
    pairs = [(4 * y + z, 4 * z + (y ^ k)) for y in range(4) for z in range(4)]
    return lax.ppermute(block, ("y", "zl"), pairs)


def across(block, k):
    return lax.ppermute(block, "zl", [(i, i ^ k) for i in range(4)])


def per_device(
    activations,
    conv_weight,
    conv_bias,
    cotangent,
    basis_panels,
    panel_owner,
    output_basis,
    input_eigen,
    output_eigen,
):
    dma = pltpu.SemaphoreType.DMA
    y, zg, zl, core, inner = (lax.axis_index(a).astype(jnp.int32).reshape(1) for a in ("y", "zg", "zl", "c", XC))
    plane = activations.reshape(256, 128)
    inside, outside = neighbours(plane)

    stored = call(
        basis_body,
        shape((4, 64, 128), BF16),
        arrays=(basis_panels[0].T,),
        remote=(input_eigen.reshape(1, 54),),
        scratch=[pltpu.VMEM((1, 54), F32), dma],
        flops=4_000_000_000,
    )
    delta, send, even, odd = call(
        forward_body,
        [shape((256, 256), BF16), shape((8, 384, 128), BF16)] + [shape((2, 64, 128), BF16)] * 2,
        (y, core, inner),
        (inside, outside, plane, conv_weight, conv_bias.reshape(1, 256), cotangent.reshape(256, 256), stored),
        scratch=[pltpu.VMEM((256, 3456), BF16), pltpu.VMEM((3, 256, 128), BF16)],
        flops=2 * 256 * 3456 * 256,
    )
    even, odd = turned(even, 0), turned(odd, 1)
    part, pair = call(
        weight_grad_body,
        [shape((16, 64, 128), BF16), shape((2, 64, 128), BF16)],
        arrays=(exchange(send, XC), even, odd),
        scratch=[pltpu.VMEM((288, 2560), BF16), pltpu.VMEM((2048, 128), BF16), pltpu.VMEM((864, 128), F32)],
        flops=2 * 864 * 2048 * 128,
    )
    part = call(
        over_y_zl_body,
        shape((4, 320, 128), BF16),
        (zl,),
        (exchange(part, ("y", "zl")), even, odd, across(pair, 2)),
    )
    inside, outside = neighbours(delta)
    part, basis, here, there = call(
        over_zh_zg_body,
        [shape((32, 64, 128), BF16), shape((8, 128, 128), BF16)] + [shape((2, 128, 128), BF16)] * 2,
        (panel_owner, zg, zl),
        (exchange(part, ("zh", "zg")),),
        after=(inside, outside),
    )
    there = across(there, 1)
    rotated, pair = call(
        rotate_body,
        [shape((4, 224, 128), BF16), shape((2, 128, 128), BF16)],
        arrays=(exchange(part, YXC), basis, here, there),
        scratch=[pltpu.VMEM((2, 1024, 128), F32), pltpu.VMEM((896, 256), F32)],
    )
    part = call(
        update_body,
        shape((8, 112, 128), BF16),
        (zl,),
        (exchange(rotated, "zl"), here, there, across(pair, 2)),
        (output_basis, output_eigen.reshape(1, 256)),
        scratch=[
            pltpu.VMEM((4, 128, 128), BF16),
            pltpu.VMEM((256, 256), F32),
            pltpu.VMEM((1, 256), F32),
            pltpu.VMEM((2, 440, 128), F32),
            dma((2,)),
        ],
    )
    part = call(over_xc_body, shape((4, 112, 128), F32), arrays=(exchange(part, XC),))
    data, token = call(
        data_grad_body,
        [shape((256, 128), BF16), shape((8, 128), F32)],
        (core,),
        (inside, outside, delta),
        (conv_weight,),
        after=(part,),
        scratch=[pltpu.VMEM((3456, 256), BF16), pltpu.VMEM((3, 256, 256), BF16), dma],
        flops=2 * 256 * 3456 * 256,
    )
    update = call(last_body, shape((54, 256), F32), arrays=(exchange(part, "y"),), after=(token,))
    return (data.reshape(1, 1, 16, 16, 128), update)


def solution(mesh):
    fine = Mesh(mesh.devices.reshape(SIZES), AXES)
    both = P(SAMPLE, SPACE, None, None, None)
    return jax.shard_map(
        per_device,
        mesh=fine,
        in_specs=(both, P(), P(), both, P(SAMPLE, None, SPACE), P(), P(), P(SPACE), P()),
        out_specs=(both, P(SPACE, None)),
        check_vma=False,
    )
```

```python
import jax
import jax.numpy as jnp
from jax import lax
from jax.experimental import pallas as pl
from jax.experimental.pallas import tpu as pltpu
from jax.sharding import Mesh
from jax.sharding import PartitionSpec as P

DAMPING = 0.001
CELLS = 131072
BF16 = jnp.bfloat16
F32 = jnp.float32
VMEM = pl.BlockSpec(memory_space=pltpu.VMEM)
SMEM = pl.BlockSpec(memory_space=pltpu.SMEM)
LIMIT = 48 * 1024 * 1024
ANY = pl.BlockSpec(memory_space=pl.ANY)
AXES = ("y", "zh", "zg", "zl", "x", "c")
SIZES = (4, 2, 2, 4, 4, 2)
SAMPLE = ("y", "zh")
XC = ("x", "c")
YXC = ("y", "x", "c")
SPACE = ("zg", "zl", "x", "c")


def call(body, out_shape, scalars=(), arrays=(), remote=(), after=(), scratch=(), flops=0, limit=LIMIT):
    many = isinstance(out_shape, (list, tuple))
    inputs = (*scalars, *arrays, *remote, *after)
    kept = len(inputs) - len(after)

    def kernel(*refs):
        body(*refs[:kept], *refs[len(inputs) :])

    return pl.pallas_call(
        kernel,
        out_shape=out_shape,
        in_specs=[SMEM] * len(scalars) + [VMEM] * len(arrays) + [ANY] * (len(remote) + len(after)),
        out_specs=[VMEM] * len(out_shape) if many else VMEM,
        scratch_shapes=list(scratch),
        compiler_params=pltpu.CompilerParams(vmem_limit_bytes=limit),
        cost_estimate=pl.CostEstimate(
            flops=flops,
            bytes_accessed=sum(a.size * a.dtype.itemsize for a in inputs),
            transcendentals=0,
        ),
    )(*inputs)


def shape(dims, dtype):
    return jax.ShapeDtypeStruct(dims, dtype)


def iota(dims, axis):
    return lax.broadcasted_iota(jnp.int32, dims, axis)


def exchange(x, axes):
    return lax.all_to_all(x, axes, 0, 0)


def started(copies):
    for copy in copies:
        copy.start()
    return copies


def x_shifted(rows, step):
    if step == 0:
        return rows
    x = iota(rows.shape, 0) & 15
    inside = (x + step >= 0) & (x + step < 16)
    return jnp.where(inside, pltpu.roll(rows, (-step) % 256, 0), 0.0)


def basis_body(panel, eigen_any, out_ref, eigen, sem):
    copy = pltpu.make_async_copy(eigen_any, eigen, sem)
    copy.start()
    copy.wait()
    row = iota((54, 54), 0)
    column = jnp.sum(jnp.where(row == iota((54, 54), 1), eigen[...], 0.0), axis=1, keepdims=True)
    column = jnp.concatenate([column, jnp.ones((10, 1), F32)], axis=0)
    first = column.astype(BF16).astype(F32)
    second = (column - first).astype(BF16).astype(F32)
    third = column - first - second
    for r in range(4):
        pick = iota((432, 128), 0) == 4 * iota((432, 128), 1) + r
        block = jnp.dot(panel[...], jnp.where(pick, 1.0, 0.0).astype(BF16), preferred_element_type=F32)
        block = jnp.concatenate([block, jnp.zeros((10, 128), F32)], axis=0)
        at = iota((64, 128), 1)
        block = jnp.where(at == 108, first, block)
        block = jnp.where(at == 109, second, block)
        block = jnp.where(at == 110, third, block)
        out_ref[r] = block.astype(BF16)


def by_side(inside_ref, outside_ref, planes):
    second = lax.axis_index("c")
    planes[2 - 2 * second] = inside_ref[...]
    planes[2 * second] = outside_ref[...]


def forward_body(
    inside_ref, outside_ref, mine, weight, bias, cot, basis_ref,
    delta_ref, send_ref, even_ref, odd_ref, patches, planes,
):
    y = lax.axis_index("y")
    for k, ref in ((0, even_ref), (2, odd_ref)):
        ref[0] = basis_ref[y ^ k]
        ref[1] = basis_ref[y ^ k ^ 1]
    by_side(inside_ref, outside_ref, planes)
    planes[1] = mine[...]
    none = jnp.zeros((16, 128), BF16)
    for a in range(3):
        wide = planes[a].astype(F32)
        for c in range(3):
            moved = x_shifted(wide, c - 1).astype(BF16)
            for b in range(3):
                at = (9 * a + 3 * b + c) * 128
                if b == 0:
                    shifted = jnp.concatenate([none, moved[:240]], axis=0)
                elif b == 2:
                    shifted = jnp.concatenate([moved[16:], none], axis=0)
                else:
                    shifted = moved
                patches[:, at : at + 128] = shifted
    pre = jnp.dot(patches[...], weight[...], preferred_element_type=F32) + bias[...]
    logistic = 1.0 / (1.0 + jnp.exp(-pre))
    delta = (cot[...].astype(F32) * logistic * (1.0 + pre * (1.0 - logistic))).astype(BF16)
    delta_ref[...] = delta
    act_t = mine[...].astype(F32).T.astype(BF16)
    rim_t = planes[2 * (lax.axis_index("x") >> 1)].astype(F32).T.astype(BF16)
    for x in range(4):
        for c in range(2):
            to = 2 * x + c
            for half in range(2):
                lanes = slice(128 * half, 128 * half + 128)
                rows = slice(32 * x, 32 * x + 32)
                send_ref[to, 32 * half : 32 * half + 32] = act_t[rows, lanes]
                send_ref[to, 64 + 32 * half : 96 + 32 * half] = rim_t[rows, lanes]
            send_ref[to, 128:] = delta[:, 128 * c : 128 * c + 128]


def weight_grad_body(got_ref, out_ref, moved, deltas, whole):
    pieces = []
    for plane, at in [(0, 64)] + [(e, 0) for e in range(8)] + [(7, 64)]:
        pieces.append(got_ref[plane, at : at + 32].astype(F32))
        pieces.append(got_ref[plane, at + 32 : at + 64].astype(F32))
    acts = jnp.concatenate(pieces, axis=1)
    lane = iota((32, 2560), 1)
    x = lane & 15
    y = (lane >> 4) & 15
    for b in range(3):
        for c in range(3):
            step = 16 * (b - 1) + (c - 1)
            turned = pltpu.roll(acts, (-step) % 2560, 1) if step else acts
            inside = (x + c >= 1) & (x + c < 17) & (y + b >= 1) & (y + b < 17)
            moved[32 * (3 * b + c) : 32 * (3 * b + c) + 32, :] = jnp.where(inside, turned, 0.0).astype(BF16)
    for e in range(8):
        deltas[256 * e : 256 * e + 256, :] = got_ref[e, 128:]
    for a in range(3):
        whole[288 * a : 288 * a + 288, :] = jnp.dot(
            moved[:, 256 * a : 256 * a + 2048], deltas[...], preferred_element_type=F32
        )
    none = jnp.zeros((5, 128), F32)
    for y_to in range(4):
        for z_to in range(4):
            parts = []
            for e in range(2):
                parts.append(whole[pl.ds(8 * y_to + 4 * e + z_to, 27, stride=32), :])
                parts.append(none)
            out_ref[4 * y_to + z_to] = jnp.concatenate(parts, axis=0).astype(BF16)


def pair_body(even_ref, odd_ref, out_ref):
    out_ref[0] = even_ref[1]
    out_ref[1] = odd_ref[1]


def over_y_zl_body(got_ref, even_ref, odd_ref, pair_ref, out_ref, slices, rows):
    total = sum(got_ref[i].astype(F32) for i in range(16)) * (1.0 / CELLS)
    zl = lax.axis_index("zl")
    for k, block in ((0, even_ref[0]), (2, odd_ref[0]), (1, pair_ref[0]), (3, pair_ref[1])):
        slices[zl ^ k] = block
    rows[:27, :] = total[:27]
    rows[27:54, :] = total[32:59]
    for y in range(4):
        rows[54 + 54 * y : 108 + 54 * y, :] = slices[y].astype(F32)[:54]
    rows[270:, :] = jnp.zeros((2, 128), F32)
    for to in range(4):
        out_ref[to] = rows[...].astype(BF16)


def over_zh_zg_body(owner_ref, got_ref, out_ref, basis_ref, here_ref, next_ref, rows, slices):
    for i in range(4):
        rows[i, :272, :] = got_ref[i].astype(F32)
        rows[i, 272:, :] = jnp.zeros((8, 128), F32)
        for y in range(4):
            slices[i, y] = rows[i, 54 + 54 * y : 118 + 54 * y, :].astype(BF16)
    total = (rows[0, :54, :] + rows[1, :54, :]) + (rows[2, :54, :] + rows[3, :54, :])
    none = jnp.zeros((5, 128), F32)
    total = jnp.concatenate([total[:27], none, total[27:], none], axis=0).astype(BF16)
    for to in range(32):
        out_ref[to] = total
    for j in range(8):
        for zg in range(2):
            basis_ref[j, 64 * zg : 64 * zg + 64] = slices[2 * (owner_ref[j] & 1) + zg, owner_ref[j] >> 1]
    zg, zl = lax.axis_index("zg"), lax.axis_index("zl")
    for k, ref in ((0, here_ref), (2, next_ref)):
        ref[0] = basis_ref[4 * zg + (zl ^ k)]
        ref[1] = basis_ref[4 * zg + (zl ^ k ^ 1)]


def rotate_body(got_ref, basis_ref, here_ref, next_ref, out_ref, pair_ref, grads, ordered):
    pair_ref[0] = here_ref[1]
    pair_ref[1] = next_ref[1]
    for y in range(4):
        for x in range(4):
            at = 32 * (8 * x + 2 * y)
            for c in range(2):
                grads[c, at : at + 64, :] = got_ref[8 * y + 2 * x + c].astype(F32)
    for tap in range(27):
        for c in range(2):
            ordered[32 * tap : 32 * tap + 32, 128 * c : 128 * c + 128] = grads[c, pl.ds(tap, 32, stride=32), :]
    ordered[864:, :] = jnp.zeros((32, 256), F32)
    inside = iota((128, 128), 1) < 108
    total = jnp.zeros((128, 256), F32)
    for j in range(8):
        block = jnp.where(inside, basis_ref[j].astype(F32), 0.0).astype(BF16)
        rows = ordered[108 * j : 108 * j + 128, :].astype(BF16)
        total = total + jnp.dot(block, rows, preferred_element_type=F32)
    total = jnp.concatenate(
        [total[64 * zg : 64 * zg + 56, 128 * c : 128 * c + 128] for zg in range(2) for c in range(2)], axis=0
    ).astype(BF16)
    for to in range(4):
        out_ref[to] = total


def update_body(
    got_ref, here_ref, next_ref, pair_ref, out_basis_any, out_eigen_any,
    out_ref, panel, out_basis, out_eigen, ordered, sems,
):
    zl = lax.axis_index("zl")
    for k, block in ((0, here_ref[0]), (2, next_ref[0]), (1, pair_ref[0]), (3, pair_ref[1])):
        panel[zl ^ k] = block
    copies = [
        pltpu.make_async_copy(out_basis_any, out_basis, sems.at[0]),
        pltpu.make_async_copy(out_eigen_any, out_eigen, sems.at[1]),
    ]
    started(copies)
    highest = lax.Precision.HIGHEST
    total = sum(got_ref[i].astype(F32) for i in range(4))
    none = jnp.zeros((8, 256), F32)
    parts = []
    for zg in range(2):
        at = 112 * zg
        parts.append(jnp.concatenate([total[at : at + 56], total[at + 56 : at + 112]], axis=1))
        parts.append(none)
    rotated = jnp.concatenate(parts, axis=0)
    for copy in copies:
        copy.wait()
    rotated = jnp.dot(rotated, out_basis[...], precision=highest, preferred_element_type=F32)
    terms = here_ref[0].astype(F32)
    eigen = (terms[:, 108:109] + terms[:, 109:110]) + terms[:, 110:111]
    scaled = rotated / (eigen * out_eigen[...] + DAMPING)
    scaled = jnp.where((iota((128, 256), 0) & 63) < 54, scaled, 0.0)
    turned = lax.dot_general(
        scaled, out_basis[...], (((1,), (1,)), ((), ())), precision=highest, preferred_element_type=F32
    )
    high = turned.astype(BF16)
    rest = (turned - high.astype(F32)).astype(BF16)
    for r in range(4):
        block = panel[r].astype(F32).T.astype(BF16)
        rows = jnp.dot(block, high, preferred_element_type=F32) + jnp.dot(block, rest, preferred_element_type=F32)
        for c in range(2):
            ordered[c, pl.ds(r, 108, stride=4), :] = rows[:108, 128 * c : 128 * c + 128]
    for c in range(2):
        ordered[c, 432:, :] = jnp.zeros((8, 128), F32)
    for to in range(8):
        rows = [ordered[c, 54 * to : 54 * to + 56, :] for c in range(2)]
        out_ref[to] = jnp.concatenate(rows, axis=0).astype(BF16)


def over_xc_body(got_ref, out_ref):
    total = sum(got_ref[i].astype(F32) for i in range(8))
    for to in range(4):
        out_ref[to] = total


def last_body(got_ref, out_ref):
    total = (got_ref[0] + got_ref[1]) + (got_ref[2] + got_ref[3])
    out_ref[...] = jnp.concatenate([total[:54], total[56:110]], axis=1)


def data_grad_body(inside_ref, outside_ref, mine_ref, weight_any, out_ref, token_ref, weight, planes, sem):
    copy = pltpu.make_async_copy(weight_any, weight, sem)
    copy.start()
    by_side(inside_ref, outside_ref, planes)
    planes[1] = mine_ref[...]
    none = jnp.zeros((16, 256), BF16)
    total = jnp.zeros((256, 128), F32)
    for a in range(3):
        wide = planes[2 - a].astype(F32)
        if a == 0:
            copy.wait()
        for c in range(3):
            moved = x_shifted(wide, 1 - c).astype(BF16)
            for b in range(3):
                if b == 2:
                    shifted = jnp.concatenate([none, moved[:240]], axis=0)
                elif b == 0:
                    shifted = jnp.concatenate([moved[16:], none], axis=0)
                else:
                    shifted = moved
                tap = 9 * a + 3 * b + c
                total = total + lax.dot_general(
                    shifted,
                    weight[128 * tap : 128 * tap + 128, :],
                    (((1,), (1,)), ((), ())),
                    preferred_element_type=F32,
                )
    out_ref[...] = total.astype(BF16)
    token_ref[...] = jnp.zeros((8, 128), F32)


def neighbours(block):
    inside = lax.ppermute(block, "c", [(0, 1), (1, 0)])
    pairs = [(i, i + 1) for i in range(1, 63, 2)]
    return inside, lax.ppermute(block, SPACE, pairs + [(j, i) for i, j in pairs])


def turned(block, k):
    pairs = [(4 * y + z, 4 * z + (y ^ k)) for y in range(4) for z in range(4)]
    return lax.ppermute(block, ("y", "zl"), pairs)


def across(block, k):
    return lax.ppermute(block, "zl", [(i, i ^ k) for i in range(4)])


def per_device(
    activations,
    conv_weight,
    conv_bias,
    cotangent,
    basis_panels,
    panel_owner,
    output_basis,
    input_eigen,
    output_eigen,
):
    dma = pltpu.SemaphoreType.DMA
    plane = activations.reshape(256, 128)
    inside, outside = neighbours(plane)

    stored = call(
        basis_body,
        shape((4, 64, 128), BF16),
        arrays=(basis_panels[0].T,),
        remote=(input_eigen.reshape(1, 54),),
        scratch=[pltpu.VMEM((1, 54), F32), dma],
        flops=4_000_000_000,
    )
    delta, send, even, odd = call(
        forward_body,
        [shape((256, 256), BF16), shape((8, 384, 128), BF16)] + [shape((2, 64, 128), BF16)] * 2,
        (),
        (inside, outside, plane, conv_weight, conv_bias.reshape(1, 256), cotangent.reshape(256, 256), stored),
        scratch=[pltpu.VMEM((256, 3456), BF16), pltpu.VMEM((3, 256, 128), BF16)],
        flops=2 * 256 * 3456 * 256,
    )
    even, odd = turned(even, 0), turned(odd, 2)
    part = call(
        weight_grad_body,
        shape((16, 64, 128), BF16),
        arrays=(exchange(send, XC),),
        after=(even,),
        scratch=[pltpu.VMEM((288, 2560), BF16), pltpu.VMEM((2048, 128), BF16), pltpu.VMEM((864, 128), F32)],
        flops=2 * 864 * 2048 * 128,
    )
    pair = call(pair_body, shape((2, 64, 128), BF16), arrays=(even, odd), after=(part,))
    part = call(
        over_y_zl_body,
        shape((4, 272, 128), BF16),
        arrays=(exchange(part, ("y", "zl")), even, odd, across(pair, 1)),
        scratch=[pltpu.VMEM((4, 64, 128), BF16), pltpu.VMEM((272, 128), F32)],
    )
    inside, outside = neighbours(delta)
    part, basis, here, there = call(
        over_zh_zg_body,
        [shape((32, 64, 128), BF16), shape((8, 128, 128), BF16)] + [shape((2, 128, 128), BF16)] * 2,
        (panel_owner,),
        (exchange(part, ("zh", "zg")),),
        after=(inside, outside),
        scratch=[pltpu.VMEM((4, 280, 128), F32), pltpu.VMEM((4, 4, 64, 128), BF16)],
    )
    there = across(there, 2)
    rotated, pair = call(
        rotate_body,
        [shape((4, 224, 128), BF16), shape((2, 128, 128), BF16)],
        arrays=(exchange(part, YXC), basis, here, there),
        scratch=[pltpu.VMEM((2, 1024, 128), F32), pltpu.VMEM((896, 256), F32)],
    )
    part = call(
        update_body,
        shape((8, 112, 128), BF16),
        (),
        (exchange(rotated, "zl"), here, there, across(pair, 1)),
        (output_basis, output_eigen.reshape(1, 256)),
        scratch=[
            pltpu.VMEM((4, 128, 128), BF16),
            pltpu.VMEM((256, 256), F32),
            pltpu.VMEM((1, 256), F32),
            pltpu.VMEM((2, 440, 128), F32),
            dma((2,)),
        ],
    )
    part = call(over_xc_body, shape((4, 112, 128), F32), arrays=(exchange(part, XC),))
    data, token = call(
        data_grad_body,
        [shape((256, 128), BF16), shape((8, 128), F32)],
        (),
        (inside, outside, delta),
        (conv_weight,),
        after=(part,),
        scratch=[pltpu.VMEM((3456, 256), BF16), pltpu.VMEM((3, 256, 256), BF16), dma],
        flops=2 * 256 * 3456 * 256,
    )
    update = call(last_body, shape((54, 256), F32), arrays=(exchange(part, "y"),), after=(token,))
    return (data.reshape(1, 1, 16, 16, 128), update)


def solution(mesh):
    fine = Mesh(mesh.devices.reshape(SIZES), AXES)
    both = P(SAMPLE, SPACE, None, None, None)
    return jax.shard_map(
        per_device,
        mesh=fine,
        in_specs=(both, P(), P(), both, P(SAMPLE, None, SPACE), P(), P(), P(SPACE), P()),
        out_specs=(both, P(SPACE, None)),
        check_vma=False,
    )
```

```python
import jax
import jax.numpy as jnp
from jax import lax
from jax.experimental import pallas as pl
from jax.experimental.pallas import tpu as pltpu
from jax.sharding import Mesh
from jax.sharding import PartitionSpec as P

DAMPING = 0.001
CELLS = 131072
BF16 = jnp.bfloat16
F32 = jnp.float32
VMEM = pl.BlockSpec(memory_space=pltpu.VMEM)
SMEM = pl.BlockSpec(memory_space=pltpu.SMEM)
LIMIT = 48 * 1024 * 1024
ANY = pl.BlockSpec(memory_space=pl.ANY)
AXES = ("y", "zh", "zg", "zl", "x", "c")
SIZES = (4, 2, 2, 4, 4, 2)
SAMPLE = ("y", "zh")
XC = ("x", "c")
YXC = ("y", "x", "c")
SPACE = ("zg", "zl", "x", "c")


def call(body, out_shape, scalars=(), arrays=(), remote=(), after=(), scratch=(), flops=0, limit=LIMIT):
    many = isinstance(out_shape, (list, tuple))
    inputs = (*scalars, *arrays, *remote, *after)
    kept = len(inputs) - len(after)

    def kernel(*refs):
        body(*refs[:kept], *refs[len(inputs) :])

    return pl.pallas_call(
        kernel,
        out_shape=out_shape,
        in_specs=[SMEM] * len(scalars) + [VMEM] * len(arrays) + [ANY] * (len(remote) + len(after)),
        out_specs=[VMEM] * len(out_shape) if many else VMEM,
        scratch_shapes=list(scratch),
        compiler_params=pltpu.CompilerParams(vmem_limit_bytes=limit),
        cost_estimate=pl.CostEstimate(
            flops=flops,
            bytes_accessed=sum(a.size * a.dtype.itemsize for a in inputs),
            transcendentals=0,
        ),
    )(*inputs)


def shape(dims, dtype):
    return jax.ShapeDtypeStruct(dims, dtype)


def iota(dims, axis):
    return lax.broadcasted_iota(jnp.int32, dims, axis)


def exchange(x, axes):
    return lax.all_to_all(x, axes, 0, 0)


def started(copies):
    for copy in copies:
        copy.start()
    return copies


def x_shifted(rows, step):
    if step == 0:
        return rows
    x = iota(rows.shape, 0) & 15
    inside = (x + step >= 0) & (x + step < 16)
    return jnp.where(inside, pltpu.roll(rows, (-step) % 256, 0), 0.0)


def basis_body(panel, eigen_any, out_ref, eigen, sem):
    copy = pltpu.make_async_copy(eigen_any, eigen, sem)
    copy.start()
    copy.wait()
    row = iota((54, 54), 0)
    column = jnp.sum(jnp.where(row == iota((54, 54), 1), eigen[...], 0.0), axis=1, keepdims=True)
    column = jnp.concatenate([column, jnp.ones((10, 1), F32)], axis=0)
    first = column.astype(BF16).astype(F32)
    second = (column - first).astype(BF16).astype(F32)
    third = column - first - second
    for r in range(4):
        pick = iota((432, 128), 0) == 4 * iota((432, 128), 1) + r
        block = jnp.dot(panel[...], jnp.where(pick, 1.0, 0.0).astype(BF16), preferred_element_type=F32)
        block = jnp.concatenate([block, jnp.zeros((10, 128), F32)], axis=0)
        at = iota((64, 128), 1)
        block = jnp.where(at == 108, first, block)
        block = jnp.where(at == 109, second, block)
        block = jnp.where(at == 110, third, block)
        out_ref[r] = block.astype(BF16)


def by_side(inside_ref, outside_ref, planes):
    second = lax.axis_index("c")
    planes[2 - 2 * second] = inside_ref[...]
    planes[2 * second] = outside_ref[...]


def first_body(out_ref):
    out_ref[...] = jnp.zeros((8, 128), F32)


def forward_body(
    inside_ref, outside_ref, mine, weight, bias, cot, basis_ref,
    delta_ref, send_ref, even_ref, odd_ref, patches, planes,
):
    y = lax.axis_index("y")
    for k, ref in ((0, even_ref), (2, odd_ref)):
        ref[0] = basis_ref[y ^ k]
        ref[1] = basis_ref[y ^ k ^ 1]
    by_side(inside_ref, outside_ref, planes)
    planes[1] = mine[...]
    none = jnp.zeros((16, 128), BF16)
    for a in range(3):
        wide = planes[a].astype(F32)
        for c in range(3):
            moved = x_shifted(wide, c - 1).astype(BF16)
            for b in range(3):
                at = (9 * a + 3 * b + c) * 128
                if b == 0:
                    shifted = jnp.concatenate([none, moved[:240]], axis=0)
                elif b == 2:
                    shifted = jnp.concatenate([moved[16:], none], axis=0)
                else:
                    shifted = moved
                patches[:, at : at + 128] = shifted
    pre = jnp.dot(patches[...], weight[...], preferred_element_type=F32) + bias[...]
    logistic = 1.0 / (1.0 + jnp.exp(-pre))
    delta = (cot[...].astype(F32) * logistic * (1.0 + pre * (1.0 - logistic))).astype(BF16)
    delta_ref[...] = delta
    act_t = mine[...].astype(F32).T.astype(BF16)
    rim_t = planes[2 * (lax.axis_index("x") >> 1)].astype(F32).T.astype(BF16)
    for x in range(4):
        for c in range(2):
            to = 2 * x + c
            for half in range(2):
                lanes = slice(128 * half, 128 * half + 128)
                rows = slice(32 * x, 32 * x + 32)
                send_ref[to, 32 * half : 32 * half + 32] = act_t[rows, lanes]
                send_ref[to, 64 + 32 * half : 96 + 32 * half] = rim_t[rows, lanes]
            send_ref[to, 128:] = delta[:, 128 * c : 128 * c + 128]


def weight_grad_body(got_ref, even_ref, odd_ref, out_ref, pair_ref, moved, deltas, whole):
    pieces = []
    for plane, at in [(0, 64)] + [(e, 0) for e in range(8)] + [(7, 64)]:
        pieces.append(got_ref[plane, at : at + 32].astype(F32))
        pieces.append(got_ref[plane, at + 32 : at + 64].astype(F32))
    acts = jnp.concatenate(pieces, axis=1)
    lane = iota((32, 2560), 1)
    x = lane & 15
    y = (lane >> 4) & 15
    for b in range(3):
        for c in range(3):
            step = 16 * (b - 1) + (c - 1)
            turned = pltpu.roll(acts, (-step) % 2560, 1) if step else acts
            inside = (x + c >= 1) & (x + c < 17) & (y + b >= 1) & (y + b < 17)
            moved[32 * (3 * b + c) : 32 * (3 * b + c) + 32, :] = jnp.where(inside, turned, 0.0).astype(BF16)
    for e in range(8):
        deltas[256 * e : 256 * e + 256, :] = got_ref[e, 128:]
    for a in range(3):
        whole[288 * a : 288 * a + 288, :] = jnp.dot(
            moved[:, 256 * a : 256 * a + 2048], deltas[...], preferred_element_type=F32
        )
    pair_ref[0] = even_ref[1]
    pair_ref[1] = odd_ref[1]
    none = jnp.zeros((1, 128), F32)
    for y_to in range(4):
        for z_to in range(4):
            parts = []
            for e in range(2):
                parts.append(whole[pl.ds(8 * y_to + 4 * e + z_to, 27, stride=32), :])
                parts.append(none)
            out_ref[4 * y_to + z_to] = jnp.concatenate(parts, axis=0).astype(BF16)


def over_y_zl_body(got_ref, even_ref, odd_ref, pair_ref, out_ref, slices, rows):
    total = sum(got_ref[i].astype(F32) for i in range(16)) * (1.0 / CELLS)
    zl = lax.axis_index("zl")
    for k, block in ((0, even_ref[0]), (2, odd_ref[0]), (1, pair_ref[0]), (3, pair_ref[1])):
        slices[zl ^ k] = block
    rows[:27, :] = total[:27]
    rows[27:54, :] = total[28:55]
    for y in range(4):
        rows[54 + 54 * y : 108 + 54 * y, :] = slices[y].astype(F32)[:54]
    rows[270:, :] = jnp.zeros((2, 128), F32)
    for to in range(4):
        out_ref[to] = rows[...].astype(BF16)


def over_zh_zg_body(owner_ref, got_ref, out_ref, basis_ref, here_ref, next_ref, rows, slices):
    for i in range(4):
        rows[i, :272, :] = got_ref[i].astype(F32)
        rows[i, 272:, :] = jnp.zeros((8, 128), F32)
        for y in range(4):
            slices[i, y] = rows[i, 54 + 54 * y : 118 + 54 * y, :].astype(BF16)
    total = (rows[0, :54, :] + rows[1, :54, :]) + (rows[2, :54, :] + rows[3, :54, :])
    none = jnp.zeros((1, 128), F32)
    total = jnp.concatenate([total[:27], none, total[27:], none], axis=0).astype(BF16)
    for to in range(32):
        out_ref[to] = total
    for j in range(8):
        for zg in range(2):
            basis_ref[j, 64 * zg : 64 * zg + 64] = slices[2 * (owner_ref[j] & 1) + zg, owner_ref[j] >> 1]
    zg, zl = lax.axis_index("zg"), lax.axis_index("zl")
    for k, ref in ((0, here_ref), (2, next_ref)):
        ref[0] = basis_ref[4 * zg + (zl ^ k)]
        ref[1] = basis_ref[4 * zg + (zl ^ k ^ 1)]


def rotate_body(got_ref, basis_ref, here_ref, next_ref, out_ref, pair_ref, grads, ordered):
    pair_ref[0] = here_ref[1]
    pair_ref[1] = next_ref[1]
    for y in range(4):
        for x in range(4):
            at = 28 * (8 * x + 2 * y)
            for c in range(2):
                grads[c, at : at + 56, :] = got_ref[8 * y + 2 * x + c].astype(F32)
    for tap in range(27):
        for c in range(2):
            ordered[32 * tap : 32 * tap + 32, 128 * c : 128 * c + 128] = grads[c, pl.ds(tap, 32, stride=28), :]
    ordered[864:, :] = jnp.zeros((32, 256), F32)
    inside = iota((128, 128), 1) < 108
    total = jnp.zeros((128, 256), F32)
    for j in range(8):
        block = jnp.where(inside, basis_ref[j].astype(F32), 0.0).astype(BF16)
        rows = ordered[108 * j : 108 * j + 128, :].astype(BF16)
        total = total + jnp.dot(block, rows, preferred_element_type=F32)
    total = jnp.concatenate(
        [total[64 * zg : 64 * zg + 56, 128 * c : 128 * c + 128] for zg in range(2) for c in range(2)], axis=0
    ).astype(BF16)
    for to in range(4):
        out_ref[to] = total


def update_body(
    got_ref, here_ref, next_ref, pair_ref, out_basis_any, out_eigen_any,
    out_ref, panel, out_basis, out_eigen, ordered, sems,
):
    zl = lax.axis_index("zl")
    for k, block in ((0, here_ref[0]), (2, next_ref[0]), (1, pair_ref[0]), (3, pair_ref[1])):
        panel[zl ^ k] = block
    copies = [
        pltpu.make_async_copy(out_basis_any, out_basis, sems.at[0]),
        pltpu.make_async_copy(out_eigen_any, out_eigen, sems.at[1]),
    ]
    started(copies)
    highest = lax.Precision.HIGHEST
    total = sum(got_ref[i].astype(F32) for i in range(4))
    none = jnp.zeros((8, 256), F32)
    parts = []
    for zg in range(2):
        at = 112 * zg
        parts.append(jnp.concatenate([total[at : at + 56], total[at + 56 : at + 112]], axis=1))
        parts.append(none)
    rotated = jnp.concatenate(parts, axis=0)
    for copy in copies:
        copy.wait()
    rotated = jnp.dot(rotated, out_basis[...], precision=highest, preferred_element_type=F32)
    terms = here_ref[0].astype(F32)
    eigen = (terms[:, 108:109] + terms[:, 109:110]) + terms[:, 110:111]
    scaled = rotated / (eigen * out_eigen[...] + DAMPING)
    scaled = jnp.where((iota((128, 256), 0) & 63) < 54, scaled, 0.0)
    turned = lax.dot_general(
        scaled, out_basis[...], (((1,), (1,)), ((), ())), precision=highest, preferred_element_type=F32
    )
    high = turned.astype(BF16)
    rest = (turned - high.astype(F32)).astype(BF16)
    for r in range(4):
        block = panel[r].astype(F32).T.astype(BF16)
        rows = jnp.dot(block, high, preferred_element_type=F32) + jnp.dot(block, rest, preferred_element_type=F32)
        for c in range(2):
            ordered[c, pl.ds(r, 108, stride=4), :] = rows[:108, 128 * c : 128 * c + 128]
    for c in range(2):
        ordered[c, 432:, :] = jnp.zeros((8, 128), F32)
    for to in range(8):
        rows = [ordered[c, 54 * to : 54 * to + 56, :] for c in range(2)]
        out_ref[to] = jnp.concatenate(rows, axis=0).astype(BF16)


def over_xc_body(got_ref, out_ref):
    total = sum(got_ref[i].astype(F32) for i in range(8))
    for to in range(4):
        out_ref[to] = total


def last_body(got_ref, out_ref):
    total = (got_ref[0] + got_ref[1]) + (got_ref[2] + got_ref[3])
    out_ref[...] = jnp.concatenate([total[:54], total[56:110]], axis=1)


def data_grad_body(inside_ref, outside_ref, mine_ref, weight_any, out_ref, token_ref, weight, planes, sem):
    copy = pltpu.make_async_copy(weight_any, weight, sem)
    copy.start()
    by_side(inside_ref, outside_ref, planes)
    planes[1] = mine_ref[...]
    none = jnp.zeros((16, 256), BF16)
    total = jnp.zeros((256, 128), F32)
    for a in range(3):
        wide = planes[2 - a].astype(F32)
        if a == 0:
            copy.wait()
        for c in range(3):
            moved = x_shifted(wide, 1 - c).astype(BF16)
            for b in range(3):
                if b == 2:
                    shifted = jnp.concatenate([none, moved[:240]], axis=0)
                elif b == 0:
                    shifted = jnp.concatenate([moved[16:], none], axis=0)
                else:
                    shifted = moved
                tap = 9 * a + 3 * b + c
                total = total + lax.dot_general(
                    shifted,
                    weight[128 * tap : 128 * tap + 128, :],
                    (((1,), (1,)), ((), ())),
                    preferred_element_type=F32,
                )
    out_ref[...] = total.astype(BF16)
    token_ref[...] = jnp.zeros((8, 128), F32)


def neighbours(block):
    inside = lax.ppermute(block, "c", [(0, 1), (1, 0)])
    pairs = [(i, i + 1) for i in range(1, 63, 2)]
    return inside, lax.ppermute(block, SPACE, pairs + [(j, i) for i, j in pairs])


def turned(block, k):
    pairs = [(4 * y + z, 4 * z + (y ^ k)) for y in range(4) for z in range(4)]
    return lax.ppermute(block, ("y", "zl"), pairs)


def across(block, k):
    return lax.ppermute(block, "zl", [(i, i ^ k) for i in range(4)])


def per_device(
    activations,
    conv_weight,
    conv_bias,
    cotangent,
    basis_panels,
    panel_owner,
    output_basis,
    input_eigen,
    output_eigen,
):
    dma = pltpu.SemaphoreType.DMA
    plane = activations.reshape(256, 128)
    inside, outside = neighbours(plane)

    first = call(first_body, shape((8, 128), F32), flops=4_000_000_000)
    stored = call(
        basis_body,
        shape((4, 64, 128), BF16),
        arrays=(basis_panels[0].T,),
        remote=(input_eigen.reshape(1, 54),),
        after=(first,),
        scratch=[pltpu.VMEM((1, 54), F32), dma],
    )
    delta, send, even, odd = call(
        forward_body,
        [shape((256, 256), BF16), shape((8, 384, 128), BF16)] + [shape((2, 64, 128), BF16)] * 2,
        (),
        (inside, outside, plane, conv_weight, conv_bias.reshape(1, 256), cotangent.reshape(256, 256), stored),
        scratch=[pltpu.VMEM((256, 3456), BF16), pltpu.VMEM((3, 256, 128), BF16)],
        flops=2 * 256 * 3456 * 256,
    )
    even, odd = turned(even, 0), turned(odd, 2)
    part, pair = call(
        weight_grad_body,
        [shape((16, 56, 128), BF16), shape((2, 64, 128), BF16)],
        arrays=(exchange(send, XC), even, odd),
        scratch=[pltpu.VMEM((288, 2560), BF16), pltpu.VMEM((2048, 128), BF16), pltpu.VMEM((864, 128), F32)],
        flops=2 * 864 * 2048 * 128,
    )
    part = call(
        over_y_zl_body,
        shape((4, 272, 128), BF16),
        arrays=(exchange(part, ("y", "zl")), even, odd, across(pair, 1)),
        scratch=[pltpu.VMEM((4, 64, 128), BF16), pltpu.VMEM((272, 128), F32)],
    )
    inside, outside = neighbours(delta)
    part, basis, here, there = call(
        over_zh_zg_body,
        [shape((32, 56, 128), BF16), shape((8, 128, 128), BF16)] + [shape((2, 128, 128), BF16)] * 2,
        (panel_owner,),
        (exchange(part, ("zh", "zg")),),
        after=(inside, outside),
        scratch=[pltpu.VMEM((4, 280, 128), F32), pltpu.VMEM((4, 4, 64, 128), BF16)],
    )
    there = across(there, 2)
    rotated, pair = call(
        rotate_body,
        [shape((4, 224, 128), BF16), shape((2, 128, 128), BF16)],
        arrays=(exchange(part, YXC), basis, here, there),
        scratch=[pltpu.VMEM((2, 896, 128), F32), pltpu.VMEM((896, 256), F32)],
    )
    part = call(
        update_body,
        shape((8, 112, 128), BF16),
        (),
        (exchange(rotated, "zl"), here, there, across(pair, 1)),
        (output_basis, output_eigen.reshape(1, 256)),
        scratch=[
            pltpu.VMEM((4, 128, 128), BF16),
            pltpu.VMEM((256, 256), F32),
            pltpu.VMEM((1, 256), F32),
            pltpu.VMEM((2, 440, 128), F32),
            dma((2,)),
        ],
    )
    part = call(over_xc_body, shape((4, 112, 128), F32), arrays=(exchange(part, XC),))
    data, token = call(
        data_grad_body,
        [shape((256, 128), BF16), shape((8, 128), F32)],
        (),
        (inside, outside, delta),
        (conv_weight,),
        after=(part,),
        scratch=[pltpu.VMEM((3456, 256), BF16), pltpu.VMEM((3, 256, 256), BF16), dma],
        flops=2 * 256 * 3456 * 256,
    )
    update = call(last_body, shape((54, 256), F32), arrays=(exchange(part, "y"),), after=(token,))
    return (data.reshape(1, 1, 16, 16, 128), update)


def solution(mesh):
    fine = Mesh(mesh.devices.reshape(SIZES), AXES)
    both = P(SAMPLE, SPACE, None, None, None)
    return jax.shard_map(
        per_device,
        mesh=fine,
        in_specs=(both, P(), P(), both, P(SAMPLE, None, SPACE), P(), P(), P(SPACE), P()),
        out_specs=(both, P(SPACE, None)),
        check_vma=False,
    )
```

```python
import jax
import jax.numpy as jnp
from jax import lax
from jax.experimental import pallas as pl
from jax.experimental.pallas import tpu as pltpu
from jax.sharding import Mesh
from jax.sharding import PartitionSpec as P

DAMPING = 0.001
CELLS = 131072
BF16 = jnp.bfloat16
F32 = jnp.float32
VMEM = pl.BlockSpec(memory_space=pltpu.VMEM)
SMEM = pl.BlockSpec(memory_space=pltpu.SMEM)
LIMIT = 48 * 1024 * 1024
ANY = pl.BlockSpec(memory_space=pl.ANY)
AXES = ("y", "zh", "zg", "zl", "x", "c")
SIZES = (4, 2, 2, 4, 4, 2)
SAMPLE = ("y", "zh")
XC = ("x", "c")
YXC = ("y", "x", "c")
SPACE = ("zg", "zl", "x", "c")


def call(body, out_shape, scalars=(), arrays=(), remote=(), after=(), scratch=(), flops=0, limit=LIMIT):
    many = isinstance(out_shape, (list, tuple))
    inputs = (*scalars, *arrays, *remote, *after)
    kept = len(inputs) - len(after)

    def kernel(*refs):
        body(*refs[:kept], *refs[len(inputs) :])

    return pl.pallas_call(
        kernel,
        out_shape=out_shape,
        in_specs=[SMEM] * len(scalars) + [VMEM] * len(arrays) + [ANY] * (len(remote) + len(after)),
        out_specs=[VMEM] * len(out_shape) if many else VMEM,
        scratch_shapes=list(scratch),
        compiler_params=pltpu.CompilerParams(vmem_limit_bytes=limit),
        cost_estimate=pl.CostEstimate(
            flops=flops,
            bytes_accessed=sum(a.size * a.dtype.itemsize for a in inputs),
            transcendentals=0,
        ),
    )(*inputs)


def shape(dims, dtype):
    return jax.ShapeDtypeStruct(dims, dtype)


def iota(dims, axis):
    return lax.broadcasted_iota(jnp.int32, dims, axis)


def exchange(x, axes):
    return lax.all_to_all(x, axes, 0, 0)


def started(copies):
    for copy in copies:
        copy.start()
    return copies


def x_shifted(rows, step):
    if step == 0:
        return rows
    x = iota(rows.shape, 0) & 15
    inside = (x + step >= 0) & (x + step < 16)
    return jnp.where(inside, pltpu.roll(rows, (-step) % 256, 0), 0.0)


def basis_body(panel, eigen_any, out_ref, eigen, sem):
    copy = pltpu.make_async_copy(eigen_any, eigen, sem)
    copy.start()
    copy.wait()
    row = iota((54, 54), 0)
    column = jnp.sum(jnp.where(row == iota((54, 54), 1), eigen[...], 0.0), axis=1, keepdims=True)
    column = jnp.concatenate([column, jnp.ones((10, 1), F32)], axis=0)
    first = column.astype(BF16).astype(F32)
    second = (column - first).astype(BF16).astype(F32)
    third = column - first - second
    for r in range(4):
        pick = iota((432, 128), 0) == 4 * iota((432, 128), 1) + r
        block = jnp.dot(panel[...], jnp.where(pick, 1.0, 0.0).astype(BF16), preferred_element_type=F32)
        block = jnp.concatenate([block, jnp.zeros((10, 128), F32)], axis=0)
        at = iota((64, 128), 1)
        block = jnp.where(at == 108, first, block)
        block = jnp.where(at == 109, second, block)
        block = jnp.where(at == 110, third, block)
        out_ref[r] = block.astype(BF16)


def by_side(inside_ref, outside_ref, planes):
    second = lax.axis_index("c")
    planes[2 - 2 * second] = inside_ref[...]
    planes[2 * second] = outside_ref[...]


def first_body(out_ref):
    out_ref[...] = jnp.zeros((8, 128), F32)


def forward_body(
    inside_ref, outside_ref, mine, weight, bias, cot, basis_ref,
    delta_ref, send_ref, even_ref, odd_ref, patches, planes,
):
    y = lax.axis_index("y")
    for k, ref in ((0, even_ref), (2, odd_ref)):
        ref[0] = basis_ref[y ^ k]
        ref[1] = basis_ref[y ^ k ^ 1]
    by_side(inside_ref, outside_ref, planes)
    planes[1] = mine[...]
    none = jnp.zeros((16, 128), BF16)
    for a in range(3):
        wide = planes[a].astype(F32)
        for c in range(3):
            moved = x_shifted(wide, c - 1).astype(BF16)
            for b in range(3):
                at = (9 * a + 3 * b + c) * 128
                if b == 0:
                    shifted = jnp.concatenate([none, moved[:240]], axis=0)
                elif b == 2:
                    shifted = jnp.concatenate([moved[16:], none], axis=0)
                else:
                    shifted = moved
                patches[:, at : at + 128] = shifted
    pre = jnp.dot(patches[...], weight[...], preferred_element_type=F32) + bias[...]
    logistic = 1.0 / (1.0 + jnp.exp(-pre))
    delta = (cot[...].astype(F32) * logistic * (1.0 + pre * (1.0 - logistic))).astype(BF16)
    delta_ref[...] = delta
    act_t = mine[...].astype(F32).T.astype(BF16)
    rim_t = planes[2 * (lax.axis_index("x") >> 1)].astype(F32).T.astype(BF16)
    for x in range(4):
        for c in range(2):
            to = 2 * x + c
            for half in range(2):
                lanes = slice(128 * half, 128 * half + 128)
                rows = slice(32 * x, 32 * x + 32)
                send_ref[to, 32 * half : 32 * half + 32] = act_t[rows, lanes]
                send_ref[to, 64 + 32 * half : 96 + 32 * half] = rim_t[rows, lanes]
            send_ref[to, 128:] = delta[:, 128 * c : 128 * c + 128]


def weight_grad_body(got_ref, even_ref, odd_ref, out_ref, pair_ref, moved, deltas, whole):
    pieces = []
    for plane, at in [(0, 64)] + [(e, 0) for e in range(8)] + [(7, 64)]:
        pieces.append(got_ref[plane, at : at + 32].astype(F32))
        pieces.append(got_ref[plane, at + 32 : at + 64].astype(F32))
    acts = jnp.concatenate(pieces, axis=1)
    lane = iota((8, 2560), 1)
    x = lane & 15
    y = (lane >> 4) & 15
    for b in range(3):
        for c in range(3):
            step = 16 * (b - 1) + (c - 1)
            turned = pltpu.roll(acts, (-step) % 2560, 1) if step else acts
            inside = (x + c >= 1) & (x + c < 17) & (y + b >= 1) & (y + b < 17)
            kept = jnp.where(inside[None], turned.reshape(4, 8, 2560), 0.0).reshape(32, 2560)
            moved[32 * (3 * b + c) : 32 * (3 * b + c) + 32, :] = kept.astype(BF16)
    for e in range(8):
        deltas[256 * e : 256 * e + 256, :] = got_ref[e, 128:]
    for a in range(3):
        whole[288 * a : 288 * a + 288, :] = jnp.dot(
            moved[:, 256 * a : 256 * a + 2048], deltas[...], preferred_element_type=F32
        )
    pair_ref[0] = even_ref[1]
    pair_ref[1] = odd_ref[1]
    none = jnp.zeros((1, 128), F32)
    for y_to in range(4):
        for z_to in range(4):
            parts = []
            for e in range(2):
                parts.append(whole[pl.ds(8 * y_to + 4 * e + z_to, 27, stride=32), :])
                parts.append(none)
            out_ref[4 * y_to + z_to] = jnp.concatenate(parts, axis=0).astype(BF16)


def over_y_zl_body(got_ref, even_ref, odd_ref, pair_ref, out_ref, slices, rows):
    total = sum(got_ref[i].astype(F32) for i in range(16)) * (1.0 / CELLS)
    zl = lax.axis_index("zl")
    for k, block in ((0, even_ref[0]), (2, odd_ref[0]), (1, pair_ref[0]), (3, pair_ref[1])):
        slices[zl ^ k] = block
    rows[:27, :] = total[:27]
    rows[27:54, :] = total[28:55]
    for y in range(4):
        rows[54 + 54 * y : 108 + 54 * y, :] = slices[y].astype(F32)[:54]
    rows[270:, :] = jnp.zeros((2, 128), F32)
    for to in range(4):
        out_ref[to] = rows[...].astype(BF16)


def over_zh_zg_body(owner_ref, got_ref, out_ref, basis_ref, here_ref, next_ref, rows, slices):
    for i in range(4):
        rows[i, :272, :] = got_ref[i].astype(F32)
        rows[i, 272:, :] = jnp.zeros((8, 128), F32)
        for y in range(4):
            slices[i, y] = rows[i, 54 + 54 * y : 118 + 54 * y, :].astype(BF16)
    total = (rows[0, :54, :] + rows[1, :54, :]) + (rows[2, :54, :] + rows[3, :54, :])
    none = jnp.zeros((1, 128), F32)
    total = jnp.concatenate([total[:27], none, total[27:], none], axis=0).astype(BF16)
    for to in range(32):
        out_ref[to] = total
    for j in range(8):
        for zg in range(2):
            basis_ref[j, 64 * zg : 64 * zg + 64] = slices[2 * (owner_ref[j] & 1) + zg, owner_ref[j] >> 1]
    zg, zl = lax.axis_index("zg"), lax.axis_index("zl")
    for k, ref in ((0, here_ref), (2, next_ref)):
        ref[0] = basis_ref[4 * zg + (zl ^ k)]
        ref[1] = basis_ref[4 * zg + (zl ^ k ^ 1)]


def rotate_body(got_ref, basis_ref, here_ref, next_ref, out_ref, pair_ref, grads, ordered):
    pair_ref[0] = here_ref[1]
    pair_ref[1] = next_ref[1]
    for y in range(4):
        for x in range(4):
            at = 28 * (8 * x + 2 * y)
            for c in range(2):
                grads[c, at : at + 56, :] = got_ref[8 * y + 2 * x + c].astype(F32)
    for tap in range(27):
        for c in range(2):
            ordered[32 * tap : 32 * tap + 32, 128 * c : 128 * c + 128] = grads[c, pl.ds(tap, 32, stride=28), :]
    ordered[864:, :] = jnp.zeros((32, 256), F32)
    inside = iota((128, 128), 1) < 108
    total = jnp.zeros((128, 256), F32)
    for j in range(8):
        block = jnp.where(inside, basis_ref[j].astype(F32), 0.0).astype(BF16)
        rows = ordered[108 * j : 108 * j + 128, :].astype(BF16)
        total = total + jnp.dot(block, rows, preferred_element_type=F32)
    total = jnp.concatenate(
        [total[64 * zg : 64 * zg + 56, 128 * c : 128 * c + 128] for zg in range(2) for c in range(2)], axis=0
    ).astype(BF16)
    for to in range(4):
        out_ref[to] = total


def update_body(
    got_ref, here_ref, next_ref, pair_ref, out_basis_any, out_eigen_any,
    out_ref, panel, out_basis, out_eigen, ordered, sems,
):
    zl = lax.axis_index("zl")
    for k, block in ((0, here_ref[0]), (2, next_ref[0]), (1, pair_ref[0]), (3, pair_ref[1])):
        panel[zl ^ k] = block
    copies = [
        pltpu.make_async_copy(out_basis_any, out_basis, sems.at[0]),
        pltpu.make_async_copy(out_eigen_any, out_eigen, sems.at[1]),
    ]
    started(copies)
    highest = lax.Precision.HIGHEST
    total = sum(got_ref[i].astype(F32) for i in range(4))
    none = jnp.zeros((8, 256), F32)
    parts = []
    for zg in range(2):
        at = 112 * zg
        parts.append(jnp.concatenate([total[at : at + 56], total[at + 56 : at + 112]], axis=1))
        parts.append(none)
    rotated = jnp.concatenate(parts, axis=0)
    for copy in copies:
        copy.wait()
    rotated = jnp.dot(rotated, out_basis[...], precision=highest, preferred_element_type=F32)
    terms = here_ref[0].astype(F32)
    eigen = (terms[:, 108:109] + terms[:, 109:110]) + terms[:, 110:111]
    scaled = rotated / (eigen * out_eigen[...] + DAMPING)
    scaled = jnp.where((iota((128, 256), 0) & 63) < 54, scaled, 0.0)
    turned = lax.dot_general(
        scaled, out_basis[...], (((1,), (1,)), ((), ())), precision=highest, preferred_element_type=F32
    )
    high = turned.astype(BF16)
    rest = (turned - high.astype(F32)).astype(BF16)
    for r in range(4):
        block = panel[r].astype(F32).T.astype(BF16)
        rows = jnp.dot(block, high, preferred_element_type=F32) + jnp.dot(block, rest, preferred_element_type=F32)
        for c in range(2):
            ordered[c, pl.ds(r, 108, stride=4), :] = rows[:108, 128 * c : 128 * c + 128]
    for c in range(2):
        ordered[c, 432:, :] = jnp.zeros((8, 128), F32)
    for to in range(8):
        rows = [ordered[c, 54 * to : 54 * to + 56, :] for c in range(2)]
        out_ref[to] = jnp.concatenate(rows, axis=0).astype(BF16)


def over_xc_body(got_ref, out_ref):
    total = sum(got_ref[i].astype(F32) for i in range(8))
    for to in range(4):
        out_ref[to] = total.astype(BF16)


def last_body(got_ref, out_ref):
    total = sum(got_ref[i].astype(F32) for i in range(4))
    out_ref[...] = jnp.concatenate([total[:54], total[56:110]], axis=1)


def data_grad_body(inside_ref, outside_ref, mine_ref, weight_any, out_ref, token_ref, weight, planes, sem):
    copy = pltpu.make_async_copy(weight_any, weight, sem)
    copy.start()
    by_side(inside_ref, outside_ref, planes)
    planes[1] = mine_ref[...]
    none = jnp.zeros((16, 256), BF16)
    total = jnp.zeros((256, 128), F32)
    for a in range(3):
        wide = planes[2 - a].astype(F32)
        if a == 0:
            copy.wait()
        for c in range(3):
            moved = x_shifted(wide, 1 - c).astype(BF16)
            for b in range(3):
                if b == 2:
                    shifted = jnp.concatenate([none, moved[:240]], axis=0)
                elif b == 0:
                    shifted = jnp.concatenate([moved[16:], none], axis=0)
                else:
                    shifted = moved
                tap = 9 * a + 3 * b + c
                total = total + lax.dot_general(
                    shifted,
                    weight[128 * tap : 128 * tap + 128, :],
                    (((1,), (1,)), ((), ())),
                    preferred_element_type=F32,
                )
    out_ref[...] = total.astype(BF16)
    token_ref[...] = jnp.zeros((8, 128), F32)


def neighbours(block):
    inside = lax.ppermute(block, "c", [(0, 1), (1, 0)])
    pairs = [(i, i + 1) for i in range(1, 63, 2)]
    return inside, lax.ppermute(block, SPACE, pairs + [(j, i) for i, j in pairs])


def turned(block, k):
    pairs = [(4 * y + z, 4 * z + (y ^ k)) for y in range(4) for z in range(4)]
    return lax.ppermute(block, ("y", "zl"), pairs)


def across(block, k):
    return lax.ppermute(block, "zl", [(i, i ^ k) for i in range(4)])


def per_device(
    activations,
    conv_weight,
    conv_bias,
    cotangent,
    basis_panels,
    panel_owner,
    output_basis,
    input_eigen,
    output_eigen,
):
    dma = pltpu.SemaphoreType.DMA
    plane = activations.reshape(256, 128)
    inside, outside = neighbours(plane)

    first = call(first_body, shape((8, 128), F32), flops=4_000_000_000)
    stored = call(
        basis_body,
        shape((4, 64, 128), BF16),
        arrays=(basis_panels[0].T,),
        remote=(input_eigen.reshape(1, 54),),
        after=(first,),
        scratch=[pltpu.VMEM((1, 54), F32), dma],
    )
    delta, send, even, odd = call(
        forward_body,
        [shape((256, 256), BF16), shape((8, 384, 128), BF16)] + [shape((2, 64, 128), BF16)] * 2,
        (),
        (inside, outside, plane, conv_weight, conv_bias.reshape(1, 256), cotangent.reshape(256, 256), stored),
        scratch=[pltpu.VMEM((256, 3456), BF16), pltpu.VMEM((3, 256, 128), BF16)],
        flops=2 * 256 * 3456 * 256,
    )
    even, odd = turned(even, 0), turned(odd, 2)
    part, pair = call(
        weight_grad_body,
        [shape((16, 56, 128), BF16), shape((2, 64, 128), BF16)],
        arrays=(exchange(send, XC), even, odd),
        scratch=[pltpu.VMEM((288, 2560), BF16), pltpu.VMEM((2048, 128), BF16), pltpu.VMEM((864, 128), F32)],
        flops=2 * 864 * 2048 * 128,
    )
    part = call(
        over_y_zl_body,
        shape((4, 272, 128), BF16),
        arrays=(exchange(part, ("y", "zl")), even, odd, across(pair, 1)),
        scratch=[pltpu.VMEM((4, 64, 128), BF16), pltpu.VMEM((272, 128), F32)],
    )
    inside, outside = neighbours(delta)
    part, basis, here, there = call(
        over_zh_zg_body,
        [shape((32, 56, 128), BF16), shape((8, 128, 128), BF16)] + [shape((2, 128, 128), BF16)] * 2,
        (panel_owner,),
        (exchange(part, ("zh", "zg")),),
        after=(inside, outside),
        scratch=[pltpu.VMEM((4, 280, 128), F32), pltpu.VMEM((4, 4, 64, 128), BF16)],
    )
    there = across(there, 2)
    rotated, pair = call(
        rotate_body,
        [shape((4, 224, 128), BF16), shape((2, 128, 128), BF16)],
        arrays=(exchange(part, YXC), basis, here, there),
        scratch=[pltpu.VMEM((2, 896, 128), F32), pltpu.VMEM((896, 256), F32)],
    )
    data, token = call(
        data_grad_body,
        [shape((256, 128), BF16), shape((8, 128), F32)],
        (),
        (inside, outside, delta),
        (conv_weight,),
        after=(pair,),
        scratch=[pltpu.VMEM((3456, 256), BF16), pltpu.VMEM((3, 256, 256), BF16), dma],
        flops=2 * 256 * 3456 * 256,
    )
    part = call(
        update_body,
        shape((8, 112, 128), BF16),
        (),
        (exchange(rotated, "zl"), here, there, across(pair, 1)),
        (output_basis, output_eigen.reshape(1, 256)),
        after=(token,),
        scratch=[
            pltpu.VMEM((4, 128, 128), BF16),
            pltpu.VMEM((256, 256), F32),
            pltpu.VMEM((1, 256), F32),
            pltpu.VMEM((2, 440, 128), F32),
            dma((2,)),
        ],
    )
    part = call(over_xc_body, shape((4, 112, 128), BF16), arrays=(exchange(part, XC),))
    update = call(last_body, shape((54, 256), F32), arrays=(exchange(part, "y"),))
    return (data.reshape(1, 1, 16, 16, 128), update)


def solution(mesh):
    fine = Mesh(mesh.devices.reshape(SIZES), AXES)
    both = P(SAMPLE, SPACE, None, None, None)
    return jax.shard_map(
        per_device,
        mesh=fine,
        in_specs=(both, P(), P(), both, P(SAMPLE, None, SPACE), P(), P(), P(SPACE), P()),
        out_specs=(both, P(SPACE, None)),
        check_vma=False,
    )
```

```python
import jax
import jax.numpy as jnp
from jax import lax
from jax.experimental import pallas as pl
from jax.experimental.pallas import tpu as pltpu
from jax.sharding import Mesh
from jax.sharding import PartitionSpec as P

DAMPING = 0.001
CELLS = 131072
BF16 = jnp.bfloat16
F32 = jnp.float32
VMEM = pl.BlockSpec(memory_space=pltpu.VMEM)
SMEM = pl.BlockSpec(memory_space=pltpu.SMEM)
LIMIT = 48 * 1024 * 1024
ANY = pl.BlockSpec(memory_space=pl.ANY)
AXES = ("y", "zh", "zg", "zl", "x", "c")
SIZES = (4, 2, 2, 4, 4, 2)
SAMPLE = ("y", "zh")
XC = ("x", "c")
YXC = ("y", "x", "c")
SPACE = ("zg", "zl", "x", "c")


def call(body, out_shape, scalars=(), arrays=(), remote=(), after=(), scratch=(), flops=0, limit=LIMIT):
    many = isinstance(out_shape, (list, tuple))
    inputs = (*scalars, *arrays, *remote, *after)
    kept = len(inputs) - len(after)

    def kernel(*refs):
        body(*refs[:kept], *refs[len(inputs) :])

    return pl.pallas_call(
        kernel,
        out_shape=out_shape,
        in_specs=[SMEM] * len(scalars) + [VMEM] * len(arrays) + [ANY] * (len(remote) + len(after)),
        out_specs=[VMEM] * len(out_shape) if many else VMEM,
        scratch_shapes=list(scratch),
        compiler_params=pltpu.CompilerParams(vmem_limit_bytes=limit),
        cost_estimate=pl.CostEstimate(
            flops=flops,
            bytes_accessed=sum(a.size * a.dtype.itemsize for a in inputs),
            transcendentals=0,
        ),
    )(*inputs)


def shape(dims, dtype):
    return jax.ShapeDtypeStruct(dims, dtype)


def iota(dims, axis):
    return lax.broadcasted_iota(jnp.int32, dims, axis)


def exchange(x, axes):
    return lax.all_to_all(x, axes, 0, 0)


def started(copies):
    for copy in copies:
        copy.start()
    return copies


def x_shifted(rows, step):
    if step == 0:
        return rows
    x = iota(rows.shape, 0) & 15
    inside = (x + step >= 0) & (x + step < 16)
    return jnp.where(inside, pltpu.roll(rows, (-step) % 256, 0), 0.0)


def basis_body(panel, eigen_any, out_ref, eigen, sem):
    copy = pltpu.make_async_copy(eigen_any, eigen, sem)
    copy.start()
    copy.wait()
    row = iota((54, 54), 0)
    column = jnp.sum(jnp.where(row == iota((54, 54), 1), eigen[...], 0.0), axis=1, keepdims=True)
    column = jnp.concatenate([column, jnp.ones((10, 1), F32)], axis=0)
    first = column.astype(BF16).astype(F32)
    second = (column - first).astype(BF16).astype(F32)
    third = column - first - second
    for r in range(4):
        pick = iota((432, 128), 0) == 4 * iota((432, 128), 1) + r
        block = jnp.dot(panel[...], jnp.where(pick, 1.0, 0.0).astype(BF16), preferred_element_type=F32)
        block = jnp.concatenate([block, jnp.zeros((10, 128), F32)], axis=0)
        at = iota((64, 128), 1)
        block = jnp.where(at == 108, first, block)
        block = jnp.where(at == 109, second, block)
        block = jnp.where(at == 110, third, block)
        out_ref[r] = block.astype(BF16)


def by_side(inside_ref, outside_ref, planes):
    second = lax.axis_index("c")
    planes[2 - 2 * second] = inside_ref[...]
    planes[2 * second] = outside_ref[...]


def first_body(out_ref):
    out_ref[...] = jnp.zeros((8, 128), F32)


def forward_body(
    inside_ref, outside_ref, mine, weight, bias, cot, basis_ref,
    delta_ref, send_ref, even_ref, odd_ref, patches, planes,
):
    y = lax.axis_index("y")
    for k, ref in ((0, even_ref), (2, odd_ref)):
        ref[0] = basis_ref[y ^ k]
        ref[1] = basis_ref[y ^ k ^ 1]
    by_side(inside_ref, outside_ref, planes)
    planes[1] = mine[...]
    none = jnp.zeros((16, 128), BF16)
    for a in range(3):
        wide = planes[a].astype(F32)
        for c in range(3):
            moved = x_shifted(wide, c - 1).astype(BF16)
            for b in range(3):
                at = (9 * a + 3 * b + c) * 128
                if b == 0:
                    shifted = jnp.concatenate([none, moved[:240]], axis=0)
                elif b == 2:
                    shifted = jnp.concatenate([moved[16:], none], axis=0)
                else:
                    shifted = moved
                patches[:, at : at + 128] = shifted
    pre = jnp.dot(patches[...], weight[...], preferred_element_type=F32) + bias[...]
    logistic = 1.0 / (1.0 + jnp.exp(-pre))
    delta = (cot[...].astype(F32) * logistic * (1.0 + pre * (1.0 - logistic))).astype(BF16)
    delta_ref[...] = delta
    act_t = mine[...].astype(F32).T.astype(BF16)
    rim_t = planes[2 * (lax.axis_index("x") >> 1)].astype(F32).T.astype(BF16)
    for x in range(4):
        for c in range(2):
            to = 2 * x + c
            for half in range(2):
                lanes = slice(128 * half, 128 * half + 128)
                rows = slice(32 * x, 32 * x + 32)
                send_ref[to, 32 * half : 32 * half + 32] = act_t[rows, lanes]
                send_ref[to, 64 + 32 * half : 96 + 32 * half] = rim_t[rows, lanes]
            send_ref[to, 128:] = delta[:, 128 * c : 128 * c + 128]


def weight_grad_body(got_ref, even_ref, odd_ref, out_ref, pair_ref, moved, deltas, whole):
    pieces = []
    for plane, at in [(0, 64)] + [(e, 0) for e in range(8)] + [(7, 64)]:
        pieces.append(got_ref[plane, at : at + 32].astype(F32))
        pieces.append(got_ref[plane, at + 32 : at + 64].astype(F32))
    acts = jnp.concatenate(pieces, axis=1)
    lane = iota((8, 2560), 1)
    x = lane & 15
    y = (lane >> 4) & 15
    for b in range(3):
        for c in range(3):
            step = 16 * (b - 1) + (c - 1)
            turned = pltpu.roll(acts, (-step) % 2560, 1) if step else acts
            inside = (x + c >= 1) & (x + c < 17) & (y + b >= 1) & (y + b < 17)
            kept = jnp.where(inside[None], turned.reshape(4, 8, 2560), 0.0).reshape(32, 2560)
            moved[32 * (3 * b + c) : 32 * (3 * b + c) + 32, :] = kept.astype(BF16)
    for e in range(8):
        deltas[256 * e : 256 * e + 256, :] = got_ref[e, 128:]
    for a in range(3):
        whole[288 * a : 288 * a + 288, :] = jnp.dot(
            moved[:, 256 * a : 256 * a + 2048], deltas[...], preferred_element_type=F32
        )
    pair_ref[0] = even_ref[1]
    pair_ref[1] = odd_ref[1]
    none = jnp.zeros((1, 128), F32)
    for y_to in range(4):
        for z_to in range(4):
            parts = []
            for e in range(2):
                parts.append(whole[pl.ds(8 * y_to + 4 * e + z_to, 27, stride=32), :])
                parts.append(none)
            out_ref[4 * y_to + z_to] = jnp.concatenate(parts, axis=0).astype(BF16)


def over_y_zl_body(got_ref, even_ref, odd_ref, pair_ref, out_ref, slices, rows):
    total = sum(got_ref[i].astype(F32) for i in range(16)) * (1.0 / CELLS)
    zl = lax.axis_index("zl")
    for k, block in ((0, even_ref[0]), (2, odd_ref[0]), (1, pair_ref[0]), (3, pair_ref[1])):
        slices[zl ^ k] = block
    rows[:27, :] = total[:27]
    rows[27:54, :] = total[28:55]
    for y in range(4):
        rows[54 + 54 * y : 108 + 54 * y, :] = slices[y].astype(F32)[:54]
    rows[270:, :] = jnp.zeros((2, 128), F32)
    for to in range(4):
        out_ref[to] = rows[...].astype(BF16)


def over_zh_zg_body(owner_ref, got_ref, out_ref, basis_ref, here_ref, next_ref, rows, slices):
    for i in range(4):
        rows[i, :272, :] = got_ref[i].astype(F32)
        rows[i, 272:, :] = jnp.zeros((8, 128), F32)
        for y in range(4):
            slices[i, y] = rows[i, 54 + 54 * y : 118 + 54 * y, :].astype(BF16)
    total = (rows[0, :54, :] + rows[1, :54, :]) + (rows[2, :54, :] + rows[3, :54, :])
    none = jnp.zeros((1, 128), F32)
    total = jnp.concatenate([total[:27], none, total[27:], none], axis=0).astype(BF16)
    for to in range(32):
        out_ref[to] = total
    for j in range(8):
        for zg in range(2):
            basis_ref[j, 64 * zg : 64 * zg + 64] = slices[2 * (owner_ref[j] & 1) + zg, owner_ref[j] >> 1]
    zg, zl = lax.axis_index("zg"), lax.axis_index("zl")
    for k, ref in ((0, here_ref), (2, next_ref)):
        ref[0] = basis_ref[4 * zg + (zl ^ k)]
        ref[1] = basis_ref[4 * zg + (zl ^ k ^ 1)]


def rotate_body(got_ref, basis_ref, here_ref, next_ref, out_ref, pair_ref, grads, ordered):
    pair_ref[0] = here_ref[1]
    pair_ref[1] = next_ref[1]
    for y in range(4):
        for x in range(4):
            at = 28 * (8 * x + 2 * y)
            for c in range(2):
                grads[c, at : at + 56, :] = got_ref[8 * y + 2 * x + c].astype(F32)
    for tap in range(27):
        for c in range(2):
            ordered[32 * tap : 32 * tap + 32, 128 * c : 128 * c + 128] = grads[c, pl.ds(tap, 32, stride=28), :]
    ordered[864:, :] = jnp.zeros((32, 256), F32)
    inside = iota((128, 128), 1) < 108
    total = jnp.zeros((128, 256), F32)
    for j in range(8):
        block = jnp.where(inside, basis_ref[j].astype(F32), 0.0).astype(BF16)
        rows = ordered[108 * j : 108 * j + 128, :].astype(BF16)
        total = total + jnp.dot(block, rows, preferred_element_type=F32)
    total = jnp.concatenate(
        [total[64 * zg : 64 * zg + 56, 128 * c : 128 * c + 128] for zg in range(2) for c in range(2)], axis=0
    ).astype(BF16)
    for to in range(4):
        out_ref[to] = total


def update_body(
    got_ref, here_ref, next_ref, pair_ref, out_basis_any, out_eigen_any,
    out_ref, panel, out_basis, out_eigen, ordered, sems,
):
    zl = lax.axis_index("zl")
    for k, block in ((0, here_ref[0]), (2, next_ref[0]), (1, pair_ref[0]), (3, pair_ref[1])):
        panel[zl ^ k] = block
    copies = [
        pltpu.make_async_copy(out_basis_any, out_basis, sems.at[0]),
        pltpu.make_async_copy(out_eigen_any, out_eigen, sems.at[1]),
    ]
    started(copies)
    highest = lax.Precision.HIGHEST
    total = sum(got_ref[i].astype(F32) for i in range(4))
    none = jnp.zeros((8, 256), F32)
    parts = []
    for zg in range(2):
        at = 112 * zg
        parts.append(jnp.concatenate([total[at : at + 56], total[at + 56 : at + 112]], axis=1))
        parts.append(none)
    rotated = jnp.concatenate(parts, axis=0)
    for copy in copies:
        copy.wait()
    rotated = jnp.dot(rotated, out_basis[...], precision=highest, preferred_element_type=F32)
    terms = here_ref[0].astype(F32)
    eigen = (terms[:, 108:109] + terms[:, 109:110]) + terms[:, 110:111]
    scaled = rotated / (eigen * out_eigen[...] + DAMPING)
    scaled = jnp.where((iota((128, 256), 0) & 63) < 54, scaled, 0.0)
    turned = lax.dot_general(
        scaled, out_basis[...], (((1,), (1,)), ((), ())), precision=highest, preferred_element_type=F32
    )
    high = turned.astype(BF16)
    rest = (turned - high.astype(F32)).astype(BF16)
    for r in range(4):
        block = panel[r].astype(F32).T.astype(BF16)
        rows = jnp.dot(block, high, preferred_element_type=F32) + jnp.dot(block, rest, preferred_element_type=F32)
        for c in range(2):
            ordered[c, pl.ds(r, 108, stride=4), :] = rows[:108, 128 * c : 128 * c + 128]
    for c in range(2):
        ordered[c, 432:, :] = jnp.zeros((8, 128), F32)
    for to in range(8):
        rows = [ordered[c, 54 * to : 54 * to + 56, :] for c in range(2)]
        out_ref[to] = jnp.concatenate(rows, axis=0).astype(BF16)


def over_xc_body(got_ref, out_ref):
    total = sum(got_ref[i].astype(F32) for i in range(8))
    for to in range(4):
        out_ref[to] = total.astype(BF16)


def last_body(got_ref, out_ref):
    total = sum(got_ref[i].astype(F32) for i in range(4))
    out_ref[...] = jnp.concatenate([total[:54], total[56:110]], axis=1)


def data_grad_body(inside_ref, outside_ref, mine_ref, weight_any, out_ref, token_ref, weight, planes, sem):
    copy = pltpu.make_async_copy(weight_any, weight, sem)
    copy.start()
    by_side(inside_ref, outside_ref, planes)
    planes[1] = mine_ref[...]
    none = jnp.zeros((16, 256), BF16)
    total = jnp.zeros((256, 128), F32)
    for a in range(3):
        wide = planes[2 - a].astype(F32)
        if a == 0:
            copy.wait()
        for c in range(3):
            moved = x_shifted(wide, 1 - c).astype(BF16)
            for b in range(3):
                if b == 2:
                    shifted = jnp.concatenate([none, moved[:240]], axis=0)
                elif b == 0:
                    shifted = jnp.concatenate([moved[16:], none], axis=0)
                else:
                    shifted = moved
                tap = 9 * a + 3 * b + c
                total = total + lax.dot_general(
                    shifted,
                    weight[128 * tap : 128 * tap + 128, :],
                    (((1,), (1,)), ((), ())),
                    preferred_element_type=F32,
                )
    out_ref[...] = total.astype(BF16)
    token_ref[...] = jnp.zeros((8, 128), F32)


def neighbours(block):
    inside = lax.ppermute(block, "c", [(0, 1), (1, 0)])
    pairs = [(i, i + 1) for i in range(1, 63, 2)]
    return inside, lax.ppermute(block, SPACE, pairs + [(j, i) for i, j in pairs])


def turned(block, k):
    pairs = [(4 * y + z, 4 * z + (y ^ k)) for y in range(4) for z in range(4)]
    return lax.ppermute(block, ("y", "zl"), pairs)


def across(block, k):
    return lax.ppermute(block, "zl", [(i, i ^ k) for i in range(4)])


def per_device(
    activations,
    conv_weight,
    conv_bias,
    cotangent,
    basis_panels,
    panel_owner,
    output_basis,
    input_eigen,
    output_eigen,
):
    dma = pltpu.SemaphoreType.DMA
    plane = activations.reshape(256, 128)
    inside, outside = neighbours(plane)

    first = call(first_body, shape((8, 128), F32), flops=4_000_000_000)
    stored = call(
        basis_body,
        shape((4, 64, 128), BF16),
        arrays=(basis_panels[0].T,),
        remote=(input_eigen.reshape(1, 54),),
        after=(first,),
        scratch=[pltpu.VMEM((1, 54), F32), dma],
    )
    delta, send, even, odd = call(
        forward_body,
        [shape((256, 256), BF16), shape((8, 384, 128), BF16)] + [shape((2, 64, 128), BF16)] * 2,
        (),
        (inside, outside, plane, conv_weight, conv_bias.reshape(1, 256), cotangent.reshape(256, 256), stored),
        scratch=[pltpu.VMEM((256, 3456), BF16), pltpu.VMEM((3, 256, 128), BF16)],
        flops=2 * 256 * 3456 * 256,
    )
    even, odd = turned(even, 0), turned(odd, 2)
    part, pair = call(
        weight_grad_body,
        [shape((16, 56, 128), BF16), shape((2, 64, 128), BF16)],
        arrays=(exchange(send, XC), even, odd),
        scratch=[pltpu.VMEM((288, 2560), BF16), pltpu.VMEM((2048, 128), BF16), pltpu.VMEM((864, 128), F32)],
        flops=2 * 864 * 2048 * 128,
    )
    part = call(
        over_y_zl_body,
        shape((4, 272, 128), BF16),
        arrays=(exchange(part, ("y", "zl")), even, odd, across(pair, 1)),
        scratch=[pltpu.VMEM((4, 64, 128), BF16), pltpu.VMEM((272, 128), F32)],
    )
    inside, outside = neighbours(delta)
    part, basis, here, there = call(
        over_zh_zg_body,
        [shape((32, 56, 128), BF16), shape((8, 128, 128), BF16)] + [shape((2, 128, 128), BF16)] * 2,
        (panel_owner,),
        (exchange(part, ("zh", "zg")),),
        after=(outside,),
        scratch=[pltpu.VMEM((4, 280, 128), F32), pltpu.VMEM((4, 4, 64, 128), BF16)],
    )
    there = across(there, 2)
    rotated, pair = call(
        rotate_body,
        [shape((4, 224, 128), BF16), shape((2, 128, 128), BF16)],
        arrays=(exchange(part, YXC), basis, here, there),
        scratch=[pltpu.VMEM((2, 896, 128), F32), pltpu.VMEM((896, 256), F32)],
    )
    part = call(
        update_body,
        shape((8, 112, 128), BF16),
        (),
        (exchange(rotated, "zl"), here, there, across(pair, 1)),
        (output_basis, output_eigen.reshape(1, 256)),
        scratch=[
            pltpu.VMEM((4, 128, 128), BF16),
            pltpu.VMEM((256, 256), F32),
            pltpu.VMEM((1, 256), F32),
            pltpu.VMEM((2, 440, 128), F32),
            dma((2,)),
        ],
    )
    part = call(over_xc_body, shape((4, 112, 128), BF16), arrays=(exchange(part, XC),), after=(inside,))
    data, token = call(
        data_grad_body,
        [shape((256, 128), BF16), shape((8, 128), F32)],
        (),
        (inside, outside, delta),
        (conv_weight,),
        after=(part,),
        scratch=[pltpu.VMEM((3456, 256), BF16), pltpu.VMEM((3, 256, 256), BF16), dma],
        flops=2 * 256 * 3456 * 256,
    )
    update = call(last_body, shape((54, 256), F32), arrays=(exchange(part, "y"),), after=(token,))
    return (data.reshape(1, 1, 16, 16, 128), update)


def solution(mesh):
    fine = Mesh(mesh.devices.reshape(SIZES), AXES)
    both = P(SAMPLE, SPACE, None, None, None)
    return jax.shard_map(
        per_device,
        mesh=fine,
        in_specs=(both, P(), P(), both, P(SAMPLE, None, SPACE), P(), P(), P(SPACE), P()),
        out_specs=(both, P(SPACE, None)),
        check_vma=False,
    )
```

```python
import jax
import jax.numpy as jnp
from jax import lax
from jax.experimental import pallas as pl
from jax.experimental.pallas import tpu as pltpu
from jax.sharding import Mesh
from jax.sharding import PartitionSpec as P

DAMPING = 0.001
CELLS = 131072
BF16 = jnp.bfloat16
F32 = jnp.float32
VMEM = pl.BlockSpec(memory_space=pltpu.VMEM)
SMEM = pl.BlockSpec(memory_space=pltpu.SMEM)
LIMIT = 48 * 1024 * 1024
ANY = pl.BlockSpec(memory_space=pl.ANY)
AXES = ("y", "zh", "zg", "zl", "x", "c")
SIZES = (4, 2, 2, 4, 4, 2)
SAMPLE = ("y", "zh")
CX = ("c", "x")
CXY = ("c", "x", "y")
SPACE = ("zg", "zl", "x", "c")


def call(body, out_shape, scalars=(), arrays=(), remote=(), after=(), scratch=(), flops=0, limit=LIMIT):
    many = isinstance(out_shape, (list, tuple))
    inputs = (*scalars, *arrays, *remote, *after)
    kept = len(inputs) - len(after)

    def kernel(*refs):
        body(*refs[:kept], *refs[len(inputs) :])

    return pl.pallas_call(
        kernel,
        out_shape=out_shape,
        in_specs=[SMEM] * len(scalars) + [VMEM] * len(arrays) + [ANY] * (len(remote) + len(after)),
        out_specs=[VMEM] * len(out_shape) if many else VMEM,
        scratch_shapes=list(scratch),
        compiler_params=pltpu.CompilerParams(vmem_limit_bytes=limit),
        cost_estimate=pl.CostEstimate(
            flops=flops,
            bytes_accessed=sum(a.size * a.dtype.itemsize for a in inputs),
            transcendentals=0,
        ),
    )(*inputs)


def shape(dims, dtype):
    return jax.ShapeDtypeStruct(dims, dtype)


def iota(dims, axis):
    return lax.broadcasted_iota(jnp.int32, dims, axis)


def exchange(x, axes):
    return lax.all_to_all(x, axes, 0, 0)


def started(copies):
    for copy in copies:
        copy.start()
    return copies


def x_shifted(rows, step):
    if step == 0:
        return rows
    x = iota(rows.shape, 0) & 15
    inside = (x + step >= 0) & (x + step < 16)
    return jnp.where(inside, pltpu.roll(rows, (-step) % 256, 0), 0.0)


def basis_body(panel, eigen_any, out_ref, eigen, sem):
    copy = pltpu.make_async_copy(eigen_any, eigen, sem)
    copy.start()
    copy.wait()
    row = iota((54, 54), 0)
    column = jnp.sum(jnp.where(row == iota((54, 54), 1), eigen[...], 0.0), axis=1, keepdims=True)
    column = jnp.concatenate([column, jnp.ones((10, 1), F32)], axis=0)
    first = column.astype(BF16).astype(F32)
    second = (column - first).astype(BF16).astype(F32)
    third = column - first - second
    for r in range(4):
        pick = iota((432, 128), 0) == 4 * iota((432, 128), 1) + r
        block = jnp.dot(panel[...], jnp.where(pick, 1.0, 0.0).astype(BF16), preferred_element_type=F32)
        block = jnp.concatenate([block, jnp.zeros((10, 128), F32)], axis=0)
        at = iota((64, 128), 1)
        block = jnp.where(at == 108, first, block)
        block = jnp.where(at == 109, second, block)
        block = jnp.where(at == 110, third, block)
        out_ref[r] = block.astype(BF16)


def by_side(inside_ref, outside_ref, planes):
    second = lax.axis_index("c")
    planes[2 - 2 * second] = inside_ref[...]
    planes[2 * second] = outside_ref[...]


def first_body(out_ref):
    out_ref[...] = jnp.zeros((8, 128), F32)


def forward_body(
    inside_ref, outside_ref, mine, weight, bias, cot, basis_ref,
    delta_ref, send_ref, even_ref, odd_ref, patches, planes,
):
    y = lax.axis_index("y")
    for k, ref in ((0, even_ref), (2, odd_ref)):
        ref[0] = basis_ref[y ^ k]
        ref[1] = basis_ref[y ^ k ^ 1]
    by_side(inside_ref, outside_ref, planes)
    planes[1] = mine[...]
    none = jnp.zeros((16, 128), BF16)
    for a in range(3):
        wide = planes[a].astype(F32)
        for c in range(3):
            moved = x_shifted(wide, c - 1).astype(BF16)
            for b in range(3):
                at = (9 * a + 3 * b + c) * 128
                if b == 0:
                    shifted = jnp.concatenate([none, moved[:240]], axis=0)
                elif b == 2:
                    shifted = jnp.concatenate([moved[16:], none], axis=0)
                else:
                    shifted = moved
                patches[:, at : at + 128] = shifted
    pre = jnp.dot(patches[...], weight[...], preferred_element_type=F32) + bias[...]
    logistic = 1.0 / (1.0 + jnp.exp(-pre))
    delta = (cot[...].astype(F32) * logistic * (1.0 + pre * (1.0 - logistic))).astype(BF16)
    delta_ref[...] = delta
    act_t = mine[...].astype(F32).T.astype(BF16)
    rim_t = planes[2 * (lax.axis_index("x") >> 1)].astype(F32).T.astype(BF16)
    for x in range(4):
        for c in range(2):
            to = 4 * c + x
            for half in range(2):
                lanes = slice(128 * half, 128 * half + 128)
                rows = slice(32 * x, 32 * x + 32)
                send_ref[to, 32 * half : 32 * half + 32] = act_t[rows, lanes]
                send_ref[to, 64 + 32 * half : 96 + 32 * half] = rim_t[rows, lanes]
            send_ref[to, 128:] = delta[:, 128 * c : 128 * c + 128]


def slot(e):
    return 4 * (e % 2) + e // 2


def weight_grad_body(got_ref, even_ref, odd_ref, out_ref, pair_ref, moved, deltas, whole):
    pieces = []
    for plane, at in [(0, 64)] + [(e, 0) for e in range(8)] + [(7, 64)]:
        pieces.append(got_ref[slot(plane), at : at + 32].astype(F32))
        pieces.append(got_ref[slot(plane), at + 32 : at + 64].astype(F32))
    acts = jnp.concatenate(pieces, axis=1)
    lane = iota((8, 2560), 1)
    x = lane & 15
    y = (lane >> 4) & 15
    for b in range(3):
        for c in range(3):
            step = 16 * (b - 1) + (c - 1)
            turned = pltpu.roll(acts, (-step) % 2560, 1) if step else acts
            inside = (x + c >= 1) & (x + c < 17) & (y + b >= 1) & (y + b < 17)
            kept = jnp.where(inside[None], turned.reshape(4, 8, 2560), 0.0).reshape(32, 2560)
            moved[32 * (3 * b + c) : 32 * (3 * b + c) + 32, :] = kept.astype(BF16)
    for e in range(8):
        deltas[256 * e : 256 * e + 256, :] = got_ref[slot(e), 128:]
    for a in range(3):
        whole[288 * a : 288 * a + 288, :] = jnp.dot(
            moved[:, 256 * a : 256 * a + 2048], deltas[...], preferred_element_type=F32
        )
    pair_ref[0] = even_ref[1]
    pair_ref[1] = odd_ref[1]
    none = jnp.zeros((1, 128), F32)
    for y_to in range(4):
        for z_to in range(4):
            parts = []
            for e in range(2):
                parts.append(whole[pl.ds(8 * y_to + 4 * e + z_to, 27, stride=32), :])
                parts.append(none)
            out_ref[4 * z_to + y_to] = jnp.concatenate(parts, axis=0).astype(BF16)


def over_y_zl_body(got_ref, even_ref, odd_ref, pair_ref, out_ref, slices, rows):
    total = sum(got_ref[i].astype(F32) for i in range(16)) * (1.0 / CELLS)
    zl = lax.axis_index("zl")
    for k, block in ((0, even_ref[0]), (2, odd_ref[0]), (1, pair_ref[0]), (3, pair_ref[1])):
        slices[zl ^ k] = block
    rows[:27, :] = total[:27]
    rows[27:54, :] = total[28:55]
    for y in range(4):
        rows[54 + 54 * y : 108 + 54 * y, :] = slices[y].astype(F32)[:54]
    rows[270:, :] = jnp.zeros((2, 128), F32)
    for to in range(4):
        out_ref[to] = rows[...].astype(BF16)


def over_zh_zg_body(owner_ref, got_ref, out_ref, basis_ref, here_ref, next_ref, rows, slices):
    for i in range(4):
        rows[i, :272, :] = got_ref[i].astype(F32)
        rows[i, 272:, :] = jnp.zeros((8, 128), F32)
        for y in range(4):
            slices[i, y] = rows[i, 54 + 54 * y : 118 + 54 * y, :].astype(BF16)
    total = (rows[0, :54, :] + rows[1, :54, :]) + (rows[2, :54, :] + rows[3, :54, :])
    none = jnp.zeros((1, 128), F32)
    total = jnp.concatenate([total[:27], none, total[27:], none], axis=0).astype(BF16)
    for to in range(32):
        out_ref[to] = total
    for j in range(8):
        for zg in range(2):
            basis_ref[j, 64 * zg : 64 * zg + 64] = slices[2 * zg + (owner_ref[j] & 1), owner_ref[j] >> 1]
    zg, zl = lax.axis_index("zg"), lax.axis_index("zl")
    for k, ref in ((0, here_ref), (2, next_ref)):
        ref[0] = basis_ref[4 * zg + (zl ^ k)]
        ref[1] = basis_ref[4 * zg + (zl ^ k ^ 1)]


def rotate_body(got_ref, basis_ref, here_ref, next_ref, out_ref, pair_ref, grads, ordered):
    pair_ref[0] = here_ref[1]
    pair_ref[1] = next_ref[1]
    for y in range(4):
        for x in range(4):
            at = 28 * (8 * x + 2 * y)
            for c in range(2):
                grads[c, at : at + 56, :] = got_ref[16 * c + 4 * x + y].astype(F32)
    for tap in range(27):
        for c in range(2):
            ordered[32 * tap : 32 * tap + 32, 128 * c : 128 * c + 128] = grads[c, pl.ds(tap, 32, stride=28), :]
    ordered[864:, :] = jnp.zeros((32, 256), F32)
    inside = iota((128, 128), 1) < 108
    total = jnp.zeros((128, 256), F32)
    for j in range(8):
        block = jnp.where(inside, basis_ref[j].astype(F32), 0.0).astype(BF16)
        rows = ordered[108 * j : 108 * j + 128, :].astype(BF16)
        total = total + jnp.dot(block, rows, preferred_element_type=F32)
    total = jnp.concatenate(
        [total[64 * zg : 64 * zg + 56, 128 * c : 128 * c + 128] for zg in range(2) for c in range(2)], axis=0
    ).astype(BF16)
    for to in range(4):
        out_ref[to] = total


def update_body(
    got_ref, here_ref, next_ref, pair_ref, out_basis_any, out_eigen_any,
    out_ref, panel, out_basis, out_eigen, ordered, sems,
):
    zl = lax.axis_index("zl")
    for k, block in ((0, here_ref[0]), (2, next_ref[0]), (1, pair_ref[0]), (3, pair_ref[1])):
        panel[zl ^ k] = block
    copies = [
        pltpu.make_async_copy(out_basis_any, out_basis, sems.at[0]),
        pltpu.make_async_copy(out_eigen_any, out_eigen, sems.at[1]),
    ]
    started(copies)
    highest = lax.Precision.HIGHEST
    total = sum(got_ref[i].astype(F32) for i in range(4))
    none = jnp.zeros((8, 256), F32)
    parts = []
    for zg in range(2):
        at = 112 * zg
        parts.append(jnp.concatenate([total[at : at + 56], total[at + 56 : at + 112]], axis=1))
        parts.append(none)
    rotated = jnp.concatenate(parts, axis=0)
    for copy in copies:
        copy.wait()
    rotated = jnp.dot(rotated, out_basis[...], precision=highest, preferred_element_type=F32)
    terms = here_ref[0].astype(F32)
    eigen = (terms[:, 108:109] + terms[:, 109:110]) + terms[:, 110:111]
    scaled = rotated / (eigen * out_eigen[...] + DAMPING)
    scaled = jnp.where((iota((128, 256), 0) & 63) < 54, scaled, 0.0)
    turned = lax.dot_general(
        scaled, out_basis[...], (((1,), (1,)), ((), ())), precision=highest, preferred_element_type=F32
    )
    high = turned.astype(BF16)
    rest = (turned - high.astype(F32)).astype(BF16)
    for r in range(4):
        block = panel[r].astype(F32).T.astype(BF16)
        rows = jnp.dot(block, high, preferred_element_type=F32) + jnp.dot(block, rest, preferred_element_type=F32)
        for c in range(2):
            ordered[c, pl.ds(r, 108, stride=4), :] = rows[:108, 128 * c : 128 * c + 128]
    for c in range(2):
        ordered[c, 432:, :] = jnp.zeros((8, 128), F32)
    for to in range(8):
        rows = [ordered[c, 54 * to : 54 * to + 56, :] for c in range(2)]
        out_ref[slot(to)] = jnp.concatenate(rows, axis=0).astype(BF16)


def over_xc_body(got_ref, out_ref):
    total = sum(got_ref[i].astype(F32) for i in range(8))
    for to in range(4):
        out_ref[to] = total.astype(BF16)


def last_body(got_ref, out_ref):
    total = sum(got_ref[i].astype(F32) for i in range(4))
    out_ref[...] = jnp.concatenate([total[:54], total[56:110]], axis=1)


def data_grad_body(inside_ref, outside_ref, mine_ref, weight_any, out_ref, token_ref, weight, planes, sem):
    copy = pltpu.make_async_copy(weight_any, weight, sem)
    copy.start()
    by_side(inside_ref, outside_ref, planes)
    planes[1] = mine_ref[...]
    none = jnp.zeros((16, 256), BF16)
    total = jnp.zeros((256, 128), F32)
    for a in range(3):
        wide = planes[2 - a].astype(F32)
        if a == 0:
            copy.wait()
        for c in range(3):
            moved = x_shifted(wide, 1 - c).astype(BF16)
            for b in range(3):
                if b == 2:
                    shifted = jnp.concatenate([none, moved[:240]], axis=0)
                elif b == 0:
                    shifted = jnp.concatenate([moved[16:], none], axis=0)
                else:
                    shifted = moved
                tap = 9 * a + 3 * b + c
                total = total + lax.dot_general(
                    shifted,
                    weight[128 * tap : 128 * tap + 128, :],
                    (((1,), (1,)), ((), ())),
                    preferred_element_type=F32,
                )
    out_ref[...] = total.astype(BF16)
    token_ref[...] = jnp.zeros((8, 128), F32)


def neighbours(block):
    inside = lax.ppermute(block, "c", [(0, 1), (1, 0)])
    pairs = [(i, i + 1) for i in range(1, 63, 2)]
    return inside, lax.ppermute(block, SPACE, pairs + [(j, i) for i, j in pairs])


def turned(block, k):
    pairs = [(4 * y + z, 4 * z + (y ^ k)) for y in range(4) for z in range(4)]
    return lax.ppermute(block, ("y", "zl"), pairs)


def across(block, k):
    return lax.ppermute(block, "zl", [(i, i ^ k) for i in range(4)])


def per_device(
    activations,
    conv_weight,
    conv_bias,
    cotangent,
    basis_panels,
    panel_owner,
    output_basis,
    input_eigen,
    output_eigen,
):
    dma = pltpu.SemaphoreType.DMA
    plane = activations.reshape(256, 128)
    inside, outside = neighbours(plane)

    first = call(first_body, shape((8, 128), F32), flops=4_000_000_000)
    stored = call(
        basis_body,
        shape((4, 64, 128), BF16),
        arrays=(basis_panels[0].T,),
        remote=(input_eigen.reshape(1, 54),),
        after=(first,),
        scratch=[pltpu.VMEM((1, 54), F32), dma],
    )
    delta, send, even, odd = call(
        forward_body,
        [shape((256, 256), BF16), shape((8, 384, 128), BF16)] + [shape((2, 64, 128), BF16)] * 2,
        (),
        (inside, outside, plane, conv_weight, conv_bias.reshape(1, 256), cotangent.reshape(256, 256), stored),
        scratch=[pltpu.VMEM((256, 3456), BF16), pltpu.VMEM((3, 256, 128), BF16)],
        flops=2 * 256 * 3456 * 256,
    )
    even, odd = turned(even, 0), turned(odd, 2)
    part, pair = call(
        weight_grad_body,
        [shape((16, 56, 128), BF16), shape((2, 64, 128), BF16)],
        arrays=(exchange(send, CX), even, odd),
        scratch=[pltpu.VMEM((288, 2560), BF16), pltpu.VMEM((2048, 128), BF16), pltpu.VMEM((864, 128), F32)],
        flops=2 * 864 * 2048 * 128,
    )
    part = call(
        over_y_zl_body,
        shape((4, 272, 128), BF16),
        arrays=(exchange(part, ("zl", "y")), even, odd, across(pair, 1)),
        scratch=[pltpu.VMEM((4, 64, 128), BF16), pltpu.VMEM((272, 128), F32)],
    )
    inside, outside = neighbours(delta)
    part, basis, here, there = call(
        over_zh_zg_body,
        [shape((32, 56, 128), BF16), shape((8, 128, 128), BF16)] + [shape((2, 128, 128), BF16)] * 2,
        (panel_owner,),
        (exchange(part, ("zg", "zh")),),
        after=(inside, outside),
        scratch=[pltpu.VMEM((4, 280, 128), F32), pltpu.VMEM((4, 4, 64, 128), BF16)],
    )
    there = across(there, 2)
    rotated, pair = call(
        rotate_body,
        [shape((4, 224, 128), BF16), shape((2, 128, 128), BF16)],
        arrays=(exchange(part, CXY), basis, here, there),
        scratch=[pltpu.VMEM((2, 896, 128), F32), pltpu.VMEM((896, 256), F32)],
    )
    data, token = call(
        data_grad_body,
        [shape((256, 128), BF16), shape((8, 128), F32)],
        (),
        (inside, outside, delta),
        (conv_weight,),
        after=(pair,),
        scratch=[pltpu.VMEM((3456, 256), BF16), pltpu.VMEM((3, 256, 256), BF16), dma],
        flops=2 * 256 * 3456 * 256,
    )
    part = call(
        update_body,
        shape((8, 112, 128), BF16),
        (),
        (exchange(rotated, "zl"), here, there, across(pair, 1)),
        (output_basis, output_eigen.reshape(1, 256)),
        after=(token,),
        scratch=[
            pltpu.VMEM((4, 128, 128), BF16),
            pltpu.VMEM((256, 256), F32),
            pltpu.VMEM((1, 256), F32),
            pltpu.VMEM((2, 440, 128), F32),
            dma((2,)),
        ],
    )
    part = call(over_xc_body, shape((4, 112, 128), BF16), arrays=(exchange(part, CX),))
    update = call(last_body, shape((54, 256), F32), arrays=(exchange(part, "y"),))
    return (data.reshape(1, 1, 16, 16, 128), update)


def solution(mesh):
    fine = Mesh(mesh.devices.reshape(SIZES), AXES)
    both = P(SAMPLE, SPACE, None, None, None)
    return jax.shard_map(
        per_device,
        mesh=fine,
        in_specs=(both, P(), P(), both, P(SAMPLE, None, SPACE), P(), P(), P(SPACE), P()),
        out_specs=(both, P(SPACE, None)),
        check_vma=False,
    )
```

```python
import jax
import jax.numpy as jnp
from jax import lax
from jax.experimental import pallas as pl
from jax.experimental.pallas import tpu as pltpu
from jax.sharding import Mesh
from jax.sharding import PartitionSpec as P

DAMPING = 0.001
CELLS = 131072
BF16 = jnp.bfloat16
F32 = jnp.float32
VMEM = pl.BlockSpec(memory_space=pltpu.VMEM)
SMEM = pl.BlockSpec(memory_space=pltpu.SMEM)
LIMIT = 48 * 1024 * 1024
ANY = pl.BlockSpec(memory_space=pl.ANY)
AXES = ("y", "zh", "zg", "zl", "x", "c")
SIZES = (4, 2, 2, 4, 4, 2)
SAMPLE = ("y", "zh")
CX = ("c", "x")
CXY = ("c", "x", "y")
SPACE = ("zg", "zl", "x", "c")


def call(body, out_shape, scalars=(), arrays=(), remote=(), after=(), scratch=(), flops=0, limit=LIMIT):
    many = isinstance(out_shape, (list, tuple))
    inputs = (*scalars, *arrays, *remote, *after)
    kept = len(inputs) - len(after)

    def kernel(*refs):
        body(*refs[:kept], *refs[len(inputs) :])

    return pl.pallas_call(
        kernel,
        out_shape=out_shape,
        in_specs=[SMEM] * len(scalars) + [VMEM] * len(arrays) + [ANY] * (len(remote) + len(after)),
        out_specs=[VMEM] * len(out_shape) if many else VMEM,
        scratch_shapes=list(scratch),
        compiler_params=pltpu.CompilerParams(vmem_limit_bytes=limit),
        cost_estimate=pl.CostEstimate(
            flops=flops,
            bytes_accessed=sum(a.size * a.dtype.itemsize for a in inputs),
            transcendentals=0,
        ),
    )(*inputs)


def shape(dims, dtype):
    return jax.ShapeDtypeStruct(dims, dtype)


def iota(dims, axis):
    return lax.broadcasted_iota(jnp.int32, dims, axis)


def exchange(x, axes):
    return lax.all_to_all(x, axes, 0, 0)


def started(copies):
    for copy in copies:
        copy.start()
    return copies


def x_shifted(rows, step):
    if step == 0:
        return rows
    x = iota(rows.shape, 0) & 15
    inside = (x + step >= 0) & (x + step < 16)
    return jnp.where(inside, pltpu.roll(rows, (-step) % 256, 0), 0.0)


def basis_body(panel, eigen_any, out_ref, eigen, sem):
    copy = pltpu.make_async_copy(eigen_any, eigen, sem)
    copy.start()
    copy.wait()
    row = iota((54, 54), 0)
    column = jnp.sum(jnp.where(row == iota((54, 54), 1), eigen[...], 0.0), axis=1, keepdims=True)
    column = jnp.concatenate([column, jnp.ones((10, 1), F32)], axis=0)
    first = column.astype(BF16).astype(F32)
    second = (column - first).astype(BF16).astype(F32)
    third = column - first - second
    for r in range(4):
        pick = iota((432, 128), 0) == 4 * iota((432, 128), 1) + r
        block = jnp.dot(panel[...], jnp.where(pick, 1.0, 0.0).astype(BF16), preferred_element_type=F32)
        block = jnp.concatenate([block, jnp.zeros((10, 128), F32)], axis=0)
        at = iota((64, 128), 1)
        block = jnp.where(at == 108, first, block)
        block = jnp.where(at == 109, second, block)
        block = jnp.where(at == 110, third, block)
        out_ref[r] = block.astype(BF16)


def by_side(inside_ref, outside_ref, planes):
    second = lax.axis_index("c")
    planes[2 - 2 * second] = inside_ref[...]
    planes[2 * second] = outside_ref[...]


def first_body(out_ref):
    out_ref[...] = jnp.zeros((8, 128), F32)


def forward_body(
    inside_ref, outside_ref, mine, weight, bias, cot, basis_ref,
    delta_ref, send_ref, even_ref, odd_ref, patches, planes,
):
    y = lax.axis_index("y")
    for k, ref in ((0, even_ref), (2, odd_ref)):
        ref[0] = basis_ref[y ^ k]
        ref[1] = basis_ref[y ^ k ^ 1]
    by_side(inside_ref, outside_ref, planes)
    planes[1] = mine[...]
    none = jnp.zeros((16, 128), BF16)
    for a in range(3):
        wide = planes[a].astype(F32)
        for c in range(3):
            moved = x_shifted(wide, c - 1).astype(BF16)
            for b in range(3):
                at = (9 * a + 3 * b + c) * 128
                if b == 0:
                    shifted = jnp.concatenate([none, moved[:240]], axis=0)
                elif b == 2:
                    shifted = jnp.concatenate([moved[16:], none], axis=0)
                else:
                    shifted = moved
                patches[:, at : at + 128] = shifted
    pre = jnp.dot(patches[...], weight[...], preferred_element_type=F32) + bias[...]
    logistic = 1.0 / (1.0 + jnp.exp(-pre))
    delta = (cot[...].astype(F32) * logistic * (1.0 + pre * (1.0 - logistic))).astype(BF16)
    delta_ref[...] = delta
    act_t = mine[...].astype(F32).T.astype(BF16)
    rim_t = planes[2 * (lax.axis_index("x") >> 1)].astype(F32).T.astype(BF16)
    for x in range(4):
        for c in range(2):
            to = 4 * c + x
            for half in range(2):
                lanes = slice(128 * half, 128 * half + 128)
                rows = slice(32 * x, 32 * x + 32)
                send_ref[to, 32 * half : 32 * half + 32] = act_t[rows, lanes]
                send_ref[to, 64 + 32 * half : 96 + 32 * half] = rim_t[rows, lanes]
            send_ref[to, 128:] = delta[:, 128 * c : 128 * c + 128]


def slot(e):
    return 4 * (e % 2) + e // 2


def weight_grad_body(got_ref, even_ref, odd_ref, out_ref, pair_ref, moved, deltas, whole):
    pieces = []
    for plane, at in [(0, 64)] + [(e, 0) for e in range(8)] + [(7, 64)]:
        pieces.append(got_ref[slot(plane), at : at + 32].astype(F32))
        pieces.append(got_ref[slot(plane), at + 32 : at + 64].astype(F32))
    acts = jnp.concatenate(pieces, axis=1)
    lane = iota((8, 2560), 1)
    x = lane & 15
    y = (lane >> 4) & 15
    for b in range(3):
        for c in range(3):
            step = 16 * (b - 1) + (c - 1)
            turned = pltpu.roll(acts, (-step) % 2560, 1) if step else acts
            inside = (x + c >= 1) & (x + c < 17) & (y + b >= 1) & (y + b < 17)
            kept = jnp.where(inside[None], turned.reshape(4, 8, 2560), 0.0).reshape(32, 2560)
            moved[32 * (3 * b + c) : 32 * (3 * b + c) + 32, :] = kept.astype(BF16)
    for e in range(8):
        deltas[256 * e : 256 * e + 256, :] = got_ref[slot(e), 128:]
    for a in range(3):
        whole[288 * a : 288 * a + 288, :] = jnp.dot(
            moved[:, 256 * a : 256 * a + 2048], deltas[...], preferred_element_type=F32
        )
    pair_ref[0] = even_ref[1]
    pair_ref[1] = odd_ref[1]
    none = jnp.zeros((1, 128), F32)
    for y_to in range(4):
        for z_to in range(4):
            parts = []
            for e in range(2):
                parts.append(whole[pl.ds(8 * y_to + 4 * e + z_to, 27, stride=32), :])
                parts.append(none)
            out_ref[4 * z_to + y_to] = jnp.concatenate(parts, axis=0).astype(BF16)


def over_y_zl_body(got_ref, even_ref, odd_ref, pair_ref, out_ref, slices, rows):
    total = sum(got_ref[i].astype(F32) for i in range(16)) * (1.0 / CELLS)
    zl = lax.axis_index("zl")
    for k, block in ((0, even_ref[0]), (2, odd_ref[0]), (1, pair_ref[0]), (3, pair_ref[1])):
        slices[zl ^ k] = block
    rows[:27, :] = total[:27]
    rows[27:54, :] = total[28:55]
    for y in range(4):
        rows[54 + 54 * y : 108 + 54 * y, :] = slices[y].astype(F32)[:54]
    rows[270:, :] = jnp.zeros((2, 128), F32)
    for to in range(4):
        out_ref[to] = rows[...].astype(BF16)


def over_zh_zg_body(owner_ref, got_ref, out_ref, basis_ref, here_ref, next_ref, rows, slices):
    for i in range(4):
        rows[i, :272, :] = got_ref[i].astype(F32)
        rows[i, 272:, :] = jnp.zeros((16, 128), F32)
        for y in range(4):
            slices[i, y] = rows[i, 54 + 54 * y : 118 + 54 * y, :].astype(BF16)
    total = (rows[0, :54, :] + rows[1, :54, :]) + (rows[2, :54, :] + rows[3, :54, :])
    none = jnp.zeros((1, 128), F32)
    total = jnp.concatenate([total[:27], none, total[27:], none], axis=0).astype(BF16)
    for to in range(32):
        out_ref[to] = total
    for j in range(8):
        for zg in range(2):
            basis_ref[j, 64 * zg : 64 * zg + 64] = slices[2 * zg + (owner_ref[j] & 1), owner_ref[j] >> 1]
    zg, zl = lax.axis_index("zg"), lax.axis_index("zl")
    for k, ref in ((0, here_ref), (2, next_ref)):
        ref[0] = basis_ref[4 * zg + (zl ^ k)]
        ref[1] = basis_ref[4 * zg + (zl ^ k ^ 1)]


def rotate_body(got_ref, basis_ref, here_ref, next_ref, out_ref, pair_ref, grads, ordered):
    pair_ref[0] = here_ref[1]
    pair_ref[1] = next_ref[1]
    for y in range(4):
        for x in range(4):
            at = 28 * (8 * x + 2 * y)
            for c in range(2):
                grads[c, at : at + 56, :] = got_ref[16 * c + 4 * x + y].astype(F32)
    for tap in range(27):
        for c in range(2):
            ordered[32 * tap : 32 * tap + 32, 128 * c : 128 * c + 128] = grads[c, pl.ds(tap, 32, stride=28), :]
    ordered[864:, :] = jnp.zeros((32, 256), F32)
    inside = iota((128, 128), 1) < 108
    total = jnp.zeros((128, 256), F32)
    for j in range(8):
        block = jnp.where(inside, basis_ref[j].astype(F32), 0.0).astype(BF16)
        rows = ordered[108 * j : 108 * j + 128, :].astype(BF16)
        total = total + jnp.dot(block, rows, preferred_element_type=F32)
    total = jnp.concatenate(
        [total[64 * zg : 64 * zg + 56, 128 * c : 128 * c + 128] for zg in range(2) for c in range(2)], axis=0
    ).astype(BF16)
    for to in range(4):
        out_ref[to] = total


def update_body(
    got_ref, here_ref, next_ref, pair_ref, out_basis_any, out_eigen_any,
    out_ref, panel, out_basis, out_eigen, ordered, sems,
):
    zl = lax.axis_index("zl")
    for k, block in ((0, here_ref[0]), (2, next_ref[0]), (1, pair_ref[0]), (3, pair_ref[1])):
        panel[zl ^ k] = block
    copies = [
        pltpu.make_async_copy(out_basis_any, out_basis, sems.at[0]),
        pltpu.make_async_copy(out_eigen_any, out_eigen, sems.at[1]),
    ]
    started(copies)
    highest = lax.Precision.HIGHEST
    total = sum(got_ref[i].astype(F32) for i in range(4))
    none = jnp.zeros((8, 256), F32)
    parts = []
    for zg in range(2):
        at = 112 * zg
        parts.append(jnp.concatenate([total[at : at + 56], total[at + 56 : at + 112]], axis=1))
        parts.append(none)
    rotated = jnp.concatenate(parts, axis=0)
    for copy in copies:
        copy.wait()
    rotated = jnp.dot(rotated, out_basis[...], precision=highest, preferred_element_type=F32)
    terms = here_ref[0].astype(F32)
    eigen = (terms[:, 108:109] + terms[:, 109:110]) + terms[:, 110:111]
    scaled = rotated / (eigen * out_eigen[...] + DAMPING)
    scaled = jnp.where((iota((128, 256), 0) & 63) < 54, scaled, 0.0)
    turned = lax.dot_general(
        scaled, out_basis[...], (((1,), (1,)), ((), ())), precision=highest, preferred_element_type=F32
    )
    high = turned.astype(BF16)
    rest = (turned - high.astype(F32)).astype(BF16)
    for r in range(4):
        block = panel[r].astype(F32).T.astype(BF16)
        rows = jnp.dot(block, high, preferred_element_type=F32) + jnp.dot(block, rest, preferred_element_type=F32)
        for c in range(2):
            ordered[c, pl.ds(r, 108, stride=4), :] = rows[:108, 128 * c : 128 * c + 128]
    for c in range(2):
        ordered[c, 432:, :] = jnp.zeros((16, 128), F32)
    for to in range(8):
        rows = [ordered[c, 54 * to : 54 * to + 56, :] for c in range(2)]
        out_ref[slot(to)] = jnp.concatenate(rows, axis=0).astype(BF16)


def over_xc_body(got_ref, out_ref):
    total = sum(got_ref[i].astype(F32) for i in range(8))
    for to in range(4):
        out_ref[to] = total.astype(BF16)


def last_body(got_ref, out_ref):
    total = sum(got_ref[i].astype(F32) for i in range(4))
    out_ref[...] = jnp.concatenate([total[:54], total[56:110]], axis=1)


def data_grad_body(inside_ref, outside_ref, mine_ref, weight_any, out_ref, token_ref, weight, planes, sem):
    copy = pltpu.make_async_copy(weight_any, weight, sem)
    copy.start()
    by_side(inside_ref, outside_ref, planes)
    planes[1] = mine_ref[...]
    none = jnp.zeros((16, 256), BF16)
    total = jnp.zeros((256, 128), F32)
    for a in range(3):
        wide = planes[2 - a].astype(F32)
        if a == 0:
            copy.wait()
        for c in range(3):
            moved = x_shifted(wide, 1 - c).astype(BF16)
            for b in range(3):
                if b == 2:
                    shifted = jnp.concatenate([none, moved[:240]], axis=0)
                elif b == 0:
                    shifted = jnp.concatenate([moved[16:], none], axis=0)
                else:
                    shifted = moved
                tap = 9 * a + 3 * b + c
                total = total + lax.dot_general(
                    shifted,
                    weight[128 * tap : 128 * tap + 128, :],
                    (((1,), (1,)), ((), ())),
                    preferred_element_type=F32,
                )
    out_ref[...] = total.astype(BF16)
    token_ref[...] = jnp.zeros((8, 128), F32)


def neighbours(block):
    inside = lax.ppermute(block, "c", [(0, 1), (1, 0)])
    pairs = [(i, i + 1) for i in range(1, 63, 2)]
    return inside, lax.ppermute(block, SPACE, pairs + [(j, i) for i, j in pairs])


def turned(block, k):
    pairs = [(4 * y + z, 4 * z + (y ^ k)) for y in range(4) for z in range(4)]
    return lax.ppermute(block, ("y", "zl"), pairs)


def across(block, k):
    return lax.ppermute(block, "zl", [(i, i ^ k) for i in range(4)])


def per_device(
    activations,
    conv_weight,
    conv_bias,
    cotangent,
    basis_panels,
    panel_owner,
    output_basis,
    input_eigen,
    output_eigen,
):
    dma = pltpu.SemaphoreType.DMA
    plane = activations.reshape(256, 128)
    inside, outside = neighbours(plane)

    first = call(first_body, shape((8, 128), F32), flops=4_000_000_000)
    stored = call(
        basis_body,
        shape((4, 64, 128), BF16),
        arrays=(basis_panels[0].T,),
        remote=(input_eigen.reshape(1, 54),),
        after=(first,),
        scratch=[pltpu.VMEM((1, 54), F32), dma],
    )
    delta, send, even, odd = call(
        forward_body,
        [shape((256, 256), BF16), shape((8, 384, 128), BF16)] + [shape((2, 64, 128), BF16)] * 2,
        (),
        (inside, outside, plane, conv_weight, conv_bias.reshape(1, 256), cotangent.reshape(256, 256), stored),
        scratch=[pltpu.VMEM((256, 3456), BF16), pltpu.VMEM((3, 256, 128), BF16)],
        flops=2 * 256 * 3456 * 256,
    )
    even, odd = turned(even, 0), turned(odd, 2)
    part, pair = call(
        weight_grad_body,
        [shape((16, 56, 128), BF16), shape((2, 64, 128), BF16)],
        arrays=(exchange(send, CX), even, odd),
        scratch=[pltpu.VMEM((288, 2560), BF16), pltpu.VMEM((2048, 128), BF16), pltpu.VMEM((1024, 128), F32)],
        flops=2 * 864 * 2048 * 128,
    )
    part = call(
        over_y_zl_body,
        shape((4, 272, 128), BF16),
        arrays=(exchange(part, ("zl", "y")), even, odd, across(pair, 1)),
        scratch=[pltpu.VMEM((4, 64, 128), BF16), pltpu.VMEM((272, 128), F32)],
    )
    inside, outside = neighbours(delta)
    part, basis, here, there = call(
        over_zh_zg_body,
        [shape((32, 56, 128), BF16), shape((8, 128, 128), BF16)] + [shape((2, 128, 128), BF16)] * 2,
        (panel_owner,),
        (exchange(part, ("zg", "zh")),),
        after=(inside, outside),
        scratch=[pltpu.VMEM((4, 288, 128), F32), pltpu.VMEM((4, 4, 64, 128), BF16)],
    )
    there = across(there, 2)
    rotated, pair = call(
        rotate_body,
        [shape((4, 224, 128), BF16), shape((2, 128, 128), BF16)],
        arrays=(exchange(part, CXY), basis, here, there),
        scratch=[pltpu.VMEM((2, 896, 128), F32), pltpu.VMEM((896, 256), F32)],
    )
    data, token = call(
        data_grad_body,
        [shape((256, 128), BF16), shape((8, 128), F32)],
        (),
        (inside, outside, delta),
        (conv_weight,),
        after=(pair,),
        scratch=[pltpu.VMEM((3456, 256), BF16), pltpu.VMEM((3, 256, 256), BF16), dma],
        flops=2 * 256 * 3456 * 256,
    )
    part = call(
        update_body,
        shape((8, 112, 128), BF16),
        (),
        (exchange(rotated, "zl"), here, there, across(pair, 1)),
        (output_basis, output_eigen.reshape(1, 256)),
        after=(token,),
        scratch=[
            pltpu.VMEM((4, 128, 128), BF16),
            pltpu.VMEM((256, 256), F32),
            pltpu.VMEM((1, 256), F32),
            pltpu.VMEM((2, 448, 128), F32),
            dma((2,)),
        ],
    )
    part = call(over_xc_body, shape((4, 112, 128), BF16), arrays=(exchange(part, CX),))
    update = call(last_body, shape((54, 256), F32), arrays=(exchange(part, "y"),))
    return (data.reshape(1, 1, 16, 16, 128), update)


def solution(mesh):
    fine = Mesh(mesh.devices.reshape(SIZES), AXES)
    both = P(SAMPLE, SPACE, None, None, None)
    return jax.shard_map(
        per_device,
        mesh=fine,
        in_specs=(both, P(), P(), both, P(SAMPLE, None, SPACE), P(), P(), P(SPACE), P()),
        out_specs=(both, P(SPACE, None)),
        check_vma=False,
    )
```

```python
import jax
import jax.numpy as jnp
from jax import lax
from jax.experimental import pallas as pl
from jax.experimental.pallas import tpu as pltpu
from jax.sharding import Mesh
from jax.sharding import PartitionSpec as P

DAMPING = 0.001
CELLS = 131072
BF16 = jnp.bfloat16
F32 = jnp.float32
VMEM = pl.BlockSpec(memory_space=pltpu.VMEM)
SMEM = pl.BlockSpec(memory_space=pltpu.SMEM)
LIMIT = 48 * 1024 * 1024
ANY = pl.BlockSpec(memory_space=pl.ANY)
AXES = ("y", "zh", "zg", "zl", "x", "c")
SIZES = (4, 2, 2, 4, 4, 2)
SAMPLE = ("y", "zh")
CX = ("c", "x")
CXY = ("c", "x", "y")
SPACE = ("zg", "zl", "x", "c")


def call(body, out_shape, scalars=(), arrays=(), remote=(), after=(), scratch=(), flops=0, limit=LIMIT):
    many = isinstance(out_shape, (list, tuple))
    inputs = (*scalars, *arrays, *remote, *after)
    kept = len(inputs) - len(after)

    def kernel(*refs):
        body(*refs[:kept], *refs[len(inputs) :])

    return pl.pallas_call(
        kernel,
        out_shape=out_shape,
        in_specs=[SMEM] * len(scalars) + [VMEM] * len(arrays) + [ANY] * (len(remote) + len(after)),
        out_specs=[VMEM] * len(out_shape) if many else VMEM,
        scratch_shapes=list(scratch),
        compiler_params=pltpu.CompilerParams(vmem_limit_bytes=limit),
        cost_estimate=pl.CostEstimate(
            flops=flops,
            bytes_accessed=sum(a.size * a.dtype.itemsize for a in inputs),
            transcendentals=0,
        ),
    )(*inputs)


def shape(dims, dtype):
    return jax.ShapeDtypeStruct(dims, dtype)


def iota(dims, axis):
    return lax.broadcasted_iota(jnp.int32, dims, axis)


def exchange(x, axes):
    return lax.all_to_all(x, axes, 0, 0)


def started(copies):
    for copy in copies:
        copy.start()
    return copies


def x_shifted(rows, step):
    if step == 0:
        return rows
    x = iota(rows.shape, 0) & 15
    inside = (x + step >= 0) & (x + step < 16)
    return jnp.where(inside, pltpu.roll(rows, (-step) % 256, 0), 0.0)


def basis_body(panel, eigen_any, out_ref, eigen, sem):
    copy = pltpu.make_async_copy(eigen_any, eigen, sem)
    copy.start()
    copy.wait()
    row = iota((54, 54), 0)
    column = jnp.sum(jnp.where(row == iota((54, 54), 1), eigen[...], 0.0), axis=1, keepdims=True)
    column = jnp.concatenate([column, jnp.ones((10, 1), F32)], axis=0)
    first = column.astype(BF16).astype(F32)
    second = (column - first).astype(BF16).astype(F32)
    third = column - first - second
    for r in range(4):
        pick = iota((432, 128), 0) == 4 * iota((432, 128), 1) + r
        block = jnp.dot(panel[...], jnp.where(pick, 1.0, 0.0).astype(BF16), preferred_element_type=F32)
        block = jnp.concatenate([block, jnp.zeros((10, 128), F32)], axis=0)
        at = iota((64, 128), 1)
        block = jnp.where(at == 108, first, block)
        block = jnp.where(at == 109, second, block)
        block = jnp.where(at == 110, third, block)
        out_ref[r] = block.astype(BF16)


def by_side(inside_ref, outside_ref, planes):
    second = lax.axis_index("c")
    planes[2 - 2 * second] = inside_ref[...]
    planes[2 * second] = outside_ref[...]


def first_body(out_ref):
    out_ref[...] = jnp.zeros((8, 128), F32)


def forward_body(
    inside_ref, outside_ref, mine, weight, bias, cot, basis_ref,
    delta_ref, send_ref, even_ref, odd_ref, patches, planes,
):
    y = lax.axis_index("y")
    for k, ref in ((0, even_ref), (2, odd_ref)):
        ref[0] = basis_ref[y ^ k]
        ref[1] = basis_ref[y ^ k ^ 1]
    by_side(inside_ref, outside_ref, planes)
    planes[1] = mine[...]
    none = jnp.zeros((16, 128), BF16)
    for a in range(3):
        wide = planes[a].astype(F32)
        for c in range(3):
            moved = x_shifted(wide, c - 1).astype(BF16)
            for b in range(3):
                at = (9 * a + 3 * b + c) * 128
                if b == 0:
                    shifted = jnp.concatenate([none, moved[:240]], axis=0)
                elif b == 2:
                    shifted = jnp.concatenate([moved[16:], none], axis=0)
                else:
                    shifted = moved
                patches[:, at : at + 128] = shifted
    pre = jnp.dot(patches[...], weight[...], preferred_element_type=F32) + bias[...]
    logistic = 1.0 / (1.0 + jnp.exp(-pre))
    delta = (cot[...].astype(F32) * logistic * (1.0 + pre * (1.0 - logistic))).astype(BF16)
    delta_ref[...] = delta
    act_t = mine[...].astype(F32).T.astype(BF16)
    rim_t = planes[2 * (lax.axis_index("x") >> 1)].astype(F32).T.astype(BF16)
    for x in range(4):
        for c in range(2):
            to = 4 * c + x
            for half in range(2):
                lanes = slice(128 * half, 128 * half + 128)
                rows = slice(32 * x, 32 * x + 32)
                send_ref[to, 32 * half : 32 * half + 32] = act_t[rows, lanes]
                send_ref[to, 64 + 32 * half : 96 + 32 * half] = rim_t[rows, lanes]
            send_ref[to, 128:] = delta[:, 128 * c : 128 * c + 128]


def slot(e):
    return 4 * (e % 2) + e // 2


def weight_grad_body(got_ref, even_ref, odd_ref, out_ref, pair_ref, moved, deltas, whole):
    pieces = []
    for plane, at in [(0, 64)] + [(e, 0) for e in range(8)] + [(7, 64)]:
        pieces.append(got_ref[slot(plane), at : at + 32].astype(F32))
        pieces.append(got_ref[slot(plane), at + 32 : at + 64].astype(F32))
    acts = jnp.concatenate(pieces, axis=1)
    lane = iota((8, 2560), 1)
    x = lane & 15
    y = (lane >> 4) & 15
    for b in range(3):
        for c in range(3):
            step = 16 * (b - 1) + (c - 1)
            turned = pltpu.roll(acts, (-step) % 2560, 1) if step else acts
            inside = (x + c >= 1) & (x + c < 17) & (y + b >= 1) & (y + b < 17)
            kept = jnp.where(inside[None], turned.reshape(4, 8, 2560), 0.0).reshape(32, 2560)
            moved[32 * (3 * b + c) : 32 * (3 * b + c) + 32, :] = kept.astype(BF16)
    for e in range(8):
        deltas[256 * e : 256 * e + 256, :] = got_ref[slot(e), 128:]
    for a in range(3):
        whole[288 * a : 288 * a + 288, :] = jnp.dot(
            moved[:, 256 * a : 256 * a + 2048], deltas[...], preferred_element_type=F32
        )
    pair_ref[0] = even_ref[1]
    pair_ref[1] = odd_ref[1]
    none = jnp.zeros((1, 128), F32)
    for y_to in range(4):
        for z_to in range(4):
            parts = []
            for e in range(2):
                parts.append(whole[pl.ds(8 * y_to + 4 * e + z_to, 27, stride=32), :])
                parts.append(none)
            out_ref[4 * z_to + y_to] = jnp.concatenate(parts, axis=0).astype(BF16)


def over_y_zl_body(got_ref, even_ref, odd_ref, pair_ref, out_ref, slices, rows):
    total = sum(got_ref[i].astype(F32) for i in range(16)) * (1.0 / CELLS)
    zl = lax.axis_index("zl")
    for k, block in ((0, even_ref[0]), (2, odd_ref[0]), (1, pair_ref[0]), (3, pair_ref[1])):
        slices[zl ^ k] = block
    rows[:27, :] = total[:27]
    rows[27:54, :] = total[28:55]
    for y in range(4):
        rows[54 + 54 * y : 108 + 54 * y, :] = slices[y].astype(F32)[:54]
    rows[270:, :] = jnp.zeros((2, 128), F32)
    for to in range(4):
        out_ref[to] = rows[...].astype(BF16)


def over_zh_zg_body(owner_ref, got_ref, out_ref, basis_ref, here_ref, next_ref, rows, slices):
    for i in range(4):
        rows[i, :272, :] = got_ref[i].astype(F32)
        rows[i, 272:, :] = jnp.zeros((16, 128), F32)
        for y in range(4):
            slices[i, y] = rows[i, 54 + 54 * y : 118 + 54 * y, :].astype(BF16)
    total = (rows[0, :54, :] + rows[1, :54, :]) + (rows[2, :54, :] + rows[3, :54, :])
    none = jnp.zeros((1, 128), F32)
    total = jnp.concatenate([total[:27], none, total[27:], none], axis=0).astype(BF16)
    for to in range(32):
        out_ref[to] = total
    for j in range(8):
        for zg in range(2):
            basis_ref[j, 64 * zg : 64 * zg + 64] = slices[2 * zg + (owner_ref[j] & 1), owner_ref[j] >> 1]
    zg, zl = lax.axis_index("zg"), lax.axis_index("zl")
    for k, ref in ((0, here_ref), (2, next_ref)):
        ref[0] = basis_ref[4 * zg + (zl ^ k)]
        ref[1] = basis_ref[4 * zg + (zl ^ k ^ 1)]


def rotate_body(got_ref, basis_ref, here_ref, next_ref, out_ref, pair_ref, grads, ordered):
    pair_ref[0] = here_ref[1]
    pair_ref[1] = next_ref[1]
    for y in range(4):
        for x in range(4):
            at = 28 * (8 * x + 2 * y)
            for c in range(2):
                grads[c, at : at + 56, :] = got_ref[16 * c + 4 * x + y].astype(F32)
    for tap in range(27):
        for c in range(2):
            ordered[32 * tap : 32 * tap + 32, 128 * c : 128 * c + 128] = grads[c, pl.ds(tap, 32, stride=28), :]
    ordered[864:, :] = jnp.zeros((32, 256), F32)
    inside = iota((128, 128), 1) < 108
    total = jnp.zeros((128, 256), F32)
    for j in range(8):
        block = jnp.where(inside, basis_ref[j].astype(F32), 0.0).astype(BF16)
        rows = ordered[108 * j : 108 * j + 128, :].astype(BF16)
        total = total + jnp.dot(block, rows, preferred_element_type=F32)
    total = jnp.concatenate(
        [total[64 * zg : 64 * zg + 56, 128 * c : 128 * c + 128] for zg in range(2) for c in range(2)], axis=0
    ).astype(BF16)
    for to in range(4):
        out_ref[to] = total


def two_terms(x):
    high = x.astype(BF16)
    return high, (x - high.astype(F32)).astype(BF16)


def product(a, b, contract):
    a_high, a_low = two_terms(a)
    b_high, b_low = two_terms(b)

    def dot(u, v):
        return lax.dot_general(u, v, (contract, ((), ())), preferred_element_type=F32)

    return dot(a_high, b_high) + (dot(a_high, b_low) + dot(a_low, b_high))


def update_body(
    got_ref, here_ref, next_ref, pair_ref, out_basis_any, out_eigen_any,
    out_ref, panel, out_basis, out_eigen, ordered, sems,
):
    zl = lax.axis_index("zl")
    for k, block in ((0, here_ref[0]), (2, next_ref[0]), (1, pair_ref[0]), (3, pair_ref[1])):
        panel[zl ^ k] = block
    copies = [
        pltpu.make_async_copy(out_basis_any, out_basis, sems.at[0]),
        pltpu.make_async_copy(out_eigen_any, out_eigen, sems.at[1]),
    ]
    started(copies)
    total = sum(got_ref[i].astype(F32) for i in range(4))
    none = jnp.zeros((8, 256), F32)
    parts = []
    for zg in range(2):
        at = 112 * zg
        parts.append(jnp.concatenate([total[at : at + 56], total[at + 56 : at + 112]], axis=1))
        parts.append(none)
    rotated = jnp.concatenate(parts, axis=0)
    for copy in copies:
        copy.wait()
    rotated = product(rotated, out_basis[...], ((1,), (0,)))
    terms = here_ref[0].astype(F32)
    eigen = (terms[:, 108:109] + terms[:, 109:110]) + terms[:, 110:111]
    scaled = rotated / (eigen * out_eigen[...] + DAMPING)
    scaled = jnp.where((iota((128, 256), 0) & 63) < 54, scaled, 0.0)
    high, rest = two_terms(product(scaled, out_basis[...], ((1,), (1,))))
    for r in range(4):
        block = panel[r].astype(F32).T.astype(BF16)
        rows = jnp.dot(block, high, preferred_element_type=F32) + jnp.dot(block, rest, preferred_element_type=F32)
        for c in range(2):
            ordered[c, pl.ds(r, 108, stride=4), :] = rows[:108, 128 * c : 128 * c + 128]
    for c in range(2):
        ordered[c, 432:, :] = jnp.zeros((16, 128), F32)
    for to in range(8):
        rows = [ordered[c, 54 * to : 54 * to + 56, :] for c in range(2)]
        out_ref[slot(to)] = jnp.concatenate(rows, axis=0).astype(BF16)


def over_xc_body(got_ref, out_ref):
    total = sum(got_ref[i].astype(F32) for i in range(8))
    for to in range(4):
        out_ref[to] = total.astype(BF16)


def last_body(got_ref, out_ref):
    total = sum(got_ref[i].astype(F32) for i in range(4))
    out_ref[...] = jnp.concatenate([total[:54], total[56:110]], axis=1)


def data_grad_body(inside_ref, outside_ref, mine_ref, weight_any, out_ref, token_ref, weight, planes, sem):
    copy = pltpu.make_async_copy(weight_any, weight, sem)
    copy.start()
    by_side(inside_ref, outside_ref, planes)
    planes[1] = mine_ref[...]
    none = jnp.zeros((16, 256), BF16)
    total = jnp.zeros((256, 128), F32)
    for a in range(3):
        wide = planes[2 - a].astype(F32)
        if a == 0:
            copy.wait()
        for c in range(3):
            moved = x_shifted(wide, 1 - c).astype(BF16)
            for b in range(3):
                if b == 2:
                    shifted = jnp.concatenate([none, moved[:240]], axis=0)
                elif b == 0:
                    shifted = jnp.concatenate([moved[16:], none], axis=0)
                else:
                    shifted = moved
                tap = 9 * a + 3 * b + c
                total = total + lax.dot_general(
                    shifted,
                    weight[128 * tap : 128 * tap + 128, :],
                    (((1,), (1,)), ((), ())),
                    preferred_element_type=F32,
                )
    out_ref[...] = total.astype(BF16)
    token_ref[...] = jnp.zeros((8, 128), F32)


def neighbours(block):
    inside = lax.ppermute(block, "c", [(0, 1), (1, 0)])
    pairs = [(i, i + 1) for i in range(1, 63, 2)]
    return inside, lax.ppermute(block, SPACE, pairs + [(j, i) for i, j in pairs])


def turned(block, k):
    pairs = [(4 * y + z, 4 * z + (y ^ k)) for y in range(4) for z in range(4)]
    return lax.ppermute(block, ("y", "zl"), pairs)


def across(block, k):
    return lax.ppermute(block, "zl", [(i, i ^ k) for i in range(4)])


def per_device(
    activations,
    conv_weight,
    conv_bias,
    cotangent,
    basis_panels,
    panel_owner,
    output_basis,
    input_eigen,
    output_eigen,
):
    dma = pltpu.SemaphoreType.DMA
    plane = activations.reshape(256, 128)
    inside, outside = neighbours(plane)

    first = call(first_body, shape((8, 128), F32), flops=4_000_000_000)
    stored = call(
        basis_body,
        shape((4, 64, 128), BF16),
        arrays=(basis_panels[0].T,),
        remote=(input_eigen.reshape(1, 54),),
        after=(first,),
        scratch=[pltpu.VMEM((1, 54), F32), dma],
    )
    delta, send, even, odd = call(
        forward_body,
        [shape((256, 256), BF16), shape((8, 384, 128), BF16)] + [shape((2, 64, 128), BF16)] * 2,
        (),
        (inside, outside, plane, conv_weight, conv_bias.reshape(1, 256), cotangent.reshape(256, 256), stored),
        scratch=[pltpu.VMEM((256, 3456), BF16), pltpu.VMEM((3, 256, 128), BF16)],
        flops=2 * 256 * 3456 * 256,
    )
    even, odd = turned(even, 0), turned(odd, 2)
    part, pair = call(
        weight_grad_body,
        [shape((16, 56, 128), BF16), shape((2, 64, 128), BF16)],
        arrays=(exchange(send, CX), even, odd),
        scratch=[pltpu.VMEM((288, 2560), BF16), pltpu.VMEM((2048, 128), BF16), pltpu.VMEM((1024, 128), F32)],
        flops=2 * 864 * 2048 * 128,
    )
    part = call(
        over_y_zl_body,
        shape((4, 272, 128), BF16),
        arrays=(exchange(part, ("zl", "y")), even, odd, across(pair, 1)),
        scratch=[pltpu.VMEM((4, 64, 128), BF16), pltpu.VMEM((272, 128), F32)],
    )
    inside, outside = neighbours(delta)
    part, basis, here, there = call(
        over_zh_zg_body,
        [shape((32, 56, 128), BF16), shape((8, 128, 128), BF16)] + [shape((2, 128, 128), BF16)] * 2,
        (panel_owner,),
        (exchange(part, ("zg", "zh")),),
        after=(inside, outside),
        scratch=[pltpu.VMEM((4, 288, 128), F32), pltpu.VMEM((4, 4, 64, 128), BF16)],
    )
    there = across(there, 2)
    rotated, pair = call(
        rotate_body,
        [shape((4, 224, 128), BF16), shape((2, 128, 128), BF16)],
        arrays=(exchange(part, CXY), basis, here, there),
        scratch=[pltpu.VMEM((2, 896, 128), F32), pltpu.VMEM((896, 256), F32)],
    )
    data, token = call(
        data_grad_body,
        [shape((256, 128), BF16), shape((8, 128), F32)],
        (),
        (inside, outside, delta),
        (conv_weight,),
        after=(pair,),
        scratch=[pltpu.VMEM((3456, 256), BF16), pltpu.VMEM((3, 256, 256), BF16), dma],
        flops=2 * 256 * 3456 * 256,
    )
    part = call(
        update_body,
        shape((8, 112, 128), BF16),
        (),
        (exchange(rotated, "zl"), here, there, across(pair, 1)),
        (output_basis, output_eigen.reshape(1, 256)),
        after=(token,),
        scratch=[
            pltpu.VMEM((4, 128, 128), BF16),
            pltpu.VMEM((256, 256), F32),
            pltpu.VMEM((1, 256), F32),
            pltpu.VMEM((2, 448, 128), F32),
            dma((2,)),
        ],
    )
    part = call(over_xc_body, shape((4, 112, 128), BF16), arrays=(exchange(part, CX),))
    update = call(last_body, shape((54, 256), F32), arrays=(exchange(part, "y"),))
    return (data.reshape(1, 1, 16, 16, 128), update)


def solution(mesh):
    fine = Mesh(mesh.devices.reshape(SIZES), AXES)
    both = P(SAMPLE, SPACE, None, None, None)
    return jax.shard_map(
        per_device,
        mesh=fine,
        in_specs=(both, P(), P(), both, P(SAMPLE, None, SPACE), P(), P(), P(SPACE), P()),
        out_specs=(both, P(SPACE, None)),
        check_vma=False,
    )
```

```python
import jax
import jax.numpy as jnp
from jax import lax
from jax.experimental import pallas as pl
from jax.experimental.pallas import tpu as pltpu
from jax.sharding import Mesh
from jax.sharding import PartitionSpec as P

DAMPING = 0.001
CELLS = 131072
BF16 = jnp.bfloat16
F32 = jnp.float32
VMEM = pl.BlockSpec(memory_space=pltpu.VMEM)
SMEM = pl.BlockSpec(memory_space=pltpu.SMEM)
LIMIT = 48 * 1024 * 1024
ANY = pl.BlockSpec(memory_space=pl.ANY)
AXES = ("y", "zh", "zg", "zl", "x", "c")
SIZES = (4, 2, 2, 4, 4, 2)
SAMPLE = ("y", "zh")
CX = ("c", "x")
CXY = ("c", "x", "y")
SPACE = ("zg", "zl", "x", "c")


def call(body, out_shape, scalars=(), arrays=(), remote=(), after=(), scratch=(), flops=0, limit=LIMIT):
    many = isinstance(out_shape, (list, tuple))
    inputs = (*scalars, *arrays, *remote, *after)
    kept = len(inputs) - len(after)

    def kernel(*refs):
        body(*refs[:kept], *refs[len(inputs) :])

    return pl.pallas_call(
        kernel,
        out_shape=out_shape,
        in_specs=[SMEM] * len(scalars) + [VMEM] * len(arrays) + [ANY] * (len(remote) + len(after)),
        out_specs=[VMEM] * len(out_shape) if many else VMEM,
        scratch_shapes=list(scratch),
        compiler_params=pltpu.CompilerParams(vmem_limit_bytes=limit),
        cost_estimate=pl.CostEstimate(
            flops=flops,
            bytes_accessed=sum(a.size * a.dtype.itemsize for a in inputs),
            transcendentals=0,
        ),
    )(*inputs)


def shape(dims, dtype):
    return jax.ShapeDtypeStruct(dims, dtype)


def iota(dims, axis):
    return lax.broadcasted_iota(jnp.int32, dims, axis)


def exchange(x, axes):
    return lax.all_to_all(x, axes, 0, 0)


def started(copies):
    for copy in copies:
        copy.start()
    return copies


def x_shifted(rows, step):
    if step == 0:
        return rows
    x = iota(rows.shape, 0) & 15
    inside = (x + step >= 0) & (x + step < 16)
    return jnp.where(inside, pltpu.roll(rows, (-step) % 256, 0), 0.0)


def basis_body(panel, eigen_any, out_ref, eigen, sem):
    copy = pltpu.make_async_copy(eigen_any, eigen, sem)
    copy.start()
    copy.wait()
    row = iota((54, 54), 0)
    column = jnp.sum(jnp.where(row == iota((54, 54), 1), eigen[...], 0.0), axis=1, keepdims=True)
    column = jnp.concatenate([column, jnp.ones((10, 1), F32)], axis=0)
    first = column.astype(BF16).astype(F32)
    second = (column - first).astype(BF16).astype(F32)
    third = column - first - second
    for r in range(4):
        pick = iota((432, 128), 0) == 4 * iota((432, 128), 1) + r
        block = jnp.dot(panel[...], jnp.where(pick, 1.0, 0.0).astype(BF16), preferred_element_type=F32)
        block = jnp.concatenate([block, jnp.zeros((10, 128), F32)], axis=0)
        at = iota((64, 128), 1)
        block = jnp.where(at == 108, first, block)
        block = jnp.where(at == 109, second, block)
        block = jnp.where(at == 110, third, block)
        out_ref[r] = block.astype(BF16)


def by_side(inside_ref, outside_ref, planes):
    second = lax.axis_index("c")
    planes[2 - 2 * second] = inside_ref[...]
    planes[2 * second] = outside_ref[...]


def first_body(out_ref):
    out_ref[...] = jnp.zeros((8, 128), F32)


def forward_body(
    inside_ref, outside_ref, mine, weight, bias, cot, basis_ref,
    delta_ref, send_ref, even_ref, odd_ref, patches, planes,
):
    y = lax.axis_index("y")
    for k, ref in ((0, even_ref), (2, odd_ref)):
        ref[0] = basis_ref[y ^ k]
        ref[1] = basis_ref[y ^ k ^ 1]
    by_side(inside_ref, outside_ref, planes)
    planes[1] = mine[...]
    none = jnp.zeros((16, 128), BF16)
    for a in range(3):
        wide = planes[a].astype(F32)
        for c in range(3):
            moved = x_shifted(wide, c - 1).astype(BF16)
            for b in range(3):
                at = (9 * a + 3 * b + c) * 128
                if b == 0:
                    shifted = jnp.concatenate([none, moved[:240]], axis=0)
                elif b == 2:
                    shifted = jnp.concatenate([moved[16:], none], axis=0)
                else:
                    shifted = moved
                patches[:, at : at + 128] = shifted
    pre = jnp.dot(patches[...], weight[...], preferred_element_type=F32) + bias[...]
    logistic = 1.0 / (1.0 + jnp.exp(-pre))
    delta = (cot[...].astype(F32) * logistic * (1.0 + pre * (1.0 - logistic))).astype(BF16)
    delta_ref[...] = delta
    act_t = mine[...].astype(F32).T.astype(BF16)
    rim_t = planes[2 * (lax.axis_index("x") >> 1)].astype(F32).T.astype(BF16)
    for x in range(4):
        for c in range(2):
            to = 4 * c + x
            for half in range(2):
                lanes = slice(128 * half, 128 * half + 128)
                rows = slice(32 * x, 32 * x + 32)
                send_ref[to, 32 * half : 32 * half + 32] = act_t[rows, lanes]
                send_ref[to, 64 + 32 * half : 96 + 32 * half] = rim_t[rows, lanes]
            send_ref[to, 128:] = delta[:, 128 * c : 128 * c + 128]


def slot(e):
    return 4 * (e % 2) + e // 2


def weight_grad_body(got_ref, odd_ref, even_ref, out_ref, pair_ref, moved, deltas, whole):
    pieces = []
    for plane, at in [(0, 64)] + [(e, 0) for e in range(8)] + [(7, 64)]:
        pieces.append(got_ref[slot(plane), at : at + 32].astype(F32))
        pieces.append(got_ref[slot(plane), at + 32 : at + 64].astype(F32))
    acts = jnp.concatenate(pieces, axis=1)
    lane = iota((8, 2560), 1)
    x = lane & 15
    y = (lane >> 4) & 15
    for b in range(3):
        for c in range(3):
            step = 16 * (b - 1) + (c - 1)
            turned = pltpu.roll(acts, (-step) % 2560, 1) if step else acts
            inside = (x + c >= 1) & (x + c < 17) & (y + b >= 1) & (y + b < 17)
            kept = jnp.where(inside[None], turned.reshape(4, 8, 2560), 0.0).reshape(32, 2560)
            moved[32 * (3 * b + c) : 32 * (3 * b + c) + 32, :] = kept.astype(BF16)
    for e in range(8):
        deltas[256 * e : 256 * e + 256, :] = got_ref[slot(e), 128:]
    for a in range(3):
        whole[288 * a : 288 * a + 288, :] = jnp.dot(
            moved[:, 256 * a : 256 * a + 2048], deltas[...], preferred_element_type=F32
        )
    pair_ref[0] = even_ref[1]
    pair_ref[1] = odd_ref[1]
    none = jnp.zeros((1, 128), F32)
    for y_to in range(4):
        for z_to in range(4):
            parts = []
            for e in range(2):
                parts.append(whole[pl.ds(8 * y_to + 4 * e + z_to, 27, stride=32), :])
                parts.append(none)
            out_ref[4 * z_to + y_to] = jnp.concatenate(parts, axis=0).astype(BF16)


def over_y_zl_body(got_ref, even_ref, odd_ref, pair_ref, out_ref, slices, rows):
    total = sum(got_ref[i].astype(F32) for i in range(16)) * (1.0 / CELLS)
    zl = lax.axis_index("zl")
    for k, block in ((0, even_ref[0]), (2, odd_ref[0]), (1, pair_ref[0]), (3, pair_ref[1])):
        slices[zl ^ k] = block
    rows[:27, :] = total[:27]
    rows[27:54, :] = total[28:55]
    for y in range(4):
        rows[54 + 54 * y : 108 + 54 * y, :] = slices[y].astype(F32)[:54]
    rows[270:, :] = jnp.zeros((2, 128), F32)
    for to in range(4):
        out_ref[to] = rows[...].astype(BF16)


def over_zh_zg_body(owner_ref, got_ref, out_ref, basis_ref, here_ref, next_ref, rows, slices):
    for i in range(4):
        rows[i, :272, :] = got_ref[i].astype(F32)
        rows[i, 272:, :] = jnp.zeros((16, 128), F32)
        for y in range(4):
            slices[i, y] = rows[i, 54 + 54 * y : 118 + 54 * y, :].astype(BF16)
    total = (rows[0, :54, :] + rows[1, :54, :]) + (rows[2, :54, :] + rows[3, :54, :])
    none = jnp.zeros((1, 128), F32)
    total = jnp.concatenate([total[:27], none, total[27:], none], axis=0).astype(BF16)
    for to in range(32):
        out_ref[to] = total
    for j in range(8):
        for zg in range(2):
            basis_ref[j, 64 * zg : 64 * zg + 64] = slices[2 * zg + (owner_ref[j] & 1), owner_ref[j] >> 1]
    zg, zl = lax.axis_index("zg"), lax.axis_index("zl")
    for k, ref in ((0, here_ref), (2, next_ref)):
        ref[0] = basis_ref[4 * zg + (zl ^ k)]
        ref[1] = basis_ref[4 * zg + (zl ^ k ^ 1)]


def rotate_body(got_ref, basis_ref, here_ref, next_ref, out_ref, pair_ref, grads, ordered):
    pair_ref[0] = here_ref[1]
    pair_ref[1] = next_ref[1]
    for y in range(4):
        for x in range(4):
            at = 28 * (8 * x + 2 * y)
            for c in range(2):
                grads[c, at : at + 56, :] = got_ref[16 * c + 4 * x + y].astype(F32)
    for tap in range(27):
        for c in range(2):
            ordered[32 * tap : 32 * tap + 32, 128 * c : 128 * c + 128] = grads[c, pl.ds(tap, 32, stride=28), :]
    ordered[864:, :] = jnp.zeros((32, 256), F32)
    inside = iota((128, 128), 1) < 108
    total = jnp.zeros((128, 256), F32)
    for j in range(8):
        block = jnp.where(inside, basis_ref[j].astype(F32), 0.0).astype(BF16)
        rows = ordered[108 * j : 108 * j + 128, :].astype(BF16)
        total = total + jnp.dot(block, rows, preferred_element_type=F32)
    total = jnp.concatenate(
        [total[64 * zg : 64 * zg + 56, 128 * c : 128 * c + 128] for zg in range(2) for c in range(2)], axis=0
    ).astype(BF16)
    for to in range(4):
        out_ref[to] = total


def two_terms(x):
    high = x.astype(BF16)
    return high, (x - high.astype(F32)).astype(BF16)


def product(a, b, contract):
    a_high, a_low = two_terms(a)
    b_high, b_low = two_terms(b)

    def dot(u, v):
        return lax.dot_general(u, v, (contract, ((), ())), preferred_element_type=F32)

    return dot(a_high, b_high) + (dot(a_high, b_low) + dot(a_low, b_high))


def update_body(
    got_ref, here_ref, next_ref, pair_ref, out_basis_any, out_eigen_any,
    out_ref, panel, out_basis, out_eigen, ordered, sems,
):
    zl = lax.axis_index("zl")
    for k, block in ((0, here_ref[0]), (2, next_ref[0]), (1, pair_ref[0]), (3, pair_ref[1])):
        panel[zl ^ k] = block
    copies = [
        pltpu.make_async_copy(out_basis_any, out_basis, sems.at[0]),
        pltpu.make_async_copy(out_eigen_any, out_eigen, sems.at[1]),
    ]
    started(copies)
    total = sum(got_ref[i].astype(F32) for i in range(4))
    none = jnp.zeros((8, 256), F32)
    parts = []
    for zg in range(2):
        at = 112 * zg
        parts.append(jnp.concatenate([total[at : at + 56], total[at + 56 : at + 112]], axis=1))
        parts.append(none)
    rotated = jnp.concatenate(parts, axis=0)
    for copy in copies:
        copy.wait()
    rotated = product(rotated, out_basis[...], ((1,), (0,)))
    terms = here_ref[0].astype(F32)
    eigen = (terms[:, 108:109] + terms[:, 109:110]) + terms[:, 110:111]
    scaled = rotated / (eigen * out_eigen[...] + DAMPING)
    scaled = jnp.where((iota((128, 256), 0) & 63) < 54, scaled, 0.0)
    high, rest = two_terms(product(scaled, out_basis[...], ((1,), (1,))))
    for r in range(4):
        block = panel[r].astype(F32).T.astype(BF16)
        rows = jnp.dot(block, high, preferred_element_type=F32) + jnp.dot(block, rest, preferred_element_type=F32)
        for c in range(2):
            ordered[c, pl.ds(r, 108, stride=4), :] = rows[:108, 128 * c : 128 * c + 128]
    for c in range(2):
        ordered[c, 432:, :] = jnp.zeros((16, 128), F32)
    for to in range(8):
        rows = [ordered[c, 54 * to : 54 * to + 56, :] for c in range(2)]
        out_ref[slot(to)] = jnp.concatenate(rows, axis=0).astype(BF16)


def over_xc_body(got_ref, out_ref):
    total = sum(got_ref[i].astype(F32) for i in range(8))
    for to in range(4):
        out_ref[to] = total.astype(BF16)


def last_body(got_ref, out_ref):
    total = sum(got_ref[i].astype(F32) for i in range(4))
    out_ref[...] = jnp.concatenate([total[:54], total[56:110]], axis=1)


def data_grad_body(inside_ref, outside_ref, mine_ref, weight_any, out_ref, token_ref, weight, planes, sem):
    copy = pltpu.make_async_copy(weight_any, weight, sem)
    copy.start()
    by_side(inside_ref, outside_ref, planes)
    planes[1] = mine_ref[...]
    none = jnp.zeros((16, 256), BF16)
    total = jnp.zeros((256, 128), F32)
    for a in range(3):
        wide = planes[2 - a].astype(F32)
        if a == 0:
            copy.wait()
        for c in range(3):
            moved = x_shifted(wide, 1 - c).astype(BF16)
            for b in range(3):
                if b == 2:
                    shifted = jnp.concatenate([none, moved[:240]], axis=0)
                elif b == 0:
                    shifted = jnp.concatenate([moved[16:], none], axis=0)
                else:
                    shifted = moved
                tap = 9 * a + 3 * b + c
                total = total + lax.dot_general(
                    shifted,
                    weight[128 * tap : 128 * tap + 128, :],
                    (((1,), (1,)), ((), ())),
                    preferred_element_type=F32,
                )
    out_ref[...] = total.astype(BF16)
    token_ref[...] = jnp.zeros((8, 128), F32)


def neighbours(block):
    inside = lax.ppermute(block, "c", [(0, 1), (1, 0)])
    pairs = [(i, i + 1) for i in range(1, 63, 2)]
    return inside, lax.ppermute(block, SPACE, pairs + [(j, i) for i, j in pairs])


def turned(block, k):
    pairs = [(4 * y + z, 4 * z + (y ^ k)) for y in range(4) for z in range(4)]
    return lax.ppermute(block, ("y", "zl"), pairs)


def across(block, k):
    return lax.ppermute(block, "zl", [(i, i ^ k) for i in range(4)])


def per_device(
    activations,
    conv_weight,
    conv_bias,
    cotangent,
    basis_panels,
    panel_owner,
    output_basis,
    input_eigen,
    output_eigen,
):
    dma = pltpu.SemaphoreType.DMA
    plane = activations.reshape(256, 128)
    inside, outside = neighbours(plane)

    first = call(first_body, shape((8, 128), F32), flops=4_000_000_000)
    stored = call(
        basis_body,
        shape((4, 64, 128), BF16),
        arrays=(basis_panels[0].T,),
        remote=(input_eigen.reshape(1, 54),),
        after=(first,),
        scratch=[pltpu.VMEM((1, 54), F32), dma],
    )
    delta, send, even, odd = call(
        forward_body,
        [shape((256, 256), BF16), shape((8, 384, 128), BF16)] + [shape((2, 64, 128), BF16)] * 2,
        (),
        (inside, outside, plane, conv_weight, conv_bias.reshape(1, 256), cotangent.reshape(256, 256), stored),
        scratch=[pltpu.VMEM((256, 3456), BF16), pltpu.VMEM((3, 256, 128), BF16)],
        flops=2 * 256 * 3456 * 256,
    )
    odd = turned(odd, 2)
    even = turned(even, 0)
    part, pair = call(
        weight_grad_body,
        [shape((16, 56, 128), BF16), shape((2, 64, 128), BF16)],
        arrays=(exchange(send, CX), odd, even),
        scratch=[pltpu.VMEM((288, 2560), BF16), pltpu.VMEM((2048, 128), BF16), pltpu.VMEM((1024, 128), F32)],
        flops=2 * 864 * 2048 * 128,
    )
    part = call(
        over_y_zl_body,
        shape((4, 272, 128), BF16),
        arrays=(exchange(part, ("zl", "y")), even, odd, across(pair, 1)),
        scratch=[pltpu.VMEM((4, 64, 128), BF16), pltpu.VMEM((272, 128), F32)],
    )
    inside, outside = neighbours(delta)
    part, basis, here, there = call(
        over_zh_zg_body,
        [shape((32, 56, 128), BF16), shape((8, 128, 128), BF16)] + [shape((2, 128, 128), BF16)] * 2,
        (panel_owner,),
        (exchange(part, ("zg", "zh")),),
        after=(inside, outside),
        scratch=[pltpu.VMEM((4, 288, 128), F32), pltpu.VMEM((4, 4, 64, 128), BF16)],
    )
    there = across(there, 2)
    rotated, pair = call(
        rotate_body,
        [shape((4, 224, 128), BF16), shape((2, 128, 128), BF16)],
        arrays=(exchange(part, CXY), basis, here, there),
        scratch=[pltpu.VMEM((2, 896, 128), F32), pltpu.VMEM((896, 256), F32)],
    )
    data, token = call(
        data_grad_body,
        [shape((256, 128), BF16), shape((8, 128), F32)],
        (),
        (inside, outside, delta),
        (conv_weight,),
        after=(pair,),
        scratch=[pltpu.VMEM((3456, 256), BF16), pltpu.VMEM((3, 256, 256), BF16), dma],
        flops=2 * 256 * 3456 * 256,
    )
    part = call(
        update_body,
        shape((8, 112, 128), BF16),
        (),
        (exchange(rotated, "zl"), here, there, across(pair, 1)),
        (output_basis, output_eigen.reshape(1, 256)),
        after=(token,),
        scratch=[
            pltpu.VMEM((4, 128, 128), BF16),
            pltpu.VMEM((256, 256), F32),
            pltpu.VMEM((1, 256), F32),
            pltpu.VMEM((2, 448, 128), F32),
            dma((2,)),
        ],
    )
    part = call(over_xc_body, shape((4, 112, 128), BF16), arrays=(exchange(part, CX),))
    update = call(last_body, shape((54, 256), F32), arrays=(exchange(part, "y"),))
    return (data.reshape(1, 1, 16, 16, 128), update)


def solution(mesh):
    fine = Mesh(mesh.devices.reshape(SIZES), AXES)
    both = P(SAMPLE, SPACE, None, None, None)
    return jax.shard_map(
        per_device,
        mesh=fine,
        in_specs=(both, P(), P(), both, P(SAMPLE, None, SPACE), P(), P(), P(SPACE), P()),
        out_specs=(both, P(SPACE, None)),
        check_vma=False,
    )
```
